32 devices in a mesh: grp: 4 (over z), mem: 8 (over y, x, core).
Axes of the slice: x: 2, y: 2, z: 4, core: 2. Of those that a mesh axis runs over, the one named last changes fastest.
Arguments:
- forcing: float32 [3, 256, 4096], P(None, ('grp', 'mem')), may hold values from -6 to 6
- viscosity: float32 [256, 4096], P(('grp', 'mem')), may hold values from 0.1 to 10
- refinement: int32 [256], P(('grp', 'mem')), may hold values from 0 to 1
- face_owner: int32 [1024, 1], P(('grp', 'mem')), may hold values from 0 to 7; in each aligned block of 32 rows (0 to 31, 32 to 63, ...) at most 8 rows name the same one
- face_block: int32 [256, 4], P(('grp', 'mem')), may hold values from 0 to 7
- plane_block: int32 [256, 2], P(('grp', 'mem')), may hold values from 0 to 7
- hanging: int32 [256, 6], P(('grp', 'mem')), may hold values 0 or 1
- coarse_solver: float32 [4, 192, 192], P('grp', 'mem'), may hold values from -0.4375 to 0.4375
Outputs:
- velocity: float32 [3, 256, 4096], P(None, ('grp', 'mem'))
- residual: float32 [3, 256, 4096], P(None, ('grp', 'mem'))
The draws below stay inside these ranges and needn't reach their ends.
Inputs may be any that keep to these rules, and one draw needn't show every extreme that they name: `face_owner`: among the 32 rows of one device no member appears more than 8 times, and some member appears exactly 8 times.
All inputs are finite; a program needn't handle non-finite values. No bound on the sum of `hanging` on one device may be relied on, other than what follows from the above.
Results may differ from the reference program's by a relative error of at most 0.0001.
Values sent between devices are 32-bit elements; how exact they have to be, the bound alone decides.
No kernel may reach another device: no remote copies, remote signals or barrier semaphores. Data moves between devices by JAX's collectives and lax.ppermute only.
A program may use at most 64 MiB of HBM per device.

```python
import math
import jax
import jax.numpy as jnp
import numpy as np
from jax import lax

EDGE = 16
B_DEV = 8
DEG = 3
CELLS = 4096
FACE = 256
BLOCKS = 256
CAP = 8
NC = 192
N_GRP = 4
N_MEM = 8


def place_ends(values, rng, smallest, top_value):
    place = [jax.random.randint(jax.random.fold_in(rng, axis), (), 0, length) for axis, length in enumerate(values.shape)]
    longest = values.shape.index(max(values.shape))
    next_to = place[:longest] + [(place[longest] + 1) % values.shape[longest]] + place[longest + 1:]
    return values.at[tuple(place)].set(smallest).at[tuple(next_to)].set(top_value)


def level_of(rng, dims, pieces, smallest, largest):
    loudness, own = 1.0, jax.random.fold_in(rng, 6)
    for dim, parts in pieces:
        steps = jnp.exp(jax.random.uniform(jax.random.fold_in(own, dim), (parts,), jnp.float32, smallest / len(pieces), largest / len(pieces)))
        loudness = loudness * jnp.repeat(steps, dims[dim] // parts).reshape([-1 if axis == dim else 1 for axis in range(len(dims))])
    return loudness


def shared_out(stream_key, own, number, rows, amount, top, most, slope):
    order = jax.random.permutation(stream_key, amount)
    crowded, usual = load_shares(amount, rows * top, most, slope, True), load_shares(amount, rows * top, most, slope, False)
    places = jnp.arange(amount)

    def named(lengths, turn):
        used = int((lengths > 0).sum())
        fixed = max(1, used // 4)
        moved = fixed + (places - fixed + turn * (used - fixed)) % max(1, amount - fixed)
        return jnp.zeros((amount,), jnp.int32).at[order[jnp.where(places < fixed, places, moved)]].set(jnp.asarray(lengths, jnp.int32))

    lengths = jnp.where(number % 4 == 0, named(crowded, number // 4), named(usual, number - number // 4 - 1))
    mixed = jax.random.permutation(jax.random.fold_in(own, 3), amount)
    donor, sink = mixed[0:amount // 2 * 2:2], mixed[1:amount // 2 * 2:2]
    margin = jnp.minimum(lengths[donor] - 1, most - lengths[sink]) // 2
    margin = jnp.where((donor == order[0]) | (sink == order[0]) | (lengths[sink] == 0), 0, jnp.maximum(margin, 0))
    moved = jax.random.randint(jax.random.fold_in(own, 4), (amount // 2,), 0, 1 << 20) % (margin + 1)
    lengths = lengths.at[donor].add(-moved).at[sink].add(moved)
    members = jnp.searchsorted(jnp.cumsum(lengths), jnp.arange(rows * top), side="right").astype(jnp.int32)
    grid = members.reshape(top, rows).T
    grid = grid[jax.random.permutation(jax.random.fold_in(own, 1), rows)]
    turn = jax.random.randint(jax.random.fold_in(own, 2), (rows, 1), 0, top)
    return jnp.take_along_axis(grid, (jnp.arange(top)[None, :] + turn) % top, axis=1)


def load_shares(amount, total, reach, skew, full):
    weights = [(1 << 20) // math.isqrt(rank ** skew) + 1 for rank in range(1, amount + 1)]
    largest = reach if full else min(reach, max(-(-total // amount), total * weights[0] // sum(weights)))
    least = 1 if total - largest >= amount - 1 else 0
    holding, surplus = [largest] + [least] * (amount - 1), total - largest - least * (amount - 1)
    while surplus > 0:
        candidates = [i for i in range(1, amount) if holding[i] < largest] or [i for i in range(1, amount) if holding[i] < reach]
        pool, remaining = sum([weights[i] for i in candidates]), surplus
        for i in candidates:
            addition = min(reach - holding[i], max(1, remaining * weights[i] // pool), surplus)
            holding[i] = holding[i] + addition
            surplus = surplus - addition
    return np.array(holding)


def centred(key, shape, deviation, reach, shards=(), kind=jnp.bfloat16):
    values = deviation * jax.random.normal(key, shape, jnp.float32)
    if shards:
        values = values * level_of(key, shape, shards, -0.22, 0.18)
    return jnp.clip(values, -reach, reach).astype(kind)


def setup_inputs(seed: int = 0) -> dict:
    seeds = jax.random.split(jax.random.key(seed), 9)
    forcing = centred(seeds[0], (3, BLOCKS, CELLS), 1.0, 6.0, ((1, 32),), jnp.float32)
    viscosity = jnp.clip(jnp.exp(math.log(10.0) - 4.6051702 * jax.random.uniform(seeds[1], (BLOCKS, CELLS), jnp.float32) ** level_of(seeds[1], (BLOCKS, CELLS), ((0, 32),), -0.2, 0.2)), 0.1, 10.0)
    refinement = place_ends(jax.random.randint(seeds[2], (BLOCKS,), 0, 2), jax.random.fold_in(seeds[2], 1), 0, 1).astype(jnp.int32)
    face_owner_keys = jax.random.split(jax.random.fold_in(seeds[3], 1), (4 * BLOCKS) // (4 * B_DEV))
    face_owner_turns = jax.random.permutation(jax.random.fold_in(seeds[3], 3), (4 * BLOCKS) // (4 * B_DEV))
    face_owner = jax.vmap(lambda own, number: shared_out(jax.random.fold_in(seeds[3], 2), own, number, 4 * B_DEV, N_MEM, 1, CAP, 2))(face_owner_keys, face_owner_turns).reshape((4 * BLOCKS, 1))
    face_block = place_ends(jax.random.randint(seeds[4], (BLOCKS, 4), 0, B_DEV), jax.random.fold_in(seeds[4], 1), 0, B_DEV - 1).astype(jnp.int32)
    plane_block = place_ends(jax.random.randint(seeds[5], (BLOCKS, 2), 0, B_DEV), jax.random.fold_in(seeds[5], 1), 0, B_DEV - 1).astype(jnp.int32)
    hanging = place_ends((jax.random.randint(seeds[6], (BLOCKS, 6), 0, 4) < 1).astype(jnp.int32), jax.random.fold_in(seeds[6], 1), 0, 1)
    coarse_solver = centred(seeds[7], (N_GRP, NC, NC), NC ** -0.5, 0.4375, ((0, 4), (1, 8)), jnp.float32)
    return {"forcing": forcing, "viscosity": viscosity, "refinement": refinement, "face_owner": face_owner, "face_block": face_block, "plane_block": plane_block, "hanging": hanging, "coarse_solver": coarse_solver}


MASS_TERM = 1.0
LOWER_BOUND = 0.25
UPPER_BOUND = 2.0

def face_set(values):
    leading = values.shape[:-1]
    cube_view = values.reshape(leading + (EDGE, EDGE, EDGE))
    return [cube_view[..., 0].reshape(leading + (FACE,)), cube_view[..., EDGE - 1].reshape(leading + (FACE,)), cube_view[..., :, 0, :].reshape(leading + (FACE,)), cube_view[..., :, EDGE - 1, :].reshape(leading + (FACE,)), cube_view[..., 0, :, :].reshape(leading + (FACE,)), cube_view[..., EDGE - 1, :, :].reshape(leading + (FACE,))]

def coarsen(plane_vals):
    leading = plane_vals.shape[:-1]
    squares = plane_vals.reshape(leading + (EDGE // 2, 2, EDGE // 2, 2))
    average = lax.optimization_barrier(jnp.mean(squares, axis=(-3, -1), keepdims=True))
    return jnp.broadcast_to(average, squares.shape).reshape(leading + (FACE,))

def spread(plane_vals):
    leading = plane_vals.shape[:-1]
    shaped = plane_vals.reshape(leading + (EDGE, 1, EDGE))
    return jnp.broadcast_to(shaped, leading + (EDGE, EDGE, EDGE)).reshape(leading + (CELLS,))

def beside(values, ghosts):
    leading = values.shape[:-1]
    cell_index = jnp.arange(CELLS, dtype=jnp.int32)
    along_k = cell_index % EDGE
    along_j = cell_index // EDGE % EDGE
    zero_one = jnp.zeros(leading + (1,), jnp.float32)
    zero_row = jnp.zeros(leading + (EDGE,), jnp.float32)
    return [jnp.where(along_k == 0, jnp.repeat(ghosts[0], EDGE, axis=-1), jnp.concatenate([zero_one, values[..., :-1]], axis=-1)), jnp.where(along_k == EDGE - 1, jnp.repeat(ghosts[1], EDGE, axis=-1), jnp.concatenate([values[..., 1:], zero_one], axis=-1)), jnp.where(along_j == 0, spread(ghosts[2]), jnp.concatenate([zero_row, values[..., :-EDGE]], axis=-1)), jnp.where(along_j == EDGE - 1, spread(ghosts[3]), jnp.concatenate([values[..., EDGE:], zero_row], axis=-1)), jnp.concatenate([ghosts[4], values[..., :-FACE]], axis=-1), jnp.concatenate([values[..., FACE:], ghosts[5]], axis=-1)]

def reference(forcing, viscosity, refinement, face_owner, face_block, plane_block, hanging, coarse_solver):
    effective = viscosity * jnp.exp2(-refinement.astype(jnp.float32))[:, None]
    stride = N_MEM * B_DEV
    block_ids = jnp.arange(BLOCKS, dtype=jnp.int32)
    group_base = block_ids // stride * stride
    local_idx = block_ids % B_DEV
    owners = face_owner.reshape(BLOCKS, 4)
    sources = [group_base + owners[:, direction] * B_DEV + face_block[:, direction] for direction in range(4)]
    lower_src = jnp.clip(block_ids - stride - local_idx + plane_block[:, 0], 0, BLOCKS - 1).astype(jnp.int32)
    upper_src = jnp.clip(block_ids + stride - local_idx + plane_block[:, 1], 0, BLOCKS - 1).astype(jnp.int32)
    lower_valid = block_ids >= stride
    upper_valid = block_ids < BLOCKS - stride

    def ghost_set(stacked):
        planes = face_set(stacked)
        result = []
        for direction in range(4):
            result.append(planes[direction ^ 1][:, sources[direction]])
        result.append(jnp.where(lower_valid[None, :, None], planes[5][:, lower_src], 0.0))
        result.append(jnp.where(upper_valid[None, :, None], planes[4][:, upper_src], 0.0))
        return [jnp.where(hanging[:, direction][None, :, None] == 1, coarsen(result[direction]), result[direction]) for direction in range(6)]
    nearby_eff = beside(effective[None], ghost_set(effective[None]))
    weights = [0.5 * (effective + nearby_eff[direction][0]) for direction in range(6)]
    diagonal = MASS_TERM * effective
    for direction in range(6):
        diagonal = diagonal + weights[direction]

    def operate(values):
        nearby = beside(values, ghost_set(values))
        applied = diagonal * values
        for direction in range(6):
            applied = applied - weights[direction] * nearby[direction]
        return applied
    midpoint = 0.5 * (UPPER_BOUND + LOWER_BOUND)
    half_width = 0.5 * (UPPER_BOUND - LOWER_BOUND)
    sigma_ratio = midpoint / half_width

    def smooth(solution, residual):
        rho_now = 1.0 / sigma_ratio
        step_dir = residual / (diagonal * midpoint)
        for sweep_index in range(DEG):
            solution = solution + step_dir
            residual = residual - operate(step_dir)
            if sweep_index < DEG - 1:
                rho_next = 1.0 / (2.0 * sigma_ratio - rho_now)
                step_dir = rho_next * rho_now * step_dir + 2.0 * rho_next / half_width * (residual / diagonal)
                rho_now = rho_next
        return (solution, residual)
    solution, residual = smooth(jnp.zeros_like(forcing), forcing)
    coarse_vec = (lax.optimization_barrier(jnp.sum(residual, axis=-1)) / math.sqrt(CELLS)).T.reshape(N_GRP, NC)
    correction = jnp.einsum('gij,gj->gi', coarse_solver, coarse_vec, precision=lax.Precision.HIGHEST)
    lifted = jnp.broadcast_to(correction.reshape(BLOCKS, 3).T[:, :, None], forcing.shape)
    solution = solution + lifted
    residual = residual - operate(lifted)
    solution, residual = smooth(solution, residual)
    return (solution, residual)
```

```python
import functools
import math

import jax
import jax.numpy as jnp
from jax import lax
from jax.experimental import pallas as pl
from jax.experimental.pallas import tpu as pltpu
from jax.sharding import PartitionSpec as P

EDGE = 16
DEG = 3
CELLS = 4096
MASS_TERM = 1.0
LOWER_BOUND = 0.25
UPPER_BOUND = 2.0
THETA = 0.5 * (UPPER_BOUND + LOWER_BOUND)
DELTA = 0.5 * (UPPER_BOUND - LOWER_BOUND)
SIGMA = THETA / DELTA

LANES = 128
BLK = 8
TILES = CELLS // LANES
F32 = jnp.float32
VMEM = pl.BlockSpec(memory_space=pltpu.VMEM)
SMEM = pl.BlockSpec(memory_space=pltpu.SMEM)
PARAMS = pltpu.CompilerParams(vmem_limit_bytes=28 * 1024 * 1024)


def lane_id():
    return lax.broadcasted_iota(jnp.int32, (BLK, LANES), 1)


def sub_id():
    return lax.broadcasted_iota(jnp.int32, (BLK, LANES), 0)


def roll(v, shift):
    shift = shift % LANES
    return v if shift == 0 else pltpu.roll(v, shift, 1)


def tile(m):
    return slice(m * LANES, (m + 1) * LANES)


def pack_faces(values, lane):
    k, g = lane & 15, lane >> 4
    faces = [[], [], [], []]
    for p in range(2):
        low = high = None
        for t in range(16):
            moved = roll(values[16 * p + t], t)
            low = moved if t == 0 else jnp.where(k == t, moved, low)
            high = moved if t == 0 else jnp.where(k == (15 + t) % 16, moved, high)
        faces[0].append(low)
        faces[1].append(roll(high, -15))
        low = high = None
        for t in range(8):
            i = 8 * p + t
            first = roll(values[2 * i], 16 * t)
            last = roll(values[2 * i + 1], 16 * t + 16)
            low = first if t == 0 else jnp.where(g == t, first, low)
            high = last if t == 0 else jnp.where(g == t, last, high)
        faces[2].append(low)
        faces[3].append(high)
    return faces


def mean_squares(v, lane, bit):
    for n in (bit, 16):
        v = v + jnp.where((lane & n) == 0, roll(v, -n), roll(v, n))
    return v * 0.25


def unpack_k(low, high, lane, m):
    t = m % 16
    return jnp.where((lane & 15) == 0, roll(low[m // 16], -t), roll(high[m // 16], 15 - t))


def unpack_j(low, high, m):
    i = m // 2
    if m % 2 == 0:
        return roll(low[i // 8], -16 * (i % 8))
    return roll(high[i // 8], 112 - 16 * (i % 8))


def gather_ghosts(starts, stride, near, first, second, meta, plane_block, hanging, ghosts, planes, lane, rows):
    even = meta[0] == 1
    has_lower, has_upper = meta[1] == 1, meta[2] == 1
    for n in range(rows):
        span = slice(n * BLK, (n + 1) * BLK)
        a, b = first[span, :], second[span, :]
        planes[span, :] = jnp.where(has_lower, jnp.where(even, b, a), 0.0)
        span_up = slice((rows + n) * BLK, (rows + n + 1) * BLK)
        planes[span_up, :] = jnp.where(has_upper, jnp.where(even, a, b), 0.0)
    for b in range(BLK):
        for d in range(4):
            row = near[pl.ds(starts(b, d), rows, stride=stride), :]
            ghosts[pl.ds(d * rows * BLK + b, rows, stride=BLK), :] = row
        for d in range(2):
            row = planes[pl.ds(d * rows * BLK + plane_block[b, d], rows, stride=BLK), :]
            ghosts[pl.ds((4 + d) * rows * BLK + b, rows, stride=BLK), :] = row
    result = []
    for d in range(6):
        hang = jnp.broadcast_to(hanging[:, d : d + 1], (BLK, LANES)) == 1
        tiles = []
        for n in range(rows):
            v = ghosts[(d * rows + n) * BLK : (d * rows + n + 1) * BLK, :]
            tiles.append(jnp.where(hang, mean_squares(v, lane, 2 if d < 2 else 1), v))
        result.append(tiles)
    return result


def emit_planes(low, high, even, first, second):
    for n in range(len(low)):
        span = slice(n * BLK, (n + 1) * BLK)
        first[span, :] = jnp.where(even, high[n], low[n])
        second[span, :] = jnp.where(even, low[n], high[n])


def emit_faces(values, chosen, meta, payload, first, second, faces, lane, members, cap):
    low, high = [], []
    for c in range(3):
        packed = pack_faces(values[c], lane)
        for f in range(4):
            for p in range(2):
                at = (f * 6 + c * 2 + p) * BLK
                faces[at : at + BLK, :] = packed[f][p]
        low += values[c][:2]
        high += values[c][-2:]
    emit_planes(low, high, meta[0] == 1, first, second)
    for n in range(members * cap):
        member, slot = divmod(n, cap)
        row = faces[pl.ds(chosen[n], 6, stride=BLK), :]
        payload[pl.ds(member * 6 * cap + slot, 6, stride=cap), :] = row


def prepare_kernel(
    members, groups, cap, viscosity, refinement, face_owner, face_block, coarse_rows,
    eff, payload, first, second, meta, starts, wants, faces, count,
):
    lane, sub = lane_id(), sub_id()
    group, member = lax.axis_index("grp"), lax.axis_index("mem")
    even = group % 2 == 0
    meta[0] = jnp.where(even, 1, 0)
    meta[1] = jnp.where(group > 0, 1, 0)
    meta[2] = jnp.where(group < groups - 1, 1, 0)
    meta[3] = member
    meta[4] = group
    level = jnp.zeros((BLK, LANES), jnp.int32)
    for b in range(BLK):
        level = jnp.where(sub == b, refinement[b], level)
    scale = jnp.exp2(-level.astype(F32))
    values = []
    for m in range(TILES):
        v = viscosity[:, tile(m)] * scale
        eff[:, tile(m)] = v
        values.append(v)
    packed = pack_faces(values, lane)
    per = 64 + BLK + 24
    for f in range(4):
        for p in range(2):
            at = (f * 2 + p) * BLK
            for n in range(members):
                payload[n * per + at : n * per + at + BLK, :] = packed[f][p]
    emit_planes(values[:2], values[-2:], even, first, second)
    columns = BLK * 3
    wide = lax.broadcasted_iota(jnp.int32, (24, LANES), 1)
    for n in range(members):
        payload[n * per + 64 : n * per + 72, :] = jnp.zeros((BLK, LANES), F32)
        at, off = divmod(n * columns, LANES)
        have = coarse_rows[:, tile(at)]
        part = have if off == 0 else pltpu.roll(have, LANES - off, 1)
        if off + columns > LANES:
            more = pltpu.roll(coarse_rows[:, tile(at + 1)], LANES - off, 1)
            part = jnp.where(wide < LANES - off, part, more)
        payload[n * per + 72 : n * per + per, :] = jnp.where(wide < columns, part, 0.0)
        count[n] = 0
    for b in range(BLK):
        for d in range(4):
            owner = face_owner[b * 4 + d, 0]
            slot = count[owner]
            count[owner] = slot + 1
            starts[b * 4 + d] = owner * 6 * cap + slot
            want = (d ^ 1) * 6 * BLK + face_block[b, d]
            payload[pl.ds(owner * per + 64 + slot, 1), :] = jnp.full((1, LANES), want, jnp.int32).astype(F32)
            wants[b * 4 + d] = owner * per + (d ^ 1) * 2 * BLK + face_block[b, d]


def weights_kernel(
    members, cap, near, from_first, from_second, eff, forcing, meta, wants, plane_block, hanging, chosen,
    step, payload, first, second, wi, gk, gj, gi, diagonal, inverse, faces, ghosts, planes,
):
    lane = lane_id()
    k, g = lane & 15, lane >> 4
    ghost = gather_ghosts(
        lambda b, d: wants[b * 4 + d], BLK, near, from_first, from_second, meta, plane_block, hanging,
        ghosts, planes, lane, 2,
    )
    values = [eff[:, tile(m)] for m in range(TILES)]
    start = [[], [], []]
    for m in range(TILES):
        i, h = divmod(m, 2)
        e = values[m]
        side_k = unpack_k(ghost[0], ghost[1], lane, m)
        side_j = unpack_j(ghost[2], ghost[3], m)
        ends_j = (g == 0) if h == 0 else (g == 7)
        n0 = jnp.where(k == 0, side_k, roll(e, 1))
        n1 = jnp.where(k == 15, side_k, roll(e, -1))
        n2 = jnp.where(g == 0, side_j if h == 0 else roll(values[m - 1], 16), roll(e, 16))
        n3 = jnp.where(g == 7, side_j if h == 1 else roll(values[m + 1], -16), roll(e, -16))
        n4 = ghost[4][h] if i == 0 else values[m - 2]
        n5 = ghost[5][h] if i == EDGE - 1 else values[m + 2]
        w = [0.5 * (e + n) for n in (n0, n1, n2, n3, n4, n5)]
        diag = MASS_TERM * e
        for d in range(6):
            diag = diag + w[d]
        inv = 1.0 / diag
        diagonal[:, tile(m)] = diag
        inverse[:, tile(m)] = inv
        wi[0, :, tile(m)] = jnp.where(k == 0, 0.0, w[0])
        wi[1, :, tile(m)] = jnp.where(k == 15, 0.0, w[1])
        wi[2, :, tile(m)] = jnp.where(ends_j, 0.0, w[2]) if h == 0 else w[2]
        wi[3, :, tile(m)] = jnp.where(ends_j, 0.0, w[3]) if h == 1 else w[3]
        wi[4, :, tile(m)] = w[4]
        gk[:, tile(m)] = jnp.where(k == 0, w[0], jnp.where(k == 15, w[1], 0.0))
        gj[:, tile(m)] = jnp.where(ends_j, w[2 + h], 0.0)
        if i == 0:
            gi[:, tile(h)] = w[4]
        if i == EDGE - 1:
            gi[:, tile(2 + h)] = w[5]
        scale = inv * (1.0 / THETA)
        for c in range(3):
            s = forcing[c, :, tile(m)] * scale
            step[c, :, tile(m)] = s
            start[c].append(s)
    emit_faces(start, chosen, meta, payload, first, second, faces, lane, members, cap)


def inside_kernel(has_x, has_lift, *refs):
    refs = list(refs)
    residual, step, wi, diagonal = refs[:4]
    refs = refs[4:]
    x = refs.pop(0) if has_x else None
    lift = refs.pop(0) if has_lift else None
    new_residual = refs.pop(0)
    new_x = refs.pop(0) if has_x else None
    g = lane_id() >> 4
    for c in range(3):
        up = None if not has_lift else lift[c * BLK : (c + 1) * BLK, :]
        for m in range(TILES):
            i, h = divmod(m, 2)
            s = step[c, :, tile(m)]
            n2, n3 = roll(s, 16), roll(s, -16)
            if h == 1:
                n2 = jnp.where(g == 0, roll(step[c, :, tile(m - 1)], 16), n2)
            else:
                n3 = jnp.where(g == 7, roll(step[c, :, tile(m + 1)], -16), n3)
            acc = residual[c, :, tile(m)] - diagonal[:, tile(m)] * s
            acc = acc + wi[0, :, tile(m)] * roll(s, 1)
            acc = acc + wi[1, :, tile(m)] * roll(s, -1)
            acc = acc + wi[2, :, tile(m)] * n2
            acc = acc + wi[3, :, tile(m)] * n3
            if i > 0:
                acc = acc + wi[4, :, tile(m)] * step[c, :, tile(m - 2)]
            if i < EDGE - 1:
                acc = acc + wi[4, :, tile(m + 2)] * step[c, :, tile(m + 2)]
            new_residual[c, :, tile(m)] = acc
            if has_x:
                total = x[c, :, tile(m)] + s
                if has_lift:
                    total = total + up
                new_x[c, :, tile(m)] = total


def add_ghosts(c, m, value, ghost, gk, gj, gi, lane):
    i, h = divmod(m, 2)
    pair = slice(2 * c, 2 * c + 2)
    value = value + gk[:, tile(m)] * unpack_k(ghost[0][pair], ghost[1][pair], lane, m)
    value = value + gj[:, tile(m)] * unpack_j(ghost[2][pair], ghost[3][pair], m)
    if i == 0:
        value = value + gi[:, tile(h)] * ghost[4][2 * c + h]
    if i == EDGE - 1:
        value = value + gi[:, tile(2 + h)] * ghost[5][2 * c + h]
    return value


def outside_kernel(
    members, cap, old, new, near, from_first, from_second, residual, step, inverse, gk, gj, gi,
    meta, starts, plane_block, hanging, chosen,
    new_residual, new_step, payload, first, second, faces, ghosts, planes,
):
    lane = lane_id()
    ghost = gather_ghosts(
        lambda b, d: starts[b * 4 + d], cap, near, from_first, from_second, meta, plane_block, hanging,
        ghosts, planes, lane, 6,
    )
    values = [[], [], []]
    for c in range(3):
        for m in range(TILES):
            r = add_ghosts(c, m, residual[c, :, tile(m)], ghost, gk, gj, gi, lane)
            new_residual[c, :, tile(m)] = r
            s = old * step[c, :, tile(m)] + new * (r * inverse[:, tile(m)])
            new_step[c, :, tile(m)] = s
            values[c].append(s)
    emit_faces(values, chosen, meta, payload, first, second, faces, lane, members, cap)


def last_kernel(
    cap, near, from_first, from_second, residual, gk, gj, gi, meta, starts, plane_block, hanging,
    new_residual, ghosts, planes,
):
    lane = lane_id()
    ghost = gather_ghosts(
        lambda b, d: starts[b * 4 + d], cap, near, from_first, from_second, meta, plane_block, hanging,
        ghosts, planes, lane, 6,
    )
    for c in range(3):
        for m in range(TILES):
            new_residual[c, :, tile(m)] = add_ghosts(c, m, residual[c, :, tile(m)], ghost, gk, gj, gi, lane)


def coarse_kernel(
    members, devices, cap, near, from_first, from_second, residual, gk, gj, gi, meta, starts, plane_block, hanging,
    coarse, new_residual, payload, ghosts, planes,
):
    lane, sub = lane_id(), sub_id()
    ghost = gather_ghosts(
        lambda b, d: starts[b * 4 + d], cap, near, from_first, from_second, meta, plane_block, hanging,
        ghosts, planes, lane, 6,
    )
    placed = jnp.zeros((BLK, LANES), F32)
    for c in range(3):
        sums = [None] * 4
        for m in range(TILES):
            r = add_ghosts(c, m, residual[c, :, tile(m)], ghost, gk, gj, gi, lane)
            new_residual[c, :, tile(m)] = r
            sums[m % 4] = r if sums[m % 4] is None else sums[m % 4] + r
        total = (sums[0] + sums[1]) + (sums[2] + sums[3])
        total = jnp.broadcast_to(jnp.sum(total, axis=1, keepdims=True), (BLK, LANES))
        placed = jnp.where(lane == 3 * sub + c, total, placed)
    own = jnp.sum(placed, axis=0, keepdims=True) * (1.0 / math.sqrt(CELLS))
    own = jnp.broadcast_to(own, (BLK, LANES))
    unknowns = members * BLK * 3
    wide = -(-unknowns // LANES)
    rows = [jnp.zeros((BLK, LANES), F32) for _ in range(wide)]
    per = 64 + BLK + 24
    for n in range(members):
        for v in range(3):
            at = n * per + 72 + v * BLK
            part = jnp.sum(coarse[at : at + BLK, :] * own, axis=1, keepdims=True)
            part = jnp.broadcast_to(part, (BLK, LANES))
            place = n * 24 + v * BLK
            for t in range(place // LANES, (place + BLK - 1) // LANES + 1):
                rows[t] = jnp.where(lane + t * LANES == place + sub, part, rows[t])
    out = jnp.zeros((BLK, LANES), F32)
    for t in range(wide):
        out = jnp.where(sub == t, jnp.sum(rows[t], axis=0, keepdims=True), out)
    for n in range(devices):
        payload[n * BLK : (n + 1) * BLK, :] = out


def lift_kernel(
    members, cap, arrived, residual, eff, inverse, gk, gj, gi, meta, face_owner, face_block, plane_block, chosen,
    new_residual, step, lift, payload, first, second, faces,
):
    lane, sub = lane_id(), sub_id()
    k = lane & 15
    wide = -(-members * BLK * 3 // LANES)
    group, member = meta[4], meta[3]
    base = [
        jnp.where(meta[1] == 1, group - 1, group), group, jnp.where(meta[2] == 1, group + 1, group)
    ]
    known = []
    for n in range(3):
        total = jnp.zeros((BLK, LANES), F32)
        for p in range(members):
            at = pl.multiple_of((base[n] * members + p) * BLK, BLK)
            total = total + arrived[pl.ds(at, BLK), :]
        if n != 1:
            total = jnp.where(meta[1 if n == 0 else 2] == 1, total, 0.0)
        known.append([jnp.broadcast_to(total[t : t + 1, :], (BLK, LANES)) for t in range(wide)])

    def look_up(table, block):
        index = jnp.zeros((BLK, LANES), jnp.int32)
        for b in range(BLK):
            index = jnp.where(sub == b, 3 * block(b), index)
        found = []
        for c in range(3):
            total = jnp.zeros((BLK, LANES), F32)
            for t in range(wide):
                total = total + jnp.where(lane + t * LANES == index + c, table[t], 0.0)
            found.append(jnp.broadcast_to(jnp.sum(total, axis=1, keepdims=True), (BLK, LANES)))
        return found

    own = look_up(known[1], lambda b: member * BLK + b)
    side = [look_up(known[1], lambda b, d=d: face_owner[b * 4 + d, 0] * BLK + face_block[b, d]) for d in range(4)]
    below = look_up(known[0], lambda b: member * BLK + plane_block[b, 0])
    above = look_up(known[2], lambda b: member * BLK + plane_block[b, 1])
    values = [[], [], []]
    for c in range(3):
        lift[c * BLK : (c + 1) * BLK, :] = own[c]
        drop_k = own[c] - jnp.where(k == 0, side[0][c], side[1][c])
        drop_j = [own[c] - side[2][c], own[c] - side[3][c]]
        drop_i = [own[c] - below[c], own[c] - above[c]]
        for m in range(TILES):
            i, h = divmod(m, 2)
            applied = (MASS_TERM * eff[:, tile(m)]) * own[c]
            applied = applied + gk[:, tile(m)] * drop_k + gj[:, tile(m)] * drop_j[h]
            if i == 0:
                applied = applied + gi[:, tile(h)] * drop_i[0]
            if i == EDGE - 1:
                applied = applied + gi[:, tile(2 + h)] * drop_i[1]
            r = residual[c, :, tile(m)] - applied
            new_residual[c, :, tile(m)] = r
            s = r * (inverse[:, tile(m)] * (1.0 / THETA))
            step[c, :, tile(m)] = s
            values[c].append(s)
    emit_faces(values, chosen, meta, payload, first, second, faces, lane, members, cap)


def local(
    forcing, viscosity, refinement, face_owner, face_block, plane_block, hanging, coarse_solver
):
    groups, members = lax.axis_size("grp"), lax.axis_size("mem")
    cap = 8 * BLK // members
    devices = groups * members
    field = jax.ShapeDtypeStruct(forcing.shape, F32)
    scalar_field = jax.ShapeDtypeStruct(viscosity.shape, F32)

    def array(*shape):
        return jax.ShapeDtypeStruct(shape, F32)

    def ints(n):
        return jax.ShapeDtypeStruct((n,), jnp.int32)

    def scratch(*shape):
        return pltpu.VMEM(shape, F32)

    def call(body, in_specs, out_shape, out_specs, scratch_shapes, name, flops=2_000_000, moved=2_000_000):
        return pl.pallas_call(
            body,
            out_shape=out_shape,
            in_specs=in_specs,
            out_specs=out_specs,
            scratch_shapes=scratch_shapes,
            compiler_params=PARAMS,
            cost_estimate=pl.CostEstimate(flops=flops, bytes_accessed=moved, transcendentals=0),
            name=name,
        )

    first_route = [(q * members + m, (q ^ 1) * members + m) for q in range(groups) for m in range(members)]
    second_route = []
    for q in range(groups):
        for m in range(members):
            if q == 0 or q == groups - 1:
                second_route.append((q * members + m, q * members + (m ^ 1)))
            else:
                second_route.append((q * members + m, (q + 1 if q % 2 else q - 1) * members + m))

    def exchange(payload, first, second):
        near = payload.reshape(members, -1, LANES)
        near = lax.all_to_all(near, "mem", split_axis=0, concat_axis=0, tiled=True)
        first = lax.ppermute(first, ("grp", "mem"), first_route)
        second = lax.ppermute(second, ("grp", "mem"), second_route)
        return near.reshape(-1, LANES), first, second

    per = 64 + BLK + 24
    solver_rows = jnp.pad(coarse_solver[0], ((0, 0), (0, -coarse_solver.shape[2] % LANES)))
    eff, payload, first, second, meta, starts, wants = call(
        functools.partial(prepare_kernel, members, groups, cap),
        [VMEM, SMEM, SMEM, SMEM, VMEM],
        [scalar_field, array(members * per, LANES), array(16, LANES), array(16, LANES), ints(8), ints(32), ints(32)],
        [VMEM] * 4 + [SMEM] * 3,
        [scratch(4 * 16, LANES), pltpu.SMEM((members,), jnp.int32)],
        "prepare",
    )(viscosity, refinement, face_owner, face_block, solver_rows)
    arrived, from_first, from_second = exchange(payload, first, second)
    chosen = arrived.reshape(members, per, LANES)[:, 64 : 64 + cap, 0].astype(jnp.int32).reshape(-1)

    payload_out = [array(members * 6 * cap, LANES), array(48, LANES), array(48, LANES)]
    face_scratch = scratch(4 * 48, LANES)
    ghost_scratch = [scratch(6 * 48, LANES), scratch(2 * 48, LANES)]

    step, payload, first, second, wi, gk, gj, gi, diagonal, inverse = call(
        functools.partial(weights_kernel, members, cap),
        [VMEM] * 5 + [SMEM] * 3 + [VMEM, SMEM],
        [field] + payload_out
        + [array(5, BLK, CELLS), scalar_field, scalar_field, array(BLK, 4 * LANES), scalar_field, scalar_field],
        [VMEM] * 10,
        [face_scratch, scratch(6 * 16, LANES), scratch(2 * 16, LANES)],
        "weights",
    )(arrived, from_first, from_second, eff, forcing, meta, wants, plane_block, hanging, chosen)

    def inside(residual, step, x=None, lift=None):
        operands = [residual, step, wi, diagonal] + [a for a in (x, lift) if a is not None]
        out = [field] + ([field] if x is not None else [])
        result = call(
            functools.partial(inside_kernel, x is not None, lift is not None),
            [VMEM] * len(operands), out, [VMEM] * len(out), [], "inside",
        )(*operands)
        return result if x is not None else (result[0], step)

    def outside(arrived, from_first, from_second, residual, step, old, new):
        return call(
            functools.partial(outside_kernel, members, cap, old, new),
            [VMEM] * 9 + [SMEM] * 3 + [VMEM, SMEM],
            [field, field] + payload_out,
            [VMEM] * 5,
            [face_scratch] + ghost_scratch,
            "outside",
        )(arrived, from_first, from_second, residual, step, inverse, gk, gj, gi, meta, starts, plane_block, hanging, chosen)

    rho = 1.0 / SIGMA
    factors = []
    for _ in range(DEG - 1):
        rho_next = 1.0 / (2.0 * SIGMA - rho)
        factors.append((rho_next * rho, 2.0 * rho_next / DELTA))
        rho = rho_next

    def steps(residual, step, payload, first, second, x, lift):
        for old, new in factors:
            arrived, from_first, from_second = exchange(payload, first, second)
            residual, x = inside(residual, step, x, lift)
            lift = None
            residual, step, payload, first, second = outside(
                arrived, from_first, from_second, residual, step, old, new
            )
        arrived, from_first, from_second = exchange(payload, first, second)
        residual, x = inside(residual, step, x, lift)
        return arrived, from_first, from_second, residual, x

    coarse_table = arrived
    arrived, from_first, from_second, residual, x = steps(forcing, step, payload, first, second, None, None)
    residual, payload = call(
        functools.partial(coarse_kernel, members, devices, cap),
        [VMEM] * 7 + [SMEM] * 3 + [VMEM, VMEM],
        [field, array(devices * BLK, LANES)],
        [VMEM] * 2,
        ghost_scratch,
        "coarse",
    )(arrived, from_first, from_second, residual, gk, gj, gi, meta, starts, plane_block, hanging, coarse_table)
    sums = payload.reshape(devices, BLK, LANES)
    sums = lax.all_to_all(sums, ("grp", "mem"), split_axis=0, concat_axis=0, tiled=True).reshape(-1, LANES)
    residual, step, lift, payload, first, second = call(
        functools.partial(lift_kernel, members, cap),
        [VMEM] * 7 + [SMEM] * 5,
        [field, field, array(3 * BLK, LANES)] + payload_out,
        [VMEM] * 6,
        [face_scratch],
        "lift",
    )(sums, residual, eff, inverse, gk, gj, gi, meta, face_owner, face_block, plane_block, chosen)
    arrived, from_first, from_second, residual, x = steps(residual, step, payload, first, second, x, lift)
    residual = call(
        functools.partial(last_kernel, cap),
        [VMEM] * 7 + [SMEM] * 3 + [VMEM],
        [field],
        [VMEM],
        ghost_scratch,
        "last",
    )(arrived, from_first, from_second, residual, gk, gj, gi, meta, starts, plane_block, hanging)[0]
    return x, residual


def solution(mesh):
    in_specs = (
        P(None, ("grp", "mem"), None),
        P(("grp", "mem"), None),
        P(("grp", "mem")),
        P(("grp", "mem"), None),
        P(("grp", "mem"), None),
        P(("grp", "mem"), None),
        P(("grp", "mem"), None),
        P("grp", "mem", None),
    )
    out_specs = (P(None, ("grp", "mem"), None), P(None, ("grp", "mem"), None))
    return jax.shard_map(local, mesh=mesh, in_specs=in_specs, out_specs=out_specs, check_vma=False)
```

```python
import functools
import math

import jax
import jax.numpy as jnp
from jax import lax
from jax.experimental import pallas as pl
from jax.experimental.pallas import tpu as pltpu
from jax.sharding import PartitionSpec as P

EDGE = 16
DEG = 3
CELLS = 4096
MASS_TERM = 1.0
LOWER_BOUND = 0.25
UPPER_BOUND = 2.0
THETA = 0.5 * (UPPER_BOUND + LOWER_BOUND)
DELTA = 0.5 * (UPPER_BOUND - LOWER_BOUND)
SIGMA = THETA / DELTA

LANES = 128
BLK = 8
TILES = CELLS // LANES
F32 = jnp.float32
VMEM = pl.BlockSpec(memory_space=pltpu.VMEM)
HBM = pl.BlockSpec(memory_space=pltpu.HBM)
PARAMS = pltpu.CompilerParams(vmem_limit_bytes=8 * 1024 * 1024)


def lane_id():
    return lax.broadcasted_iota(jnp.int32, (BLK, LANES), 1)


def sub_id():
    return lax.broadcasted_iota(jnp.int32, (BLK, LANES), 0)


def roll(v, shift):
    shift = shift % LANES
    return v if shift == 0 else pltpu.roll(v, shift, 1)


def tile(m):
    return slice(m * LANES, (m + 1) * LANES)


def pack_faces(values, lane):
    k, g = lane & 15, lane >> 4
    faces = [[], [], [], []]
    for p in range(2):
        low = high = None
        for t in range(16):
            moved = roll(values[16 * p + t], t)
            low = moved if t == 0 else jnp.where(k == t, moved, low)
            high = moved if t == 0 else jnp.where(k == (15 + t) % 16, moved, high)
        faces[0].append(low)
        faces[1].append(roll(high, -15))
        low = high = None
        for t in range(8):
            i = 8 * p + t
            first = roll(values[2 * i], 16 * t)
            last = roll(values[2 * i + 1], 16 * t + 16)
            low = first if t == 0 else jnp.where(g == t, first, low)
            high = last if t == 0 else jnp.where(g == t, last, high)
        faces[2].append(low)
        faces[3].append(high)
    return faces


def unpack_k(low, high, lane, m):
    t = m % 16
    return jnp.where((lane & 15) == 0, roll(low[m // 16], -t), roll(high[m // 16], 15 - t))


def unpack_j(low, high, m):
    i = m // 2
    if m % 2 == 0:
        return roll(low[i // 8], -16 * (i % 8))
    return roll(high[i // 8], 112 - 16 * (i % 8))


def pick(values, index):
    return jnp.take_along_axis(values, index, axis=0, mode="promise_in_bounds")


def lane_sum(v):
    return jnp.sum(v, axis=1, keepdims=True)


def splat(column):
    return jnp.broadcast_to(column, (BLK, LANES))


class Table:
    OWNER, SLOT, BLOCK, PLANE, EVEN, LOWER, UPPER, HANG = 0, 4, 8, 12, 14, 15, 16, 17
    SIZE = 23

    def __init__(self, ref):
        self.ref = ref

    def __call__(self, n):
        return self.ref[n * BLK : (n + 1) * BLK, :]


def gather_ghosts(near_tile, members, first, second, table, ghosts, lane, rows):
    even = table(Table.EVEN) == 1
    for d in range(6):
        for n in range(rows):
            if d < 4:
                v = None
                for m in range(members):
                    source, index = near_tile(m, d, n)
                    found = pick(source, index)
                    v = found if m == 0 else jnp.where(table(Table.OWNER + d) == m, found, v)
            else:
                a, b = first[n * BLK : (n + 1) * BLK, :], second[n * BLK : (n + 1) * BLK, :]
                v = jnp.where(even, b, a) if d == 4 else jnp.where(even, a, b)
                inside = table(Table.LOWER if d == 4 else Table.UPPER) == 1
                v = jnp.where(inside, pick(v, table(Table.PLANE + d - 4)), 0.0)
            at = (d * rows + n) * BLK
            ghosts[0, at : at + BLK, :] = v
    for stage in range(2):
        for d in range(6):
            bit = 16 if stage else (2 if d < 2 else 1)
            low = (lane & bit) == 0
            for n in range(rows):
                at = (d * rows + n) * BLK
                v = ghosts[stage, at : at + BLK, :]
                ghosts[stage + 1, at : at + BLK, :] = v + jnp.where(low, roll(v, -bit), roll(v, bit))
    result = []
    for d in range(6):
        hang = table(Table.HANG + d) == 1
        tiles = []
        for n in range(rows):
            at = (d * rows + n) * BLK
            tiles.append(jnp.where(hang, ghosts[2, at : at + BLK, :] * 0.25, ghosts[0, at : at + BLK, :]))
        result.append(tiles)
    return result


def step_ghosts(members, cap, near, first, second, table, ghosts, lane):
    def near_tile(m, d, n):
        start = n * cap
        at = start // BLK * BLK
        return near[m, at : at + BLK, :], table(Table.SLOT + d) + (start - at)

    return gather_ghosts(near_tile, members, first, second, table, ghosts, lane, 6)


def emit_planes(low, high, even, at, first, second):
    for n in range(2):
        span = slice((at + n) * BLK, (at + n + 1) * BLK)
        first[span, :] = jnp.where(even, high[n], low[n])
        second[span, :] = jnp.where(even, low[n], high[n])


def emit_channel(c, values, chosen, table, payload, first, second, staged, sems, lane, members, cap):
    packed = pack_faces(values, lane)
    emit_planes(values[:2], values[-2:], table(Table.EVEN) == 1, 2 * c, first, second)
    sub = sub_id()
    for m in range(members):
        want = chosen[m * BLK : (m + 1) * BLK, :]
        face, block = want >> 3, want & 7
        for u in range(2 * cap // BLK):
            out = None
            for p in range(2):
                if not u * BLK <= p * cap < (u + 1) * BLK:
                    continue
                v = None
                for f in range(4):
                    found = pick(packed[f][p], block)
                    v = found if f == 0 else jnp.where(face == f, found, v)
                out = v if out is None else jnp.where(sub < p * cap - u * BLK, out, v)
            at = c * 2 * cap + u * BLK
            staged[m, at : at + BLK, :] = out
    part = pl.ds(c * 2 * cap, 2 * cap)
    pltpu.make_async_copy(staged.at[:, part, :], payload.at[:, part, :], sems.at[c]).start()


def emit_wait(payload, staged, sems, cap):
    for c in range(3):
        part = pl.ds(c * 2 * cap, 2 * cap)
        pltpu.make_async_copy(staged.at[:, part, :], payload.at[:, part, :], sems.at[c]).wait()


def prepare_kernel(
    members, groups, cap, viscosity_hbm, refinement_hbm, owner_hbm, block_hbm, plane_hbm, hanging_hbm, coarse_rows,
    eff, payload, first, second, tables,
    viscosity, refinement, face_owner, face_block, plane_block, hanging, staged, sems, out_sem,
):
    copies = [
        pltpu.make_async_copy(source, target, sems.at[n])
        for n, (source, target) in enumerate(
            [
                (viscosity_hbm, viscosity), (refinement_hbm, refinement), (owner_hbm, face_owner),
                (block_hbm, face_block), (plane_hbm, plane_block), (hanging_hbm, hanging),
            ]
        )
    ]
    for copy in copies:
        copy.start()
    lane, sub = lane_id(), sub_id()
    group = lax.axis_index("grp")
    even = group % 2 == 0
    for copy in copies:
        copy.wait()

    def iotas(width):
        return (
            lax.broadcasted_iota(jnp.int32, (BLK, width), 1), lax.broadcasted_iota(jnp.int32, (BLK, width), 0)
        )

    lane8, sub8 = iotas(BLK)
    lane32, sub32 = iotas(4 * BLK)
    lane64, sub64 = iotas(members * cap)

    def column(row):
        wide = jnp.broadcast_to(row.astype(F32), (BLK, BLK))
        return lane_sum(jnp.where(lane8 == sub8, wide, 0.0))

    def put(n, value):
        tables[n * BLK : (n + 1) * BLK, :] = splat(value).astype(jnp.int32)

    scale = jnp.exp2(-splat(column(refinement[...])))
    values = []
    for m in range(TILES):
        v = viscosity[:, tile(m)] * scale
        eff[:, tile(m)] = v
        values.append(v)
    packed = pack_faces(values, lane)
    emit_planes(values[:2], values[-2:], even, 0, first, second)

    row = jnp.broadcast_to(face_owner[...].astype(F32), (BLK, 4 * BLK))
    wanted = jnp.zeros((BLK, members * cap), F32)
    for d in range(4):
        place = 4 * sub32 + d
        owner = lane_sum(jnp.where(lane32 == place, row, 0.0))
        slot = lane_sum(jnp.where((lane32 < place) & (row == owner), 1.0, 0.0))
        block = column(face_block[d : d + 1, :])
        put(Table.OWNER + d, owner)
        put(Table.SLOT + d, slot)
        put(Table.BLOCK + d, block)
        target = jnp.broadcast_to(owner * cap + slot, (BLK, members * cap))
        want = jnp.broadcast_to(block + (d ^ 1) * BLK, (BLK, members * cap))
        wanted = wanted + jnp.where(lane64.astype(F32) == target, want, 0.0)
    wanted = jnp.broadcast_to(jnp.sum(wanted, axis=0, keepdims=True), (BLK, members * cap))
    for d in range(2):
        put(Table.PLANE + d, column(plane_block[d : d + 1, :]))
    for n, flag in ((Table.EVEN, even), (Table.LOWER, group > 0), (Table.UPPER, group < groups - 1)):
        tables[n * BLK : (n + 1) * BLK, :] = jnp.full((BLK, LANES), jnp.where(flag, 1, 0), jnp.int32)
    for d in range(6):
        put(Table.HANG + d, hanging[:, d : d + 1])

    columns = BLK * 3
    for n in range(members):
        for f in range(4):
            for p in range(2):
                at = (f * 2 + p) * BLK
                staged[n, at : at + BLK, :] = packed[f][p]
        request = lane_sum(jnp.where(lane64 == n * cap + sub64 % cap, wanted, 0.0))
        last = splat(request)
        at, off = divmod(n * columns, LANES)
        for v in range(3):
            rows = slice(v * BLK, (v + 1) * BLK)
            part = roll(coarse_rows[rows, tile(at)], v * columns - off)
            if off + columns > LANES:
                more = roll(coarse_rows[rows, tile(at + 1)], v * columns - off)
                part = jnp.where(lane < v * columns + LANES - off, part, more)
            last = jnp.where((lane >= v * columns) & (lane < (v + 1) * columns), part, last)
        staged[n, 8 * BLK : 9 * BLK, :] = last
    copy = pltpu.make_async_copy(staged, payload, out_sem)
    copy.start()
    copy.wait()


def weights_kernel(
    members, cap, near, from_first, from_second, eff, forcing, tables,
    step, payload, first, second, wi, gk, gj, gi, diagonal, inverse, chosen, coarse, ghosts, staged, sems,
):
    lane = lane_id()
    k, g = lane & 15, lane >> 4
    table = Table(tables)
    for n in range(members):
        last = near[n, 8 * BLK : 9 * BLK, :]
        coarse[n * BLK : (n + 1) * BLK, :] = last
        chosen[n * BLK : (n + 1) * BLK, :] = splat(last[:, LANES - 1 :]).astype(jnp.int32)

    def near_tile(m, d, n):
        at = ((d ^ 1) * 2 + n) * BLK
        return near[m, at : at + BLK, :], table(Table.BLOCK + d)

    ghost = gather_ghosts(near_tile, members, from_first, from_second, table, ghosts, lane, 2)
    values = [eff[:, tile(m)] for m in range(TILES)]
    start = [[], [], []]
    for m in range(TILES):
        i, h = divmod(m, 2)
        e = values[m]
        side_k = unpack_k(ghost[0], ghost[1], lane, m)
        side_j = unpack_j(ghost[2], ghost[3], m)
        ends_j = (g == 0) if h == 0 else (g == 7)
        n0 = jnp.where(k == 0, side_k, roll(e, 1))
        n1 = jnp.where(k == 15, side_k, roll(e, -1))
        n2 = jnp.where(g == 0, side_j if h == 0 else roll(values[m - 1], 16), roll(e, 16))
        n3 = jnp.where(g == 7, side_j if h == 1 else roll(values[m + 1], -16), roll(e, -16))
        n4 = ghost[4][h] if i == 0 else values[m - 2]
        n5 = ghost[5][h] if i == EDGE - 1 else values[m + 2]
        w = [0.5 * (e + n) for n in (n0, n1, n2, n3, n4, n5)]
        diag = MASS_TERM * e
        for d in range(6):
            diag = diag + w[d]
        inv = 1.0 / diag
        diagonal[:, tile(m)] = diag
        inverse[:, tile(m)] = inv
        wi[0, :, tile(m)] = jnp.where(k == 0, 0.0, w[0])
        wi[1, :, tile(m)] = jnp.where(k == 15, 0.0, w[1])
        wi[2, :, tile(m)] = jnp.where(ends_j, 0.0, w[2]) if h == 0 else w[2]
        wi[3, :, tile(m)] = jnp.where(ends_j, 0.0, w[3]) if h == 1 else w[3]
        wi[4, :, tile(m)] = w[4]
        gk[:, tile(m)] = jnp.where(k == 0, w[0], jnp.where(k == 15, w[1], 0.0))
        gj[:, tile(m)] = jnp.where(ends_j, w[2 + h], 0.0)
        if i == 0:
            gi[:, tile(h)] = w[4]
        if i == EDGE - 1:
            gi[:, tile(2 + h)] = w[5]
        scale = inv * (1.0 / THETA)
        for c in range(3):
            s = forcing[c, :, tile(m)] * scale
            step[c, :, tile(m)] = s
            start[c].append(s)
    for c in range(3):
        emit_channel(c, start[c], chosen, table, payload, first, second, staged, sems, lane, members, cap)
    emit_wait(payload, staged, sems, cap)


def inside_kernel(has_x, has_lift, *refs):
    refs = list(refs)
    residual, step, wi, diagonal = refs[:4]
    refs = refs[4:]
    x = refs.pop(0) if has_x else None
    lift = refs.pop(0) if has_lift else None
    new_residual = refs.pop(0)
    new_x = refs.pop(0) if has_x else None
    g = lane_id() >> 4
    for c in range(3):
        up = None if not has_lift else lift[c * BLK : (c + 1) * BLK, :]
        for m in range(TILES):
            i, h = divmod(m, 2)
            s = step[c, :, tile(m)]
            n2, n3 = roll(s, 16), roll(s, -16)
            if h == 1:
                n2 = jnp.where(g == 0, roll(step[c, :, tile(m - 1)], 16), n2)
            else:
                n3 = jnp.where(g == 7, roll(step[c, :, tile(m + 1)], -16), n3)
            acc = residual[c, :, tile(m)] - diagonal[:, tile(m)] * s
            acc = acc + wi[0, :, tile(m)] * roll(s, 1)
            acc = acc + wi[1, :, tile(m)] * roll(s, -1)
            acc = acc + wi[2, :, tile(m)] * n2
            acc = acc + wi[3, :, tile(m)] * n3
            if i > 0:
                acc = acc + wi[4, :, tile(m)] * step[c, :, tile(m - 2)]
            if i < EDGE - 1:
                acc = acc + wi[4, :, tile(m + 2)] * step[c, :, tile(m + 2)]
            new_residual[c, :, tile(m)] = acc
            if has_x:
                total = x[c, :, tile(m)] + s
                if has_lift:
                    total = total + up
                new_x[c, :, tile(m)] = total


def add_ghosts(c, m, value, ghost, gk, gj, gi, lane):
    i, h = divmod(m, 2)
    pair = slice(2 * c, 2 * c + 2)
    value = value + gk[:, tile(m)] * unpack_k(ghost[0][pair], ghost[1][pair], lane, m)
    value = value + gj[:, tile(m)] * unpack_j(ghost[2][pair], ghost[3][pair], m)
    if i == 0:
        value = value + gi[:, tile(h)] * ghost[4][2 * c + h]
    if i == EDGE - 1:
        value = value + gi[:, tile(2 + h)] * ghost[5][2 * c + h]
    return value


def outside_kernel(
    members, cap, old, new, near, from_first, from_second, residual, step, inverse, gk, gj, gi, tables, chosen,
    new_residual, new_step, payload, first, second, ghosts, staged, sems,
):
    lane = lane_id()
    table = Table(tables)
    ghost = step_ghosts(members, cap, near, from_first, from_second, table, ghosts, lane)
    for c in range(3):
        values = []
        for m in range(TILES):
            r = add_ghosts(c, m, residual[c, :, tile(m)], ghost, gk, gj, gi, lane)
            new_residual[c, :, tile(m)] = r
            s = old * step[c, :, tile(m)] + new * (r * inverse[:, tile(m)])
            new_step[c, :, tile(m)] = s
            values.append(s)
        emit_channel(c, values, chosen, table, payload, first, second, staged, sems, lane, members, cap)
    emit_wait(payload, staged, sems, cap)


def last_kernel(
    members, cap, near, from_first, from_second, residual, gk, gj, gi, tables, new_residual, ghosts, staged, sems,
):
    lane = lane_id()
    ghost = step_ghosts(members, cap, near, from_first, from_second, Table(tables), ghosts, lane)
    copies = []
    for c in range(3):
        for m in range(TILES):
            staged[c, :, tile(m)] = add_ghosts(c, m, residual[c, :, tile(m)], ghost, gk, gj, gi, lane)
        copies.append(pltpu.make_async_copy(staged.at[c], new_residual.at[c], sems.at[c]))
        copies[c].start()
    for copy in copies:
        copy.wait()


def coarse_kernel(
    members, devices, cap, near, from_first, from_second, residual, gk, gj, gi, tables, coarse,
    new_residual, payload, ghosts,
):
    lane, sub = lane_id(), sub_id()
    ghost = step_ghosts(members, cap, near, from_first, from_second, Table(tables), ghosts, lane)
    placed = jnp.zeros((BLK, LANES), F32)
    for c in range(3):
        sums = [None] * 4
        for m in range(TILES):
            r = add_ghosts(c, m, residual[c, :, tile(m)], ghost, gk, gj, gi, lane)
            new_residual[c, :, tile(m)] = r
            sums[m % 4] = r if sums[m % 4] is None else sums[m % 4] + r
        total = splat(lane_sum((sums[0] + sums[1]) + (sums[2] + sums[3])))
        placed = jnp.where(lane == 3 * sub + c, total, placed)
    own = jnp.sum(placed, axis=0, keepdims=True) * (1.0 / math.sqrt(CELLS))
    own = jnp.broadcast_to(own, (BLK, LANES))
    columns = BLK * 3
    wide = -(-members * columns // LANES)
    rows = [jnp.zeros((BLK, LANES), F32) for _ in range(wide)]
    for n in range(members):
        for v in range(3):
            have = jnp.where(lane < columns, roll(coarse[n * BLK : (n + 1) * BLK, :], -v * columns), 0.0)
            part = splat(lane_sum(have * own))
            place = n * columns + v * BLK
            for t in range(place // LANES, (place + BLK - 1) // LANES + 1):
                rows[t] = jnp.where(lane + t * LANES == place + sub, part, rows[t])
    out = jnp.zeros((BLK, LANES), F32)
    for t in range(wide):
        out = jnp.where(sub == t, jnp.sum(rows[t], axis=0, keepdims=True), out)
    for n in range(devices):
        payload[n * BLK : (n + 1) * BLK, :] = out


def lift_kernel(
    members, groups, cap, arrived, residual, eff, inverse, gk, gj, gi, tables, chosen,
    new_residual, step, lift, payload, first, second, staged, sems,
):
    lane, sub = lane_id(), sub_id()
    k = lane & 15
    table = Table(tables)
    wide = -(-members * BLK * 3 // LANES)
    group, member = lax.axis_index("grp"), lax.axis_index("mem")
    base = [jnp.maximum(group - 1, 0), group, jnp.minimum(group + 1, groups - 1)]
    known = []
    for n in range(3):
        total = jnp.zeros((BLK, LANES), F32)
        for p in range(members):
            at = pl.multiple_of((base[n] * members + p) * BLK, BLK)
            total = total + arrived[pl.ds(at, BLK), :]
        if n != 1:
            total = jnp.where(table(Table.LOWER if n == 0 else Table.UPPER) == 1, total, 0.0)
        known.append([jnp.broadcast_to(total[t : t + 1, :], (BLK, LANES)) for t in range(wide)])

    def look_up(values, block):
        found = []
        for c in range(3):
            total = jnp.zeros((BLK, LANES), F32)
            for t in range(wide):
                total = total + jnp.where(lane + t * LANES == 3 * block + c, values[t], 0.0)
            found.append(splat(lane_sum(total)))
        return found

    own = look_up(known[1], member * BLK + sub)
    side = [look_up(known[1], table(Table.OWNER + d) * BLK + table(Table.BLOCK + d)) for d in range(4)]
    below = look_up(known[0], member * BLK + table(Table.PLANE))
    above = look_up(known[2], member * BLK + table(Table.PLANE + 1))
    for c in range(3):
        values = []
        lift[c * BLK : (c + 1) * BLK, :] = own[c]
        drop_k = own[c] - jnp.where(k == 0, side[0][c], side[1][c])
        drop_j = [own[c] - side[2][c], own[c] - side[3][c]]
        drop_i = [own[c] - below[c], own[c] - above[c]]
        for m in range(TILES):
            i, h = divmod(m, 2)
            applied = (MASS_TERM * eff[:, tile(m)]) * own[c]
            applied = applied + gk[:, tile(m)] * drop_k + gj[:, tile(m)] * drop_j[h]
            if i == 0:
                applied = applied + gi[:, tile(h)] * drop_i[0]
            if i == EDGE - 1:
                applied = applied + gi[:, tile(2 + h)] * drop_i[1]
            r = residual[c, :, tile(m)] - applied
            new_residual[c, :, tile(m)] = r
            s = r * (inverse[:, tile(m)] * (1.0 / THETA))
            step[c, :, tile(m)] = s
            values.append(s)
        emit_channel(c, values, chosen, table, payload, first, second, staged, sems, lane, members, cap)
    emit_wait(payload, staged, sems, cap)


def local(
    forcing, viscosity, refinement, face_owner, face_block, plane_block, hanging, coarse_solver
):
    groups, members = lax.axis_size("grp"), lax.axis_size("mem")
    cap = 8 * BLK // members
    devices = groups * members
    field = jax.ShapeDtypeStruct(forcing.shape, F32)
    scalar_field = jax.ShapeDtypeStruct(viscosity.shape, F32)

    def array(*shape):
        return jax.ShapeDtypeStruct(shape, F32)

    def ints(*shape):
        return jax.ShapeDtypeStruct(shape, jnp.int32)

    def scratch(*shape):
        return pltpu.VMEM(shape, F32)

    def call(body, in_specs, out_shape, out_specs, scratch_shapes, name):
        return pl.pallas_call(
            body,
            out_shape=out_shape,
            in_specs=in_specs,
            out_specs=out_specs,
            scratch_shapes=scratch_shapes,
            compiler_params=PARAMS,
            cost_estimate=pl.CostEstimate(flops=2_000_000, bytes_accessed=2_000_000, transcendentals=0),
            name=name,
        )

    first_route = [(q * members + m, (q ^ 1) * members + m) for q in range(groups) for m in range(members)]
    second_route = []
    for q in range(groups):
        for m in range(members):
            if q == 0 or q == groups - 1:
                second_route.append((q * members + m, q * members + (m ^ 1)))
            else:
                second_route.append((q * members + m, (q + 1 if q % 2 else q - 1) * members + m))

    def exchange(payload, first, second):
        near = lax.all_to_all(payload, "mem", split_axis=0, concat_axis=0, tiled=True)
        first = lax.ppermute(first, ("grp", "mem"), first_route)
        second = lax.ppermute(second, ("grp", "mem"), second_route)
        return near, first, second

    per = 9 * BLK
    solver_rows = jnp.pad(coarse_solver[0], ((0, 0), (0, -coarse_solver.shape[2] % LANES)))
    eff, payload, first, second, tables = call(
        functools.partial(prepare_kernel, members, groups, cap),
        [HBM] * 6 + [VMEM],
        [scalar_field, array(members, per, LANES), array(16, LANES), array(16, LANES), ints(Table.SIZE * BLK, LANES)],
        [VMEM, HBM, VMEM, VMEM, VMEM],
        [
            scratch(BLK, CELLS), pltpu.VMEM((1, BLK), jnp.int32), pltpu.VMEM((1, 4 * BLK), jnp.int32),
            pltpu.VMEM((4, BLK), jnp.int32), pltpu.VMEM((2, BLK), jnp.int32), pltpu.VMEM((BLK, 6), jnp.int32),
            scratch(members, per, LANES), pltpu.SemaphoreType.DMA((6,)), pltpu.SemaphoreType.DMA,
        ],
        "prepare",
    )(viscosity, refinement.reshape(1, BLK), face_owner.T, face_block.T, plane_block.T, hanging, solver_rows)
    arrived, from_first, from_second = exchange(payload, first, second)

    payload_out = [array(members, 6 * cap, LANES), array(48, LANES), array(48, LANES)]
    payload_specs = [HBM, VMEM, VMEM]
    ghost_scratch = [scratch(3, 6 * 48, LANES)]
    emit_scratch = [scratch(members, 6 * cap, LANES), pltpu.SemaphoreType.DMA((3,))]

    step, payload, first, second, wi, gk, gj, gi, diagonal, inverse, chosen, coarse = call(
        functools.partial(weights_kernel, members, cap),
        [VMEM] * 6,
        [field] + payload_out
        + [array(5, BLK, CELLS), scalar_field, scalar_field, array(BLK, 4 * LANES), scalar_field, scalar_field]
        + [ints(members * BLK, LANES), array(members * BLK, LANES)],
        [VMEM] + payload_specs + [VMEM] * 8,
        [scratch(3, 6 * 16, LANES)] + emit_scratch,
        "weights",
    )(arrived, from_first, from_second, eff, forcing, tables)

    def inside(residual, step, x=None, lift=None):
        operands = [residual, step, wi, diagonal] + [a for a in (x, lift) if a is not None]
        out = [field] + ([field] if x is not None else [])
        result = call(
            functools.partial(inside_kernel, x is not None, lift is not None),
            [VMEM] * len(operands), out, [VMEM] * len(out), [], "inside",
        )(*operands)
        return result if x is not None else (result[0], step)

    def outside(arrived, from_first, from_second, residual, step, old, new):
        return call(
            functools.partial(outside_kernel, members, cap, old, new),
            [VMEM] * 11,
            [field, field] + payload_out,
            [VMEM, VMEM] + payload_specs,
            ghost_scratch + emit_scratch,
            "outside",
        )(arrived, from_first, from_second, residual, step, inverse, gk, gj, gi, tables, chosen)

    rho = 1.0 / SIGMA
    factors = []
    for _ in range(DEG - 1):
        rho_next = 1.0 / (2.0 * SIGMA - rho)
        factors.append((rho_next * rho, 2.0 * rho_next / DELTA))
        rho = rho_next

    def steps(residual, step, payload, first, second, x, lift):
        for old, new in factors:
            arrived, from_first, from_second = exchange(payload, first, second)
            residual, x = inside(residual, step, x, lift)
            lift = None
            residual, step, payload, first, second = outside(
                arrived, from_first, from_second, residual, step, old, new
            )
        arrived, from_first, from_second = exchange(payload, first, second)
        residual, x = inside(residual, step, x, lift)
        return arrived, from_first, from_second, residual, x

    arrived, from_first, from_second, residual, x = steps(forcing, step, payload, first, second, None, None)
    residual, payload = call(
        functools.partial(coarse_kernel, members, devices, cap),
        [VMEM] * 9,
        [field, array(devices * BLK, LANES)],
        [VMEM] * 2,
        ghost_scratch,
        "coarse",
    )(arrived, from_first, from_second, residual, gk, gj, gi, tables, coarse)
    sums = payload.reshape(devices, BLK, LANES)
    sums = lax.all_to_all(sums, ("grp", "mem"), split_axis=0, concat_axis=0, tiled=True).reshape(-1, LANES)
    residual, step, lift, payload, first, second = call(
        functools.partial(lift_kernel, members, groups, cap),
        [VMEM] * 9,
        [field, field, array(3 * BLK, LANES)] + payload_out,
        [VMEM] * 3 + payload_specs,
        emit_scratch,
        "lift",
    )(sums, residual, eff, inverse, gk, gj, gi, tables, chosen)
    arrived, from_first, from_second, residual, x = steps(residual, step, payload, first, second, x, lift)
    residual = call(
        functools.partial(last_kernel, members, cap),
        [VMEM] * 8,
        [field],
        [HBM],
        ghost_scratch + [scratch(3, BLK, CELLS), pltpu.SemaphoreType.DMA((3,))],
        "last",
    )(arrived, from_first, from_second, residual, gk, gj, gi, tables)[0]
    return x, residual


def solution(mesh):
    in_specs = (
        P(None, ("grp", "mem"), None),
        P(("grp", "mem"), None),
        P(("grp", "mem")),
        P(("grp", "mem"), None),
        P(("grp", "mem"), None),
        P(("grp", "mem"), None),
        P(("grp", "mem"), None),
        P("grp", "mem", None),
    )
    out_specs = (P(None, ("grp", "mem"), None), P(None, ("grp", "mem"), None))
    return jax.shard_map(local, mesh=mesh, in_specs=in_specs, out_specs=out_specs, check_vma=False)
```

```python
import functools
import math

import jax
import jax.numpy as jnp
from jax import lax
from jax.experimental import pallas as pl
from jax.experimental.pallas import tpu as pltpu
from jax.sharding import PartitionSpec as P

EDGE = 16
DEG = 3
CELLS = 4096
MASS_TERM = 1.0
LOWER_BOUND = 0.25
UPPER_BOUND = 2.0
THETA = 0.5 * (UPPER_BOUND + LOWER_BOUND)
DELTA = 0.5 * (UPPER_BOUND - LOWER_BOUND)
SIGMA = THETA / DELTA

LANES = 128
BLK = 8
TILES = CELLS // LANES
BATCHES = [range(m, m + 8) for m in range(0, TILES, 8)]
F32 = jnp.float32
R, S = 0, 3
VMEM = pl.BlockSpec(memory_space=pltpu.VMEM)
ANY = pl.BlockSpec(memory_space=pl.ANY)
HBM = pl.BlockSpec(memory_space=pltpu.HBM)
PARAMS = pltpu.CompilerParams(vmem_limit_bytes=8 * 1024 * 1024)


def lane_id():
    return lax.broadcasted_iota(jnp.int32, (BLK, LANES), 1)


def sub_id():
    return lax.broadcasted_iota(jnp.int32, (BLK, LANES), 0)


def roll(v, shift):
    shift = shift % LANES
    return v if shift == 0 else pltpu.roll(v, shift, 1)


def tile(m):
    return slice(m * LANES, (m + 1) * LANES)


def pack_faces(values, lane):
    k, g = lane & 15, lane >> 4
    faces = [[], [], [], []]
    for p in range(2):
        low = high = None
        for t in range(16):
            moved = roll(values[16 * p + t], t)
            low = moved if t == 0 else jnp.where(k == t, moved, low)
            high = moved if t == 0 else jnp.where(k == (15 + t) % 16, moved, high)
        faces[0].append(low)
        faces[1].append(roll(high, -15))
        low = high = None
        for t in range(8):
            i = 8 * p + t
            first = roll(values[2 * i], 16 * t)
            last = roll(values[2 * i + 1], 16 * t + 16)
            low = first if t == 0 else jnp.where(g == t, first, low)
            high = last if t == 0 else jnp.where(g == t, last, high)
        faces[2].append(low)
        faces[3].append(high)
    return faces


def unpack_k(low, high, lane, m):
    t = m % 16
    return jnp.where((lane & 15) == 0, roll(low[m // 16], -t), roll(high[m // 16], 15 - t))


def unpack_j(low, high, m):
    i = m // 2
    if m % 2 == 0:
        return roll(low[i // 8], -16 * (i % 8))
    return roll(high[i // 8], 112 - 16 * (i % 8))


def pick(values, index):
    return jnp.take_along_axis(values, index, axis=0, mode="promise_in_bounds")


def lane_sum(v):
    return jnp.sum(v, axis=1, keepdims=True)


def splat(column):
    return jnp.broadcast_to(column, (BLK, LANES))


class Table:
    OWNER, SLOT, BLOCK, PLANE, EVEN, LOWER, UPPER, HANG, APART = 0, 4, 8, 12, 14, 15, 16, 17, 23
    SIZE = 27

    def __init__(self, ref):
        self.ref = ref

    def __call__(self, n):
        return self.ref[n * BLK : (n + 1) * BLK, :]


def gather_ghosts(near_tile, members, who, first, second, table, ghosts, lane, rows, amend=None):
    even = table(Table.EVEN) == 1
    for d in range(6):
        for n in range(rows):
            if d < 4:
                v = None
                for m in range(members):
                    source, index = near_tile(m, d, n)
                    found = pick(source, index)
                    v = found if m == 0 else jnp.where(table(who + d) == m, found, v)
                if amend:
                    v = amend(d, n, v)
            else:
                a, b = first[n * BLK : (n + 1) * BLK, :], second[n * BLK : (n + 1) * BLK, :]
                v = jnp.where(even, b, a) if d == 4 else jnp.where(even, a, b)
                if amend:
                    v = amend(d, n, v)
                inside = table(Table.LOWER if d == 4 else Table.UPPER) == 1
                v = jnp.where(inside, pick(v, table(Table.PLANE + d - 4)), 0.0)
            at = (d * rows + n) * BLK
            ghosts[0, at : at + BLK, :] = v
    for stage in range(2):
        for d in range(6):
            bit = 16 if stage else (2 if d < 2 else 1)
            low = (lane & bit) == 0
            for n in range(rows):
                at = (d * rows + n) * BLK
                v = ghosts[stage, at : at + BLK, :]
                ghosts[stage + 1, at : at + BLK, :] = v + jnp.where(low, roll(v, -bit), roll(v, bit))
    result = []
    for d in range(6):
        hang = table(Table.HANG + d) == 1
        tiles = []
        for n in range(rows):
            at = (d * rows + n) * BLK
            tiles.append(jnp.where(hang, ghosts[2, at : at + BLK, :] * 0.25, ghosts[0, at : at + BLK, :]))
        result.append(tiles)
    return result


def sent_by(near, apart, rows):
    pair, bit = divmod(apart, 2)
    return near[bit][0, rows, :] if pair == 0 else near[1 + pair][bit, rows, :]


def step_ghosts(members, cap, near, first, second, table, ghosts, lane, amend=None):
    def near_tile(m, d, n):
        start = n * cap
        at = start // BLK * BLK
        return sent_by(near, m, slice(at, at + BLK)), table(Table.SLOT + d) + (start - at)

    return gather_ghosts(near_tile, members, Table.APART, first, second, table, ghosts, lane, 6, amend)


def look_up(rows, block, lane):
    found = []
    for c in range(3):
        total = jnp.zeros((BLK, LANES), F32)
        for t, values in enumerate(rows):
            total = total + jnp.where(lane + t * LANES == 3 * block + c, values, 0.0)
        found.append(splat(lane_sum(total)))
    return found


def rows_of(v, wide):
    return [jnp.broadcast_to(v[t : t + 1, :], (BLK, LANES)) for t in range(wide)]


def from_side(first, second, table, n, upper):
    a, b = first[n * BLK : (n + 1) * BLK, :], second[n * BLK : (n + 1) * BLK, :]
    even = table(Table.EVEN) == 1
    v = jnp.where(even, a, b) if upper else jnp.where(even, b, a)
    return jnp.where(table(Table.UPPER if upper else Table.LOWER) == 1, v, 0.0)


def emit_planes(low, high, even, at, first, second):
    for n in range(len(low)):
        span = slice((at + n) * BLK, (at + n + 1) * BLK)
        first[span, :] = jnp.where(even, high[n], low[n])
        second[span, :] = jnp.where(even, low[n], high[n])


def emit_channel(c, values, chosen, table, mine, other, first, second, lane, members, cap):
    packed = pack_faces(values, lane)
    emit_planes(values[:2], values[-2:], table(Table.EVEN) == 1, 2 * c, first, second)
    sub = sub_id()
    for m in range(members):
        want = chosen[m * BLK : (m + 1) * BLK, :]
        face, block = want >> 3, want & 7
        for u in range(2 * cap // BLK):
            out = None
            for p in range(2):
                if not u * BLK <= p * cap < (u + 1) * BLK:
                    continue
                v = None
                for f in range(4):
                    found = pick(packed[f][p], block)
                    v = found if f == 0 else jnp.where(face == f, found, v)
                out = v if out is None else jnp.where(sub < p * cap - u * BLK, out, v)
            at = c * 2 * cap + u * BLK
            (mine, other)[m % 2][m // 2, at : at + BLK, :] = out


def prepare_kernel(
    members, groups, cap, eff, owner_hbm, block_hbm, plane_hbm, hanging_hbm, coarse_rows,
    payload, first, second, tables,
    face_owner, face_block, plane_block, hanging, staged, sems, out_sem,
):
    copies = [
        pltpu.make_async_copy(source, target, sems.at[n])
        for n, (source, target) in enumerate(
            [
                (owner_hbm, face_owner), (block_hbm, face_block), (plane_hbm, plane_block), (hanging_hbm, hanging),
            ]
        )
    ]
    for copy in copies:
        copy.start()
    lane, sub = lane_id(), sub_id()
    group, member = lax.axis_index("grp"), lax.axis_index("mem")
    even = group % 2 == 0
    for copy in copies:
        copy.wait()

    def iotas(width):
        return (
            lax.broadcasted_iota(jnp.int32, (BLK, width), 1), lax.broadcasted_iota(jnp.int32, (BLK, width), 0)
        )

    lane8, sub8 = iotas(BLK)
    lane32, sub32 = iotas(4 * BLK)
    lane64, sub64 = iotas(members * cap)

    def column(row):
        wide = jnp.broadcast_to(row.astype(F32), (BLK, BLK))
        return lane_sum(jnp.where(lane8 == sub8, wide, 0.0))

    def put(n, value):
        tables[n * BLK : (n + 1) * BLK, :] = splat(value).astype(jnp.int32)

    values = [eff[:, tile(m)] for m in range(TILES)]
    packed = pack_faces(values, lane)
    emit_planes(values[:2], values[-2:], even, 0, first, second)

    row = jnp.broadcast_to(face_owner[...].astype(F32), (BLK, 4 * BLK))
    wanted = jnp.zeros((BLK, members * cap), F32)
    for d in range(4):
        place = 4 * sub32 + d
        owner = lane_sum(jnp.where(lane32 == place, row, 0.0))
        slot = lane_sum(jnp.where((lane32 < place) & (row == owner), 1.0, 0.0))
        block = column(face_block[d : d + 1, :])
        put(Table.OWNER + d, owner)
        at = (Table.APART + d) * BLK
        tables[at : at + BLK, :] = splat(owner).astype(jnp.int32) ^ jnp.full((BLK, LANES), member, jnp.int32)
        put(Table.SLOT + d, slot)
        put(Table.BLOCK + d, block)
        target = jnp.broadcast_to(owner * cap + slot, (BLK, members * cap))
        want = jnp.broadcast_to(block + (d ^ 1) * BLK, (BLK, members * cap))
        wanted = wanted + jnp.where(lane64.astype(F32) == target, want, 0.0)
    wanted = jnp.broadcast_to(jnp.sum(wanted, axis=0, keepdims=True), (BLK, members * cap))
    for d in range(2):
        put(Table.PLANE + d, column(plane_block[d : d + 1, :]))
    for n, flag in ((Table.EVEN, even), (Table.LOWER, group > 0), (Table.UPPER, group < groups - 1)):
        tables[n * BLK : (n + 1) * BLK, :] = jnp.full((BLK, LANES), jnp.where(flag, 1, 0), jnp.int32)
    for d in range(6):
        put(Table.HANG + d, hanging[:, d : d + 1])

    def coarse_tile(rows, at):
        have = coarse_rows[rows, at * LANES : min((at + 1) * LANES, coarse_rows.shape[1])]
        missing = LANES - have.shape[1]
        return have if missing == 0 else jnp.concatenate([have, jnp.zeros((BLK, missing), F32)], axis=1)

    columns = BLK * 3
    for n in range(members):
        for f in range(4):
            for p in range(2):
                at = (f * 2 + p) * BLK
                staged[n, at : at + BLK, :] = packed[f][p]
        request = lane_sum(jnp.where(lane64 == n * cap + sub64 % cap, wanted, 0.0))
        last = splat(request)
        at, off = divmod(n * columns, LANES)
        for v in range(3):
            rows = slice(v * BLK, (v + 1) * BLK)
            part = roll(coarse_tile(rows, at), v * columns - off)
            if off + columns > LANES:
                more = roll(coarse_tile(rows, at + 1), v * columns - off)
                part = jnp.where(lane < v * columns + LANES - off, part, more)
            last = jnp.where((lane >= v * columns) & (lane < (v + 1) * columns), part, last)
        staged[n, 8 * BLK : 9 * BLK, :] = last
    copy = pltpu.make_async_copy(staged, payload, out_sem)
    copy.start()
    copy.wait()


def weights_kernel(
    members, cap, near, from_first, from_second, eff, forcing, tables,
    state, mine, other, first, second, wi, gk, gj, gi, diagonal, inverse, chosen, coarse, ghosts,
):
    lane = lane_id()
    k, g = lane & 15, lane >> 4
    table = Table(tables)
    for n in range(members):
        last = near[n, 8 * BLK : 9 * BLK, :]
        coarse[n * BLK : (n + 1) * BLK, :] = last
        asked = near[lax.axis_index("mem") ^ n, 8 * BLK : 9 * BLK, :]
        chosen[n * BLK : (n + 1) * BLK, :] = splat(asked[:, LANES - 1 :]).astype(jnp.int32)

    def near_tile(m, d, n):
        at = ((d ^ 1) * 2 + n) * BLK
        return near[m, at : at + BLK, :], table(Table.BLOCK + d)

    ghost = gather_ghosts(near_tile, members, Table.OWNER, from_first, from_second, table, ghosts, lane, 2)
    values = [eff[:, tile(m)] for m in range(TILES)]
    start = [[], [], []]
    for m in range(TILES):
        i, h = divmod(m, 2)
        e = values[m]
        side_k = unpack_k(ghost[0], ghost[1], lane, m)
        side_j = unpack_j(ghost[2], ghost[3], m)
        ends_j = (g == 0) if h == 0 else (g == 7)
        n0 = jnp.where(k == 0, side_k, roll(e, 1))
        n1 = jnp.where(k == 15, side_k, roll(e, -1))
        n2 = jnp.where(g == 0, side_j if h == 0 else roll(values[m - 1], 16), roll(e, 16))
        n3 = jnp.where(g == 7, side_j if h == 1 else roll(values[m + 1], -16), roll(e, -16))
        n4 = ghost[4][h] if i == 0 else values[m - 2]
        n5 = ghost[5][h] if i == EDGE - 1 else values[m + 2]
        w = [0.5 * (e + n) for n in (n0, n1, n2, n3, n4, n5)]
        diag = MASS_TERM * e
        for d in range(6):
            diag = diag + w[d]
        inv = 1.0 / diag
        diagonal[:, tile(m)] = diag
        inverse[:, tile(m)] = inv
        wi[0, :, tile(m)] = jnp.where(k == 0, 0.0, w[0])
        wi[1, :, tile(m)] = jnp.where(k == 15, 0.0, w[1])
        wi[2, :, tile(m)] = jnp.where(ends_j, 0.0, w[2]) if h == 0 else w[2]
        wi[3, :, tile(m)] = jnp.where(ends_j, 0.0, w[3]) if h == 1 else w[3]
        wi[4, :, tile(m)] = w[4]
        gk[:, tile(m)] = jnp.where(k == 0, w[0], jnp.where(k == 15, w[1], 0.0))
        gj[:, tile(m)] = jnp.where(ends_j, w[2 + h], 0.0)
        if i == 0:
            gi[:, tile(h)] = w[4]
        if i == EDGE - 1:
            gi[:, tile(2 + h)] = w[5]
        scale = inv * (1.0 / THETA)
        for c in range(3):
            f = forcing[c, :, tile(m)]
            s = f * scale
            state[R + c, :, tile(m)] = f
            state[S + c, :, tile(m)] = s
            start[c].append(s)
    for c in range(3):
        emit_channel(c, start[c], chosen, table, mine, other, first, second, lane, members, cap)


def merge_kernel(mine, got, *pairs):
    for n, pair in enumerate(pairs):
        pair[0, :, :] = mine[n + 1, :, :]
        pair[1, :, :] = got[n + 1, :, :]


def inside_kernel(first_step, has_lift, final, *refs):
    refs = list(refs)
    state, wi, diagonal = refs[:3]
    refs = refs[3:]
    x = None if first_step else refs.pop(0)
    lift, fixed = None, {}
    if has_lift:
        lift = refs.pop(0)
        fixed = lift_inside(has_lift, refs[0], refs[1], state, *refs[2:5])
        refs = refs[5:]
    out, new_x = refs[:2]
    if final:
        staged, sems = refs[2:]
    g = lane_id() >> 4
    copies = []

    def get(row, m):
        return fixed[row, m] if (row, m) in fixed else state[row, :, tile(m)]

    for c in range(3):
        up = None if not has_lift else lift[c * BLK : (c + 1) * BLK, :]
        for m in range(TILES):
            i, h = divmod(m, 2)
            s = get(S + c, m)
            n2, n3 = roll(s, 16), roll(s, -16)
            if h == 1:
                n2 = jnp.where(g == 0, roll(get(S + c, m - 1), 16), n2)
            else:
                n3 = jnp.where(g == 7, roll(get(S + c, m + 1), -16), n3)
            acc = get(R + c, m) - diagonal[:, tile(m)] * s
            acc = acc + wi[0, :, tile(m)] * roll(s, 1)
            acc = acc + wi[1, :, tile(m)] * roll(s, -1)
            acc = acc + wi[2, :, tile(m)] * n2
            acc = acc + wi[3, :, tile(m)] * n3
            if i > 0:
                acc = acc + wi[4, :, tile(m)] * get(S + c, m - 2)
            if i < EDGE - 1:
                acc = acc + wi[4, :, tile(m + 2)] * get(S + c, m + 2)
            out[R + c, :, tile(m)] = acc
            total = s if first_step else x[c, :, tile(m)] + s
            if has_lift:
                total = total + up
            if final:
                staged[c, :, tile(m)] = total
            else:
                new_x[c, :, tile(m)] = total
        if final:
            copies.append(pltpu.make_async_copy(staged.at[c], new_x.at[c], sems.at[c]))
            copies[c].start()
    for row in range(S, S + 3):
        for m in range(TILES):
            out[row, :, tile(m)] = get(row, m)
    for copy in copies:
        copy.wait()


def add_ghosts(c, m, value, ghost, gk, gj, gi, lane):
    i, h = divmod(m, 2)
    pair = slice(2 * c, 2 * c + 2)
    value = value + gk[:, tile(m)] * unpack_k(ghost[0][pair], ghost[1][pair], lane, m)
    value = value + gj[:, tile(m)] * unpack_j(ghost[2][pair], ghost[3][pair], m)
    if i == 0:
        value = value + gi[:, tile(h)] * ghost[4][2 * c + h]
    if i == EDGE - 1:
        value = value + gi[:, tile(2 + h)] * ghost[5][2 * c + h]
    return value


def outside_kernel(members, cap, old, new, has_lift, near, from_first, from_second, state, *refs):
    inverse, gk, gj, gi, tables, chosen, x = refs[:7]
    out, mine, other, first, second, same_x, ghosts = refs[-7:]
    lane = lane_id()
    table = Table(tables)
    amend = lift_outside(members, cap, near, from_first, from_second, refs[7], tables) if has_lift else None
    ghost = step_ghosts(members, cap, near, from_first, from_second, table, ghosts, lane, amend)
    for c in range(3):
        values = []
        for batch in BATCHES:
            done = []
            for m in batch:
                r = add_ghosts(c, m, state[R + c, :, tile(m)], ghost, gk, gj, gi, lane)
                done.append((m, r, old * state[S + c, :, tile(m)] + new * (r * inverse[:, tile(m)])))
            for m, r, s in done:
                out[R + c, :, tile(m)] = r
                out[S + c, :, tile(m)] = s
                values.append(s)
        emit_channel(c, values, chosen, table, mine, other, first, second, lane, members, cap)


def last_kernel(
    members, cap, near, from_first, from_second, state, gk, gj, gi, tables, new_residual, ghosts, staged, sems,
):
    lane = lane_id()
    ghost = step_ghosts(members, cap, near, from_first, from_second, Table(tables), ghosts, lane)
    copies = []
    for c in range(3):
        for m in range(TILES):
            staged[c, :, tile(m)] = add_ghosts(c, m, state[R + c, :, tile(m)], ghost, gk, gj, gi, lane)
        copies.append(pltpu.make_async_copy(staged.at[c], new_residual.at[c], sems.at[c]))
        copies[c].start()
    for copy in copies:
        copy.wait()


def coarse_kernel(
    members, cap, near, from_first, from_second, state, gk, gj, gi, tables, coarse, x,
    out_state, payload, same_x, ghosts,
):
    lane, sub = lane_id(), sub_id()
    ghost = step_ghosts(members, cap, near, from_first, from_second, Table(tables), ghosts, lane)
    placed = jnp.zeros((BLK, LANES), F32)
    for c in range(3):
        sums = [None] * 4
        for batch in BATCHES:
            done = [(m, add_ghosts(c, m, state[R + c, :, tile(m)], ghost, gk, gj, gi, lane)) for m in batch]
            for m, r in done:
                out_state[R + c, :, tile(m)] = r
                sums[m % 4] = r if sums[m % 4] is None else sums[m % 4] + r
        total = splat(lane_sum((sums[0] + sums[1]) + (sums[2] + sums[3])))
        placed = jnp.where(lane == 3 * sub + c, total, placed)
    own = jnp.sum(placed, axis=0, keepdims=True) * (1.0 / math.sqrt(CELLS))
    own = jnp.broadcast_to(own, (BLK, LANES))
    columns = BLK * 3
    wide = -(-members * columns // LANES)
    rows = [jnp.zeros((BLK, LANES), F32) for _ in range(wide)]
    for n in range(members):
        for v in range(3):
            have = jnp.where(lane < columns, roll(coarse[n * BLK : (n + 1) * BLK, :], -v * columns), 0.0)
            part = splat(lane_sum(have * own))
            place = n * columns + v * BLK
            for t in range(place // LANES, (place + BLK - 1) // LANES + 1):
                rows[t] = jnp.where(lane + t * LANES == place + sub, part, rows[t])
    out = jnp.zeros((BLK, LANES), F32)
    for t in range(wide):
        out = jnp.where(sub == t, jnp.sum(rows[t], axis=0, keepdims=True), out)
    for n in range(members):
        payload[n, :, :] = out


def lift_kernel(
    members, cap, arrived, state, eff, inverse, gk, gj, gi, tables, chosen, x,
    out, lift, unknowns, mine, other, first, second, same_x,
):
    lane, sub = lane_id(), sub_id()
    k, g = lane & 15, lane >> 4
    table = Table(tables)
    wide = -(-members * BLK * 3 // LANES)
    member = lax.axis_index("mem")
    total = arrived[0, :, :]
    for n in range(1, members):
        total = total + arrived[n, :, :]
    unknowns[...] = total
    known = rows_of(total, wide)
    own = look_up(known, member * BLK + sub, lane)
    side = [look_up(known, table(Table.OWNER + d) * BLK + table(Table.BLOCK + d), lane) for d in range(4)]
    for c in range(3):
        values = []
        lift[c * BLK : (c + 1) * BLK, :] = own[c]
        drop_k = own[c] - jnp.where(k == 0, side[0][c], side[1][c])
        drop_j = [own[c] - side[2][c], own[c] - side[3][c]]
        for batch in BATCHES:
            done = []
            for m in batch:
                i, h = divmod(m, 2)
                applied = (MASS_TERM * eff[:, tile(m)]) * own[c]
                applied = applied + gk[:, tile(m)] * drop_k + gj[:, tile(m)] * drop_j[h]
                if i == 0:
                    applied = applied + gi[:, tile(h)] * own[c]
                if i == EDGE - 1:
                    applied = applied + gi[:, tile(2 + h)] * own[c]
                r = state[R + c, :, tile(m)] - applied
                done.append((m, r, r * (inverse[:, tile(m)] * (1.0 / THETA))))
            for m, r, s in done:
                out[R + c, :, tile(m)] = r
                out[S + c, :, tile(m)] = s
                values.append(s)
        emit_channel(c, values, chosen, table, mine, other, first, second, lane, members, cap)

    ends = end_weights(inverse, gi)
    planes = [table(Table.PLANE + d).astype(F32) for d in range(2)]
    emit_planes(ends[:2] + planes[:1], ends[2:] + planes[1:], table(Table.EVEN) == 1, 6, first, second)
    for ref in (first, second):
        ref[9 * BLK : 10 * BLK, :] = total
    edges = []
    for f in range(2):
        v = jnp.zeros((BLK, LANES), F32)
        for t, end in zip((0, 1, 14, 15), ends):
            v = jnp.where(k == t, roll(end, t - 15 * f), v)
        edges.append(v)
    edges.append(jnp.where(g == 0, ends[0], jnp.where(g == 7, roll(ends[2], 112), 0.0)))
    edges.append(jnp.where(g == 0, roll(ends[1], 16), jnp.where(g == 7, ends[3], 0.0)))
    edges = [jnp.where(lane == 18, planes[0], jnp.where(lane == 19, planes[1], v)) for v in edges]
    for m in range(members):
        want = chosen[m * BLK : (m + 1) * BLK, :]
        face, block = want >> 3, want & 7
        v = None
        for f in range(4):
            found = pick(edges[f], block)
            v = found if f == 0 else jnp.where(face == f, found, v)
        (mine, other)[m % 2][m // 2, 6 * cap : 6 * cap + BLK, :] = v


def end_weights(inverse, gi):
    return [
        gi[:, tile(n)] * (inverse[:, tile(m)] * (1.0 / THETA)) for n, m in enumerate((0, 1, TILES - 2, TILES - 1))
    ]


def lift_inside(members, from_first, from_second, state, inverse, gi, tables):
    lane = lane_id()
    table = Table(tables)
    wide = -(-members * BLK * 3 // LANES)
    member = lax.axis_index("mem")
    ends = end_weights(inverse, gi)
    fixed = {}
    for upper in range(2):
        rows = rows_of(from_side(from_first, from_second, table, 9, upper == 1), wide)
        beyond = look_up(rows, member * BLK + table(Table.PLANE + upper), lane)
        for c in range(3):
            for h in range(2):
                n, m = 2 * upper + h, upper * (TILES - 2) + h
                fixed[R + c, m] = state[R + c, :, tile(m)] + gi[:, tile(n)] * beyond[c]
                fixed[S + c, m] = state[S + c, :, tile(m)] + ends[n] * beyond[c]
    return fixed


def lift_outside(members, cap, near, from_first, from_second, unknowns, tables):
    lane = lane_id()
    k, g = lane & 15, lane >> 4
    table = Table(tables)
    wide = -(-members * BLK * 3 // LANES)
    member = lax.axis_index("mem")
    below, above = [
        rows_of(from_side(from_first, from_second, table, 9, upper), wide) for upper in (False, True)
    ]
    known = rows_of(unknowns[...], wide)
    parts = []
    for d in range(4):
        v = None
        for m in range(members):
            found = pick(sent_by(near, m, slice(6 * cap, 6 * cap + BLK)), table(Table.SLOT + d))
            v = found if m == 0 else jnp.where(table(Table.APART + d) == m, found, v)
        base = table(Table.OWNER + d) * BLK
        low = look_up(below, base + splat(v[:, 18:19]).astype(jnp.int32), lane)
        high = look_up(above, base + splat(v[:, 19:20]).astype(jnp.int32), lane)
        at_low, at_high = (k < 2, k > 13) if d < 2 else (g == 0, g == 7)
        weights = [jnp.where(at_low, v, 0.0), jnp.where(at_high, v, 0.0)]
        parts.append([weights[n % 2] * (low, high)[n % 2][n // 2] for n in range(6)])
    for upper in (False, True):
        index = from_side(from_first, from_second, table, 8, upper).astype(jnp.int32)
        own = look_up(known, member * BLK + index, lane)
        weights = [from_side(from_first, from_second, table, 6 + p, upper) for p in range(2)]
        parts.append([weights[n % 2] * own[n // 2] for n in range(6)])
    return lambda d, n, v: v + parts[d][n]


def local(
    forcing, viscosity, refinement, face_owner, face_block, plane_block, hanging, coarse_solver
):
    groups, members = lax.axis_size("grp"), lax.axis_size("mem")
    cap = 8 * BLK // members
    field = jax.ShapeDtypeStruct(forcing.shape, F32)
    scalar_field = jax.ShapeDtypeStruct(viscosity.shape, F32)
    states = jax.ShapeDtypeStruct((6, BLK, CELLS), F32)

    def array(*shape):
        return jax.ShapeDtypeStruct(shape, F32)

    def ints(*shape):
        return jax.ShapeDtypeStruct(shape, jnp.int32)

    def scratch(*shape):
        return pltpu.VMEM(shape, F32)

    def call(body, in_specs, out_shape, out_specs, scratch_shapes, name, aliases=None, moved=2_000_000):
        return pl.pallas_call(
            body,
            out_shape=out_shape,
            in_specs=in_specs,
            out_specs=out_specs,
            scratch_shapes=scratch_shapes,
            compiler_params=PARAMS,
            input_output_aliases=aliases or {},
            cost_estimate=pl.CostEstimate(flops=2_000_000, bytes_accessed=moved, transcendentals=0),
            name=name,
        )

    first_route = [(q * members + m, (q ^ 1) * members + m) for q in range(groups) for m in range(members)]
    second_route = []
    for q in range(groups):
        for m in range(members):
            if q == 0 or q == groups - 1:
                second_route.append((q * members + m, q * members + (m ^ 1)))
            else:
                second_route.append((q * members + m, (q + 1 if q % 2 else q - 1) * members + m))

    def exchange(payload, first, second):
        near = lax.all_to_all(payload, "mem", split_axis=0, concat_axis=0, tiled=True)
        first = lax.ppermute(first, ("grp", "mem"), first_route)
        second = lax.ppermute(second, ("grp", "mem"), second_route)
        return near, first, second

    def swap(a, bits):
        return lax.ppermute(a, "mem", [(m, m ^ bits) for m in range(members)])

    def spread(mine, other, first, second):
        first = lax.ppermute(first, ("grp", "mem"), first_route)
        second = lax.ppermute(second, ("grp", "mem"), second_route)
        got = swap(other, 1)
        pairs = members // 2 - 1
        sent = call(
            merge_kernel, [VMEM] * 2, [array(2, *mine.shape[1:])] * pairs, [VMEM] * pairs, [], "merge", moved=200_000
        )(mine, got)
        return [mine, got] + [swap(a, 2 * n + 2) for n, a in enumerate(sent)], first, second

    per = 9 * BLK
    eff = viscosity * jnp.exp2(-refinement.astype(F32))[:, None]
    payload, first, second, tables = call(
        functools.partial(prepare_kernel, members, groups, cap),
        [VMEM] + [HBM] * 4 + [VMEM],
        [array(members, per, LANES), array(16, LANES), array(16, LANES), ints(Table.SIZE * BLK, LANES)],
        [HBM, VMEM, VMEM, VMEM],
        [
            pltpu.VMEM((1, 4 * BLK), jnp.int32), pltpu.VMEM((4, BLK), jnp.int32), pltpu.VMEM((2, BLK), jnp.int32),
            pltpu.VMEM((BLK, 6), jnp.int32), scratch(members, per, LANES),
            pltpu.SemaphoreType.DMA((4,)), pltpu.SemaphoreType.DMA,
        ],
        "prepare",
        moved=0,
    )(eff, face_owner.T, face_block.T, plane_block.T, hanging, coarse_solver[0])
    arrived, from_first, from_second = exchange(payload, first, second)

    half = array(members // 2, 6 * cap, LANES)
    sent_out = [half, half, array(48, LANES), array(48, LANES)]
    near_refs = members // 2 + 1
    ghost_scratch = [scratch(3, 6 * 48, LANES)]

    def gathered(body, *fixed):
        return lambda *refs: body(*fixed, refs[:near_refs], *refs[near_refs:])

    state, mine, other, first, second, wi, gk, gj, gi, diagonal, inverse, chosen, coarse = call(
        functools.partial(weights_kernel, members, cap),
        [VMEM] * 6,
        [states] + sent_out
        + [array(5, BLK, CELLS), scalar_field, scalar_field, array(BLK, 4 * LANES), scalar_field, scalar_field]
        + [ints(members * BLK, LANES), array(members * BLK, LANES)],
        [VMEM] * 13,
        [scratch(3, 6 * 16, LANES)],
        "weights",
    )(arrived, from_first, from_second, eff, forcing, tables)

    field_scratch = [scratch(3, BLK, CELLS), pltpu.SemaphoreType.DMA((3,))]

    def inside(state, x=None, lift=(), final=False):
        operands = [state, wi, diagonal] + ([] if x is None else [x]) + list(lift)
        return call(
            functools.partial(inside_kernel, x is None, members if lift else 0, final),
            [VMEM] * len(operands),
            [states, field],
            [VMEM, HBM if final else VMEM],
            field_scratch * final,
            "inside",
            {0: 0} if x is None or final else {0: 0, 3: 1},
        )(*operands)

    def outside(near, from_first, from_second, state, x, old, new, unknowns=None):
        more = [] if unknowns is None else [unknowns]
        return call(
            gathered(outside_kernel, members, cap, old, new, unknowns is not None),
            [VMEM] * (near_refs + 9) + [ANY] + [VMEM] * len(more),
            [states] + sent_out + [field],
            [VMEM] * 5 + [ANY],
            ghost_scratch,
            "outside",
            {near_refs + 2: 0, near_refs + 9: 5},
        )(*near, from_first, from_second, state, inverse, gk, gj, gi, tables, chosen, x, *more)

    rho = 1.0 / SIGMA
    factors = []
    for _ in range(DEG - 1):
        rho_next = 1.0 / (2.0 * SIGMA - rho)
        factors.append((rho_next * rho, 2.0 * rho_next / DELTA))
        rho = rho_next

    def steps(state, sent, x, lift=None, unknowns=None):
        for n, (old, new) in enumerate(factors):
            near, from_first, from_second = spread(*sent)
            more = (lift, from_first, from_second, inverse, gi, tables) if n == 0 and lift is not None else ()
            state, x = inside(state, x, more)
            state, *sent, x = outside(
                near, from_first, from_second, state, x, old, new, unknowns if n == 0 else None
            )
        return state, x, spread(*sent)

    state, x, (near, from_first, from_second) = steps(state, (mine, other, first, second), None)
    state, x = inside(state, x)
    state, payload, x = call(
        gathered(coarse_kernel, members, cap),
        [VMEM] * (near_refs + 8) + [ANY],
        [states, array(members, BLK, LANES), field],
        [VMEM, VMEM, ANY],
        ghost_scratch,
        "coarse",
        {near_refs + 2: 0, near_refs + 8: 2},
    )(*near, from_first, from_second, state, gk, gj, gi, tables, coarse, x)
    sums = lax.all_to_all(payload, "mem", split_axis=0, concat_axis=0, tiled=True)
    half = array(members // 2, 6 * cap + BLK, LANES)
    state, lift, unknowns, *sent, x = call(
        functools.partial(lift_kernel, members, cap),
        [VMEM] * 9 + [ANY],
        [states, array(3 * BLK, LANES), array(BLK, LANES), half, half, array(80, LANES), array(80, LANES), field],
        [VMEM] * 7 + [ANY],
        [],
        "lift",
        {1: 0, 9: 7},
    )(sums, state, eff, inverse, gk, gj, gi, tables, chosen, x)
    state, x, (near, from_first, from_second) = steps(state, sent, x, lift, unknowns)
    state, velocity = inside(state, x, final=True)
    residual = call(
        gathered(last_kernel, members, cap),
        [VMEM] * (near_refs + 7),
        [field],
        [HBM],
        ghost_scratch + field_scratch,
        "last",
    )(*near, from_first, from_second, state, gk, gj, gi, tables)[0]
    return velocity, residual


def solution(mesh):
    in_specs = (
        P(None, ("grp", "mem"), None),
        P(("grp", "mem"), None),
        P(("grp", "mem")),
        P(("grp", "mem"), None),
        P(("grp", "mem"), None),
        P(("grp", "mem"), None),
        P(("grp", "mem"), None),
        P("grp", "mem", None),
    )
    out_specs = (P(None, ("grp", "mem"), None), P(None, ("grp", "mem"), None))
    return jax.shard_map(local, mesh=mesh, in_specs=in_specs, out_specs=out_specs, check_vma=False)
```

```python
import functools
import math

import jax
import jax.numpy as jnp
from jax import lax
from jax.experimental import pallas as pl
from jax.experimental.pallas import tpu as pltpu
from jax.sharding import PartitionSpec as P

EDGE = 16
DEG = 3
CELLS = 4096
MASS_TERM = 1.0
LOWER_BOUND = 0.25
UPPER_BOUND = 2.0
THETA = 0.5 * (UPPER_BOUND + LOWER_BOUND)
DELTA = 0.5 * (UPPER_BOUND - LOWER_BOUND)
SIGMA = THETA / DELTA

LANES = 128
BLK = 8
TILES = CELLS // LANES
BATCHES = [range(m, m + 8) for m in range(0, TILES, 8)]
F32 = jnp.float32
R, S = 0, 3
VMEM = pl.BlockSpec(memory_space=pltpu.VMEM)
ANY = pl.BlockSpec(memory_space=pl.ANY)
HBM = pl.BlockSpec(memory_space=pltpu.HBM)
PARAMS = pltpu.CompilerParams(vmem_limit_bytes=8 * 1024 * 1024)


def lane_id():
    return lax.broadcasted_iota(jnp.int32, (BLK, LANES), 1)


def sub_id():
    return lax.broadcasted_iota(jnp.int32, (BLK, LANES), 0)


def roll(v, shift):
    shift = shift % LANES
    return v if shift == 0 else pltpu.roll(v, shift, 1)


def tile(m):
    return slice(m * LANES, (m + 1) * LANES)


def pack_faces(values, lane):
    k, g = lane & 15, lane >> 4
    faces = [[], [], [], []]
    for p in range(2):
        low = high = None
        for t in range(16):
            moved = roll(values[16 * p + t], t)
            low = moved if t == 0 else jnp.where(k == t, moved, low)
            high = moved if t == 0 else jnp.where(k == (15 + t) % 16, moved, high)
        faces[0].append(low)
        faces[1].append(roll(high, -15))
        low = high = None
        for t in range(8):
            i = 8 * p + t
            first = roll(values[2 * i], 16 * t)
            last = roll(values[2 * i + 1], 16 * t + 16)
            low = first if t == 0 else jnp.where(g == t, first, low)
            high = last if t == 0 else jnp.where(g == t, last, high)
        faces[2].append(low)
        faces[3].append(high)
    return faces


def unpack_k(low, high, lane, m):
    t = m % 16
    return jnp.where((lane & 15) == 0, roll(low[m // 16], -t), roll(high[m // 16], 15 - t))


def unpack_j(low, high, m):
    i = m // 2
    if m % 2 == 0:
        return roll(low[i // 8], -16 * (i % 8))
    return roll(high[i // 8], 112 - 16 * (i % 8))


def pick(values, index):
    return jnp.take_along_axis(values, index, axis=0, mode="promise_in_bounds")


def lane_sum(v):
    return jnp.sum(v, axis=1, keepdims=True)


def splat(column):
    return jnp.broadcast_to(column, (BLK, LANES))


class Table:
    OWNER, SLOT, BLOCK, PLANE, EVEN, LOWER, UPPER, HANG, APART = 0, 4, 8, 12, 14, 15, 16, 17, 23
    SIZE = 27

    def __init__(self, ref):
        self.ref = ref

    def __call__(self, n):
        return self.ref[n * BLK : (n + 1) * BLK, :]


def gather_ghosts(near_tile, members, who, first, second, table, ghosts, lane, rows, amend=None):
    even = table(Table.EVEN) == 1
    for d in range(6):
        for n in range(rows):
            if d < 4:
                v = None
                for m in range(members):
                    source, index = near_tile(m, d, n)
                    found = pick(source, index)
                    v = found if m == 0 else jnp.where(table(who + d) == m, found, v)
                if amend:
                    v = amend(d, n, v)
            else:
                a, b = first[n * BLK : (n + 1) * BLK, :], second[n * BLK : (n + 1) * BLK, :]
                v = jnp.where(even, b, a) if d == 4 else jnp.where(even, a, b)
                if amend:
                    v = amend(d, n, v)
                inside = table(Table.LOWER if d == 4 else Table.UPPER) == 1
                v = jnp.where(inside, pick(v, table(Table.PLANE + d - 4)), 0.0)
            at = (d * rows + n) * BLK
            ghosts[0, at : at + BLK, :] = v
    for stage in range(2):
        for d in range(6):
            bit = 16 if stage else (2 if d < 2 else 1)
            low = (lane & bit) == 0
            for n in range(rows):
                at = (d * rows + n) * BLK
                v = ghosts[stage, at : at + BLK, :]
                ghosts[stage + 1, at : at + BLK, :] = v + jnp.where(low, roll(v, -bit), roll(v, bit))
    result = []
    for d in range(6):
        hang = table(Table.HANG + d) == 1
        tiles = []
        for n in range(rows):
            at = (d * rows + n) * BLK
            tiles.append(jnp.where(hang, ghosts[2, at : at + BLK, :] * 0.25, ghosts[0, at : at + BLK, :]))
        result.append(tiles)
    return result


def sent_by(near, apart, rows):
    pair, bit = divmod(apart, 2)
    return near[bit][0, rows, :] if pair == 0 else near[1 + pair][bit, rows, :]


def step_ghosts(members, cap, near, first, second, table, ghosts, lane, amend=None):
    def near_tile(m, d, n):
        start = n * cap
        at = start // BLK * BLK
        return sent_by(near, m, slice(at, at + BLK)), table(Table.SLOT + d) + (start - at)

    return gather_ghosts(near_tile, members, Table.APART, first, second, table, ghosts, lane, 6, amend)


def look_up(rows, block, lane):
    found = []
    for c in range(3):
        total = jnp.zeros((BLK, LANES), F32)
        for t, values in enumerate(rows):
            total = total + jnp.where(lane + t * LANES == 3 * block + c, values, 0.0)
        found.append(splat(lane_sum(total)))
    return found


def rows_of(v, wide):
    return [jnp.broadcast_to(v[t : t + 1, :], (BLK, LANES)) for t in range(wide)]


def from_side(first, second, table, n, upper):
    a, b = first[n * BLK : (n + 1) * BLK, :], second[n * BLK : (n + 1) * BLK, :]
    even = table(Table.EVEN) == 1
    v = jnp.where(even, a, b) if upper else jnp.where(even, b, a)
    return jnp.where(table(Table.UPPER if upper else Table.LOWER) == 1, v, 0.0)


def emit_planes(low, high, even, at, first, second):
    for n in range(len(low)):
        span = slice((at + n) * BLK, (at + n + 1) * BLK)
        first[span, :] = jnp.where(even, high[n], low[n])
        second[span, :] = jnp.where(even, low[n], high[n])


def emit_channel(c, values, chosen, table, mine, other, first, second, lane, members, cap):
    packed = pack_faces(values, lane)
    emit_planes(values[:2], values[-2:], table(Table.EVEN) == 1, 2 * c, first, second)
    sub = sub_id()
    for m in range(members):
        want = chosen[m * BLK : (m + 1) * BLK, :]
        face, block = want >> 3, want & 7
        for u in range(2 * cap // BLK):
            out = None
            for p in range(2):
                if not u * BLK <= p * cap < (u + 1) * BLK:
                    continue
                v = None
                for f in range(4):
                    found = pick(packed[f][p], block)
                    v = found if f == 0 else jnp.where(face == f, found, v)
                out = v if out is None else jnp.where(sub < p * cap - u * BLK, out, v)
            at = c * 2 * cap + u * BLK
            (mine, other)[m % 2][m // 2, at : at + BLK, :] = out


def prepare_kernel(
    members, groups, cap, eff, owner_hbm, block_hbm, plane_hbm, hanging_hbm, coarse_rows,
    mine, other, first, second, tables,
    face_owner, face_block, plane_block, hanging, special, sems,
):
    copies = [
        pltpu.make_async_copy(source, target, sems.at[n])
        for n, (source, target) in enumerate(
            [
                (owner_hbm, face_owner), (block_hbm, face_block), (plane_hbm, plane_block), (hanging_hbm, hanging),
            ]
        )
    ]
    for copy in copies:
        copy.start()
    lane, sub = lane_id(), sub_id()
    group, member = lax.axis_index("grp"), lax.axis_index("mem")
    even = group % 2 == 0
    for copy in copies:
        copy.wait()

    def iotas(width):
        return (
            lax.broadcasted_iota(jnp.int32, (BLK, width), 1), lax.broadcasted_iota(jnp.int32, (BLK, width), 0)
        )

    lane8, sub8 = iotas(BLK)
    lane32, sub32 = iotas(4 * BLK)
    lane64, sub64 = iotas(members * cap)

    def column(row):
        wide = jnp.broadcast_to(row.astype(F32), (BLK, BLK))
        return lane_sum(jnp.where(lane8 == sub8, wide, 0.0))

    def put(n, value):
        tables[n * BLK : (n + 1) * BLK, :] = splat(value).astype(jnp.int32)

    values = [eff[:, tile(m)] for m in range(TILES)]
    packed = pack_faces(values, lane)
    emit_planes(values[:2], values[-2:], even, 0, first, second)

    row = jnp.broadcast_to(face_owner[...].astype(F32), (BLK, 4 * BLK))
    wanted = jnp.zeros((BLK, members * cap), F32)
    for d in range(4):
        place = 4 * sub32 + d
        owner = lane_sum(jnp.where(lane32 == place, row, 0.0))
        slot = lane_sum(jnp.where((lane32 < place) & (row == owner), 1.0, 0.0))
        block = column(face_block[d : d + 1, :])
        put(Table.OWNER + d, owner)
        at = (Table.APART + d) * BLK
        tables[at : at + BLK, :] = splat(owner).astype(jnp.int32) ^ jnp.full((BLK, LANES), member, jnp.int32)
        put(Table.SLOT + d, slot)
        put(Table.BLOCK + d, block)
        target = jnp.broadcast_to(owner * cap + slot, (BLK, members * cap))
        want = jnp.broadcast_to(block + (d ^ 1) * BLK, (BLK, members * cap))
        wanted = wanted + jnp.where(lane64.astype(F32) == target, want, 0.0)
    wanted = jnp.broadcast_to(jnp.sum(wanted, axis=0, keepdims=True), (BLK, members * cap))
    for d in range(2):
        put(Table.PLANE + d, column(plane_block[d : d + 1, :]))
    for n, flag in ((Table.EVEN, even), (Table.LOWER, group > 0), (Table.UPPER, group < groups - 1)):
        tables[n * BLK : (n + 1) * BLK, :] = jnp.full((BLK, LANES), jnp.where(flag, 1, 0), jnp.int32)
    for d in range(6):
        put(Table.HANG + d, hanging[:, d : d + 1])

    def coarse_tile(rows, at):
        have = coarse_rows[rows, at * LANES : min((at + 1) * LANES, coarse_rows.shape[1])]
        missing = LANES - have.shape[1]
        return have if missing == 0 else jnp.concatenate([have, jnp.zeros((BLK, missing), F32)], axis=1)

    columns = BLK * 3
    for n in range(members):
        for f in range(4):
            for p in range(2):
                at = (f * 2 + p) * BLK
                (mine, other)[n % 2][n // 2, at : at + BLK, :] = packed[f][p]
        request = lane_sum(jnp.where(lane64 == n * cap + sub64 % cap, wanted, 0.0))
        last = splat(request)
        at, off = divmod(n * columns, LANES)
        for v in range(3):
            rows = slice(v * BLK, (v + 1) * BLK)
            part = roll(coarse_tile(rows, at), v * columns - off)
            if off + columns > LANES:
                more = roll(coarse_tile(rows, at + 1), v * columns - off)
                part = jnp.where(lane < v * columns + LANES - off, part, more)
            last = jnp.where((lane >= v * columns) & (lane < (v + 1) * columns), part, last)
        special[member ^ n, :, :] = last
    for n in range(members):
        (mine, other)[n % 2][n // 2, 8 * BLK : 9 * BLK, :] = special[n, :, :]


def weights_kernel(
    members, cap, near, from_first, from_second, eff, forcing, tables,
    state, mine, other, first, second, wi, gk, gj, gi, diagonal, inverse, chosen, coarse, ghosts,
):
    lane = lane_id()
    k, g = lane & 15, lane >> 4
    table = Table(tables)
    for n in range(members):
        last = sent_by(near, n, slice(8 * BLK, 9 * BLK))
        chosen[n * BLK : (n + 1) * BLK, :] = splat(last[:, LANES - 1 :]).astype(jnp.int32)
        coarse[lax.axis_index("mem") ^ n, :, :] = last

    def near_tile(m, d, n):
        at = ((d ^ 1) * 2 + n) * BLK
        return sent_by(near, m, slice(at, at + BLK)), table(Table.BLOCK + d)

    ghost = gather_ghosts(near_tile, members, Table.APART, from_first, from_second, table, ghosts, lane, 2)
    values = [eff[:, tile(m)] for m in range(TILES)]
    start = [[], [], []]
    for m in range(TILES):
        i, h = divmod(m, 2)
        e = values[m]
        side_k = unpack_k(ghost[0], ghost[1], lane, m)
        side_j = unpack_j(ghost[2], ghost[3], m)
        ends_j = (g == 0) if h == 0 else (g == 7)
        n0 = jnp.where(k == 0, side_k, roll(e, 1))
        n1 = jnp.where(k == 15, side_k, roll(e, -1))
        n2 = jnp.where(g == 0, side_j if h == 0 else roll(values[m - 1], 16), roll(e, 16))
        n3 = jnp.where(g == 7, side_j if h == 1 else roll(values[m + 1], -16), roll(e, -16))
        n4 = ghost[4][h] if i == 0 else values[m - 2]
        n5 = ghost[5][h] if i == EDGE - 1 else values[m + 2]
        w = [0.5 * (e + n) for n in (n0, n1, n2, n3, n4, n5)]
        diag = MASS_TERM * e
        for d in range(6):
            diag = diag + w[d]
        inv = 1.0 / diag
        diagonal[:, tile(m)] = diag
        inverse[:, tile(m)] = inv
        wi[0, :, tile(m)] = jnp.where(k == 0, 0.0, w[0])
        wi[1, :, tile(m)] = jnp.where(k == 15, 0.0, w[1])
        wi[2, :, tile(m)] = jnp.where(ends_j, 0.0, w[2]) if h == 0 else w[2]
        wi[3, :, tile(m)] = jnp.where(ends_j, 0.0, w[3]) if h == 1 else w[3]
        wi[4, :, tile(m)] = w[4]
        gk[:, tile(m)] = jnp.where(k == 0, w[0], jnp.where(k == 15, w[1], 0.0))
        gj[:, tile(m)] = jnp.where(ends_j, w[2 + h], 0.0)
        if i == 0:
            gi[:, tile(h)] = w[4]
        if i == EDGE - 1:
            gi[:, tile(2 + h)] = w[5]
        scale = inv * (1.0 / THETA)
        for c in range(3):
            f = forcing[c, :, tile(m)]
            s = f * scale
            state[R + c, :, tile(m)] = f
            state[S + c, :, tile(m)] = s
            start[c].append(s)
    for c in range(3):
        emit_channel(c, start[c], chosen, table, mine, other, first, second, lane, members, cap)


def merge_kernel(mine, got, *pairs):
    for n, pair in enumerate(pairs):
        pair[0, :, :] = mine[n + 1, :, :]
        pair[1, :, :] = got[n + 1, :, :]


def inside_kernel(first_step, has_lift, final, *refs):
    refs = list(refs)
    state, wi, diagonal = refs[:3]
    refs = refs[3:]
    x = None if first_step else refs.pop(0)
    lift, fixed = None, {}
    if has_lift:
        lift = refs.pop(0)
        fixed = lift_inside(has_lift, refs[0], refs[1], state, *refs[2:5])
        refs = refs[5:]
    out, new_x = refs[:2]
    if final:
        staged, sems = refs[2:]
    g = lane_id() >> 4
    copies = []

    def get(row, m):
        return fixed[row, m] if (row, m) in fixed else state[row, :, tile(m)]

    for c in range(3):
        up = None if not has_lift else lift[c * BLK : (c + 1) * BLK, :]
        for m in range(TILES):
            i, h = divmod(m, 2)
            s = get(S + c, m)
            n2, n3 = roll(s, 16), roll(s, -16)
            if h == 1:
                n2 = jnp.where(g == 0, roll(get(S + c, m - 1), 16), n2)
            else:
                n3 = jnp.where(g == 7, roll(get(S + c, m + 1), -16), n3)
            acc = get(R + c, m) - diagonal[:, tile(m)] * s
            acc = acc + wi[0, :, tile(m)] * roll(s, 1)
            acc = acc + wi[1, :, tile(m)] * roll(s, -1)
            acc = acc + wi[2, :, tile(m)] * n2
            acc = acc + wi[3, :, tile(m)] * n3
            if i > 0:
                acc = acc + wi[4, :, tile(m)] * get(S + c, m - 2)
            if i < EDGE - 1:
                acc = acc + wi[4, :, tile(m + 2)] * get(S + c, m + 2)
            out[R + c, :, tile(m)] = acc
            total = s if first_step else x[c, :, tile(m)] + s
            if has_lift:
                total = total + up
            if final:
                staged[c, :, tile(m)] = total
            else:
                new_x[c, :, tile(m)] = total
        if final:
            copies.append(pltpu.make_async_copy(staged.at[c], new_x.at[c], sems.at[c]))
            copies[c].start()
    for row in range(S, S + 3):
        for m in range(TILES):
            out[row, :, tile(m)] = get(row, m)
    for copy in copies:
        copy.wait()


def add_ghosts(c, m, value, ghost, gk, gj, gi, lane):
    i, h = divmod(m, 2)
    pair = slice(2 * c, 2 * c + 2)
    value = value + gk[:, tile(m)] * unpack_k(ghost[0][pair], ghost[1][pair], lane, m)
    value = value + gj[:, tile(m)] * unpack_j(ghost[2][pair], ghost[3][pair], m)
    if i == 0:
        value = value + gi[:, tile(h)] * ghost[4][2 * c + h]
    if i == EDGE - 1:
        value = value + gi[:, tile(2 + h)] * ghost[5][2 * c + h]
    return value


def outside_kernel(members, cap, old, new, has_lift, near, from_first, from_second, state, *refs):
    inverse, gk, gj, gi, tables, chosen, x = refs[:7]
    out, mine, other, first, second, same_x, ghosts = refs[-7:]
    lane = lane_id()
    table = Table(tables)
    amend = lift_outside(members, cap, near, from_first, from_second, refs[7], tables) if has_lift else None
    ghost = step_ghosts(members, cap, near, from_first, from_second, table, ghosts, lane, amend)
    for c in range(3):
        values = []
        for batch in BATCHES:
            done = []
            for m in batch:
                r = add_ghosts(c, m, state[R + c, :, tile(m)], ghost, gk, gj, gi, lane)
                done.append((m, r, old * state[S + c, :, tile(m)] + new * (r * inverse[:, tile(m)])))
            for m, r, s in done:
                out[R + c, :, tile(m)] = r
                out[S + c, :, tile(m)] = s
                values.append(s)
        emit_channel(c, values, chosen, table, mine, other, first, second, lane, members, cap)


def last_kernel(
    members, cap, near, from_first, from_second, state, gk, gj, gi, tables, new_residual, ghosts, staged, sems,
):
    lane = lane_id()
    ghost = step_ghosts(members, cap, near, from_first, from_second, Table(tables), ghosts, lane)
    copies = []
    for c in range(3):
        for m in range(TILES):
            staged[c, :, tile(m)] = add_ghosts(c, m, state[R + c, :, tile(m)], ghost, gk, gj, gi, lane)
        copies.append(pltpu.make_async_copy(staged.at[c], new_residual.at[c], sems.at[c]))
        copies[c].start()
    for copy in copies:
        copy.wait()


def coarse_kernel(
    members, cap, near, from_first, from_second, state, gk, gj, gi, tables, coarse, x,
    out_state, payload, same_x, ghosts,
):
    lane, sub = lane_id(), sub_id()
    ghost = step_ghosts(members, cap, near, from_first, from_second, Table(tables), ghosts, lane)
    placed = jnp.zeros((BLK, LANES), F32)
    for c in range(3):
        sums = [None] * 4
        for batch in BATCHES:
            done = [(m, add_ghosts(c, m, state[R + c, :, tile(m)], ghost, gk, gj, gi, lane)) for m in batch]
            for m, r in done:
                out_state[R + c, :, tile(m)] = r
                sums[m % 4] = r if sums[m % 4] is None else sums[m % 4] + r
        total = splat(lane_sum((sums[0] + sums[1]) + (sums[2] + sums[3])))
        placed = jnp.where(lane == 3 * sub + c, total, placed)
    own = jnp.sum(placed, axis=0, keepdims=True) * (1.0 / math.sqrt(CELLS))
    own = jnp.broadcast_to(own, (BLK, LANES))
    columns = BLK * 3
    wide = -(-members * columns // LANES)
    rows = [jnp.zeros((BLK, LANES), F32) for _ in range(wide)]
    for n in range(members):
        for v in range(3):
            have = jnp.where(lane < columns, roll(coarse[n, :, :], -v * columns), 0.0)
            part = splat(lane_sum(have * own))
            place = n * columns + v * BLK
            for t in range(place // LANES, (place + BLK - 1) // LANES + 1):
                rows[t] = jnp.where(lane + t * LANES == place + sub, part, rows[t])
    out = jnp.zeros((BLK, LANES), F32)
    for t in range(wide):
        out = jnp.where(sub == t, jnp.sum(rows[t], axis=0, keepdims=True), out)
    for n in range(members):
        payload[n, :, :] = out


def lift_kernel(
    members, cap, arrived, state, eff, inverse, gk, gj, gi, tables, chosen, x,
    out, lift, unknowns, mine, other, first, second, same_x,
):
    lane, sub = lane_id(), sub_id()
    k, g = lane & 15, lane >> 4
    table = Table(tables)
    wide = -(-members * BLK * 3 // LANES)
    member = lax.axis_index("mem")
    total = arrived[0, :, :]
    for n in range(1, members):
        total = total + arrived[n, :, :]
    unknowns[...] = total
    known = rows_of(total, wide)
    own = look_up(known, member * BLK + sub, lane)
    side = [look_up(known, table(Table.OWNER + d) * BLK + table(Table.BLOCK + d), lane) for d in range(4)]
    for c in range(3):
        values = []
        lift[c * BLK : (c + 1) * BLK, :] = own[c]
        drop_k = own[c] - jnp.where(k == 0, side[0][c], side[1][c])
        drop_j = [own[c] - side[2][c], own[c] - side[3][c]]
        for batch in BATCHES:
            done = []
            for m in batch:
                i, h = divmod(m, 2)
                applied = (MASS_TERM * eff[:, tile(m)]) * own[c]
                applied = applied + gk[:, tile(m)] * drop_k + gj[:, tile(m)] * drop_j[h]
                if i == 0:
                    applied = applied + gi[:, tile(h)] * own[c]
                if i == EDGE - 1:
                    applied = applied + gi[:, tile(2 + h)] * own[c]
                r = state[R + c, :, tile(m)] - applied
                done.append((m, r, r * (inverse[:, tile(m)] * (1.0 / THETA))))
            for m, r, s in done:
                out[R + c, :, tile(m)] = r
                out[S + c, :, tile(m)] = s
                values.append(s)
        emit_channel(c, values, chosen, table, mine, other, first, second, lane, members, cap)

    ends = end_weights(inverse, gi)
    planes = [table(Table.PLANE + d).astype(F32) for d in range(2)]
    emit_planes(ends[:2] + planes[:1], ends[2:] + planes[1:], table(Table.EVEN) == 1, 6, first, second)
    for ref in (first, second):
        ref[9 * BLK : 10 * BLK, :] = total
    edges = []
    for f in range(2):
        v = jnp.zeros((BLK, LANES), F32)
        for t, end in zip((0, 1, 14, 15), ends):
            v = jnp.where(k == t, roll(end, t - 15 * f), v)
        edges.append(v)
    edges.append(jnp.where(g == 0, ends[0], jnp.where(g == 7, roll(ends[2], 112), 0.0)))
    edges.append(jnp.where(g == 0, roll(ends[1], 16), jnp.where(g == 7, ends[3], 0.0)))
    edges = [jnp.where(lane == 18, planes[0], jnp.where(lane == 19, planes[1], v)) for v in edges]
    for m in range(members):
        want = chosen[m * BLK : (m + 1) * BLK, :]
        face, block = want >> 3, want & 7
        v = None
        for f in range(4):
            found = pick(edges[f], block)
            v = found if f == 0 else jnp.where(face == f, found, v)
        (mine, other)[m % 2][m // 2, 6 * cap : 6 * cap + BLK, :] = v


def end_weights(inverse, gi):
    return [
        gi[:, tile(n)] * (inverse[:, tile(m)] * (1.0 / THETA)) for n, m in enumerate((0, 1, TILES - 2, TILES - 1))
    ]


def lift_inside(members, from_first, from_second, state, inverse, gi, tables):
    lane = lane_id()
    table = Table(tables)
    wide = -(-members * BLK * 3 // LANES)
    member = lax.axis_index("mem")
    ends = end_weights(inverse, gi)
    fixed = {}
    for upper in range(2):
        rows = rows_of(from_side(from_first, from_second, table, 9, upper == 1), wide)
        beyond = look_up(rows, member * BLK + table(Table.PLANE + upper), lane)
        for c in range(3):
            for h in range(2):
                n, m = 2 * upper + h, upper * (TILES - 2) + h
                fixed[R + c, m] = state[R + c, :, tile(m)] + gi[:, tile(n)] * beyond[c]
                fixed[S + c, m] = state[S + c, :, tile(m)] + ends[n] * beyond[c]
    return fixed


def lift_outside(members, cap, near, from_first, from_second, unknowns, tables):
    lane = lane_id()
    k, g = lane & 15, lane >> 4
    table = Table(tables)
    wide = -(-members * BLK * 3 // LANES)
    member = lax.axis_index("mem")
    below, above = [
        rows_of(from_side(from_first, from_second, table, 9, upper), wide) for upper in (False, True)
    ]
    known = rows_of(unknowns[...], wide)
    parts = []
    for d in range(4):
        v = None
        for m in range(members):
            found = pick(sent_by(near, m, slice(6 * cap, 6 * cap + BLK)), table(Table.SLOT + d))
            v = found if m == 0 else jnp.where(table(Table.APART + d) == m, found, v)
        base = table(Table.OWNER + d) * BLK
        low = look_up(below, base + splat(v[:, 18:19]).astype(jnp.int32), lane)
        high = look_up(above, base + splat(v[:, 19:20]).astype(jnp.int32), lane)
        at_low, at_high = (k < 2, k > 13) if d < 2 else (g == 0, g == 7)
        weights = [jnp.where(at_low, v, 0.0), jnp.where(at_high, v, 0.0)]
        parts.append([weights[n % 2] * (low, high)[n % 2][n // 2] for n in range(6)])
    for upper in (False, True):
        index = from_side(from_first, from_second, table, 8, upper).astype(jnp.int32)
        own = look_up(known, member * BLK + index, lane)
        weights = [from_side(from_first, from_second, table, 6 + p, upper) for p in range(2)]
        parts.append([weights[n % 2] * own[n // 2] for n in range(6)])
    return lambda d, n, v: v + parts[d][n]


def local(
    forcing, viscosity, refinement, face_owner, face_block, plane_block, hanging, coarse_solver
):
    groups, members = lax.axis_size("grp"), lax.axis_size("mem")
    cap = 8 * BLK // members
    field = jax.ShapeDtypeStruct(forcing.shape, F32)
    scalar_field = jax.ShapeDtypeStruct(viscosity.shape, F32)
    states = jax.ShapeDtypeStruct((6, BLK, CELLS), F32)

    def array(*shape):
        return jax.ShapeDtypeStruct(shape, F32)

    def ints(*shape):
        return jax.ShapeDtypeStruct(shape, jnp.int32)

    def scratch(*shape):
        return pltpu.VMEM(shape, F32)

    def call(body, in_specs, out_shape, out_specs, scratch_shapes, name, aliases=None, moved=2_000_000):
        return pl.pallas_call(
            body,
            out_shape=out_shape,
            in_specs=in_specs,
            out_specs=out_specs,
            scratch_shapes=scratch_shapes,
            compiler_params=PARAMS,
            input_output_aliases=aliases or {},
            cost_estimate=pl.CostEstimate(flops=2_000_000, bytes_accessed=moved, transcendentals=0),
            name=name,
        )

    first_route = [(q * members + m, (q ^ 1) * members + m) for q in range(groups) for m in range(members)]
    second_route = []
    for q in range(groups):
        for m in range(members):
            if q == 0 or q == groups - 1:
                second_route.append((q * members + m, q * members + (m ^ 1)))
            else:
                second_route.append((q * members + m, (q + 1 if q % 2 else q - 1) * members + m))

    def swap(a, bits):
        return lax.ppermute(a, "mem", [(m, m ^ bits) for m in range(members)])

    def spread(mine, other, first, second):
        first = lax.ppermute(first, ("grp", "mem"), first_route)
        second = lax.ppermute(second, ("grp", "mem"), second_route)
        got = swap(other, 1)
        pairs = members // 2 - 1
        sent = call(
            merge_kernel, [VMEM] * 2, [array(2, *mine.shape[1:])] * pairs, [VMEM] * pairs, [], "merge", moved=200_000
        )(mine, got)
        return [mine, got] + [swap(a, 2 * n + 2) for n, a in enumerate(sent)], first, second

    per = 9 * BLK
    half = array(members // 2, per, LANES)
    eff = viscosity * jnp.exp2(-refinement.astype(F32))[:, None]
    mine, other, first, second, tables = call(
        functools.partial(prepare_kernel, members, groups, cap),
        [VMEM] + [HBM] * 4 + [VMEM],
        [half, half, array(16, LANES), array(16, LANES), ints(Table.SIZE * BLK, LANES)],
        [VMEM] * 5,
        [
            pltpu.VMEM((1, 4 * BLK), jnp.int32), pltpu.VMEM((4, BLK), jnp.int32),
            pltpu.VMEM((2, BLK), jnp.int32), pltpu.VMEM((BLK, 6), jnp.int32), scratch(members, BLK, LANES),
            pltpu.SemaphoreType.DMA((4,)),
        ],
        "prepare",
        moved=0,
    )(eff, face_owner.T, face_block.T, plane_block.T, hanging, jnp.pad(coarse_solver[0], ((0, 0), (0, -coarse_solver.shape[2] % LANES))))
    near, from_first, from_second = spread(mine, other, first, second)

    half = array(members // 2, 6 * cap, LANES)
    sent_out = [half, half, array(48, LANES), array(48, LANES)]
    near_refs = members // 2 + 1
    ghost_scratch = [scratch(3, 6 * 48, LANES)]

    def gathered(body, *fixed):
        return lambda *refs: body(*fixed, refs[:near_refs], *refs[near_refs:])

    state, mine, other, first, second, wi, gk, gj, gi, diagonal, inverse, chosen, coarse = call(
        gathered(weights_kernel, members, cap),
        [VMEM] * (near_refs + 5),
        [states] + sent_out
        + [array(5, BLK, CELLS), scalar_field, scalar_field, array(BLK, 4 * LANES), scalar_field, scalar_field]
        + [ints(members * BLK, LANES), array(members, BLK, LANES)],
        [VMEM] * 13,
        [scratch(3, 6 * 16, LANES)],
        "weights",
    )(*near, from_first, from_second, eff, forcing, tables)

    field_scratch = [scratch(3, BLK, CELLS), pltpu.SemaphoreType.DMA((3,))]

    def inside(state, x=None, lift=(), final=False):
        operands = [state, wi, diagonal] + ([] if x is None else [x]) + list(lift)
        return call(
            functools.partial(inside_kernel, x is None, members if lift else 0, final),
            [VMEM] * len(operands),
            [states, field],
            [VMEM, HBM if final else VMEM],
            field_scratch * final,
            "inside",
            {0: 0} if x is None or final else {0: 0, 3: 1},
        )(*operands)

    def outside(near, from_first, from_second, state, x, old, new, unknowns=None):
        more = [] if unknowns is None else [unknowns]
        return call(
            gathered(outside_kernel, members, cap, old, new, unknowns is not None),
            [VMEM] * (near_refs + 9) + [ANY] + [VMEM] * len(more),
            [states] + sent_out + [field],
            [VMEM] * 5 + [ANY],
            ghost_scratch,
            "outside",
            {near_refs + 2: 0, near_refs + 9: 5},
        )(*near, from_first, from_second, state, inverse, gk, gj, gi, tables, chosen, x, *more)

    rho = 1.0 / SIGMA
    factors = []
    for _ in range(DEG - 1):
        rho_next = 1.0 / (2.0 * SIGMA - rho)
        factors.append((rho_next * rho, 2.0 * rho_next / DELTA))
        rho = rho_next

    def steps(state, sent, x, lift=None, unknowns=None):
        for n, (old, new) in enumerate(factors):
            near, from_first, from_second = spread(*sent)
            more = (lift, from_first, from_second, inverse, gi, tables) if n == 0 and lift is not None else ()
            state, x = inside(state, x, more)
            state, *sent, x = outside(
                near, from_first, from_second, state, x, old, new, unknowns if n == 0 else None
            )
        return state, x, spread(*sent)

    state, x, (near, from_first, from_second) = steps(state, (mine, other, first, second), None)
    state, x = inside(state, x)
    state, payload, x = call(
        gathered(coarse_kernel, members, cap),
        [VMEM] * (near_refs + 8) + [ANY],
        [states, array(members, BLK, LANES), field],
        [VMEM, VMEM, ANY],
        ghost_scratch,
        "coarse",
        {near_refs + 2: 0, near_refs + 8: 2},
    )(*near, from_first, from_second, state, gk, gj, gi, tables, coarse, x)
    sums = lax.all_to_all(payload, "mem", split_axis=0, concat_axis=0, tiled=True)
    half = array(members // 2, 6 * cap + BLK, LANES)
    state, lift, unknowns, *sent, x = call(
        functools.partial(lift_kernel, members, cap),
        [VMEM] * 9 + [ANY],
        [states, array(3 * BLK, LANES), array(BLK, LANES), half, half, array(80, LANES), array(80, LANES), field],
        [VMEM] * 7 + [ANY],
        [],
        "lift",
        {1: 0, 9: 7},
    )(sums, state, eff, inverse, gk, gj, gi, tables, chosen, x)
    state, x, (near, from_first, from_second) = steps(state, sent, x, lift, unknowns)
    state, velocity = inside(state, x, final=True)
    residual = call(
        gathered(last_kernel, members, cap),
        [VMEM] * (near_refs + 7),
        [field],
        [HBM],
        ghost_scratch + field_scratch,
        "last",
    )(*near, from_first, from_second, state, gk, gj, gi, tables)[0]
    return velocity, residual


def solution(mesh):
    in_specs = (
        P(None, ("grp", "mem"), None),
        P(("grp", "mem"), None),
        P(("grp", "mem")),
        P(("grp", "mem"), None),
        P(("grp", "mem"), None),
        P(("grp", "mem"), None),
        P(("grp", "mem"), None),
        P("grp", "mem", None),
    )
    out_specs = (P(None, ("grp", "mem"), None), P(None, ("grp", "mem"), None))
    return jax.shard_map(local, mesh=mesh, in_specs=in_specs, out_specs=out_specs, check_vma=False)
```

```python
import functools
import math

import jax
import jax.numpy as jnp
from jax import lax
from jax.experimental import pallas as pl
from jax.experimental.pallas import tpu as pltpu
from jax.sharding import PartitionSpec as P

EDGE = 16
DEG = 3
CELLS = 4096
MASS_TERM = 1.0
LOWER_BOUND = 0.25
UPPER_BOUND = 2.0
THETA = 0.5 * (UPPER_BOUND + LOWER_BOUND)
DELTA = 0.5 * (UPPER_BOUND - LOWER_BOUND)
SIGMA = THETA / DELTA

LANES = 128
BLK = 8
TILES = CELLS // LANES
BATCHES = [range(m, m + 8) for m in range(0, TILES, 8)]
F32 = jnp.float32
R, S = 0, 3
VMEM = pl.BlockSpec(memory_space=pltpu.VMEM)
ANY = pl.BlockSpec(memory_space=pl.ANY)
HBM = pl.BlockSpec(memory_space=pltpu.HBM)
PARAMS = pltpu.CompilerParams(vmem_limit_bytes=8 * 1024 * 1024)


def lane_id():
    return lax.broadcasted_iota(jnp.int32, (BLK, LANES), 1)


def sub_id():
    return lax.broadcasted_iota(jnp.int32, (BLK, LANES), 0)


def roll(v, shift):
    shift = shift % LANES
    return v if shift == 0 else pltpu.roll(v, shift, 1)


def tile(m):
    return slice(m * LANES, (m + 1) * LANES)


def pack_faces(values, lane):
    k, g = lane & 15, lane >> 4
    faces = [[], [], [], []]
    for p in range(2):
        low = high = None
        for t in range(16):
            moved = roll(values[16 * p + t], t)
            low = moved if t == 0 else jnp.where(k == t, moved, low)
            high = moved if t == 0 else jnp.where(k == (15 + t) % 16, moved, high)
        faces[0].append(low)
        faces[1].append(roll(high, -15))
        low = high = None
        for t in range(8):
            i = 8 * p + t
            first = roll(values[2 * i], 16 * t)
            last = roll(values[2 * i + 1], 16 * t + 16)
            low = first if t == 0 else jnp.where(g == t, first, low)
            high = last if t == 0 else jnp.where(g == t, last, high)
        faces[2].append(low)
        faces[3].append(high)
    return faces


def unpack_k(low, high, lane, m):
    t = m % 16
    return jnp.where((lane & 15) == 0, roll(low[m // 16], -t), roll(high[m // 16], 15 - t))


def unpack_j(low, high, m):
    i = m // 2
    if m % 2 == 0:
        return roll(low[i // 8], -16 * (i % 8))
    return roll(high[i // 8], 112 - 16 * (i % 8))


def pick(values, index):
    return jnp.take_along_axis(values, index, axis=0, mode="promise_in_bounds")


def lane_sum(v):
    return jnp.sum(v, axis=1, keepdims=True)


def splat(column):
    return jnp.broadcast_to(column, (BLK, LANES))


class Table:
    OWNER, SLOT, BLOCK, PLANE, EVEN, LOWER, UPPER, HANG, APART = 0, 4, 8, 12, 14, 15, 16, 17, 23
    SIZE = 27

    def __init__(self, ref):
        self.ref = ref

    def __call__(self, n):
        return self.ref[n * BLK : (n + 1) * BLK, :]


def gather_ghosts(near_tile, members, who, first, second, table, ghosts, lane, rows, amend=None, faces=range(6)):
    even = table(Table.EVEN) == 1
    for d in faces:
        for n in range(rows):
            if d < 4:
                v = None
                for m in range(members):
                    source, index = near_tile(m, d, n)
                    found = pick(source, index)
                    v = found if m == 0 else jnp.where(table(who + d) == m, found, v)
                if amend:
                    v = amend(d, n, v)
            else:
                a, b = first[n * BLK : (n + 1) * BLK, :], second[n * BLK : (n + 1) * BLK, :]
                v = jnp.where(even, b, a) if d == 4 else jnp.where(even, a, b)
                if amend:
                    v = amend(d, n, v)
                inside = table(Table.LOWER if d == 4 else Table.UPPER) == 1
                v = jnp.where(inside, pick(v, table(Table.PLANE + d - 4)), 0.0)
            at = (d * rows + n) * BLK
            ghosts[0, at : at + BLK, :] = v
    for stage in range(2):
        for d in faces:
            bit = 16 if stage else (2 if d < 2 else 1)
            low = (lane & bit) == 0
            for n in range(rows):
                at = (d * rows + n) * BLK
                v = ghosts[stage, at : at + BLK, :]
                ghosts[stage + 1, at : at + BLK, :] = v + jnp.where(low, roll(v, -bit), roll(v, bit))
    result = {}
    for d in faces:
        hang = table(Table.HANG + d) == 1
        tiles = []
        for n in range(rows):
            at = (d * rows + n) * BLK
            tiles.append(jnp.where(hang, ghosts[2, at : at + BLK, :] * 0.25, ghosts[0, at : at + BLK, :]))
        result[d] = tiles
    return result


def sent_by(near, apart, rows):
    pair, bit = divmod(apart, 2)
    return near[bit][0, rows, :] if pair == 0 else near[1 + pair][bit, rows, :]


def step_ghosts(members, cap, near, first, second, table, ghosts, lane, amend=None, faces=range(6)):
    def near_tile(m, d, n):
        start = n * cap
        at = start // BLK * BLK
        return sent_by(near, m, slice(at, at + BLK)), table(Table.SLOT + d) + (start - at)

    return gather_ghosts(near_tile, members, Table.APART, first, second, table, ghosts, lane, 6, amend, faces)


def look_up(rows, block, lane):
    found = []
    for c in range(3):
        total = jnp.zeros((BLK, LANES), F32)
        for t, values in enumerate(rows):
            total = total + jnp.where(lane + t * LANES == 3 * block + c, values, 0.0)
        found.append(splat(lane_sum(total)))
    return found


def rows_of(v, wide):
    return [jnp.broadcast_to(v[t : t + 1, :], (BLK, LANES)) for t in range(wide)]


def from_side(first, second, table, n, upper):
    a, b = first[n * BLK : (n + 1) * BLK, :], second[n * BLK : (n + 1) * BLK, :]
    even = table(Table.EVEN) == 1
    v = jnp.where(even, a, b) if upper else jnp.where(even, b, a)
    return jnp.where(table(Table.UPPER if upper else Table.LOWER) == 1, v, 0.0)


def emit_planes(low, high, even, at, first, second):
    for n in range(len(low)):
        span = slice((at + n) * BLK, (at + n + 1) * BLK)
        first[span, :] = jnp.where(even, high[n], low[n])
        second[span, :] = jnp.where(even, low[n], high[n])


def emit_channel(c, values, chosen, table, mine, other, first, second, lane, members, cap):
    packed = pack_faces(values, lane)
    emit_planes(values[:2], values[-2:], table(Table.EVEN) == 1, 2 * c, first, second)
    sub = sub_id()
    for m in range(members):
        want = chosen[m * BLK : (m + 1) * BLK, :]
        face, block = want >> 3, want & 7
        for u in range(2 * cap // BLK):
            out = None
            for p in range(2):
                if not u * BLK <= p * cap < (u + 1) * BLK:
                    continue
                v = None
                for f in range(4):
                    found = pick(packed[f][p], block)
                    v = found if f == 0 else jnp.where(face == f, found, v)
                out = v if out is None else jnp.where(sub < p * cap - u * BLK, out, v)
            at = c * 2 * cap + u * BLK
            (mine, other)[m % 2][m // 2, at : at + BLK, :] = out


def prepare_kernel(
    members, groups, cap, eff, owner_hbm, block_hbm, plane_hbm, hanging_hbm, coarse_rows,
    mine, other, first, second, tables,
    face_owner, face_block, plane_block, hanging, special, sems,
):
    copies = [
        pltpu.make_async_copy(source, target, sems.at[n])
        for n, (source, target) in enumerate(
            [
                (owner_hbm, face_owner), (block_hbm, face_block), (plane_hbm, plane_block), (hanging_hbm, hanging),
            ]
        )
    ]
    for copy in copies:
        copy.start()
    lane, sub = lane_id(), sub_id()
    group, member = lax.axis_index("grp"), lax.axis_index("mem")
    even = group % 2 == 0
    for copy in copies:
        copy.wait()

    def iotas(width):
        return (
            lax.broadcasted_iota(jnp.int32, (BLK, width), 1), lax.broadcasted_iota(jnp.int32, (BLK, width), 0)
        )

    lane8, sub8 = iotas(BLK)
    lane32, sub32 = iotas(4 * BLK)
    lane64, sub64 = iotas(members * cap)

    def column(row):
        wide = jnp.broadcast_to(row.astype(F32), (BLK, BLK))
        return lane_sum(jnp.where(lane8 == sub8, wide, 0.0))

    def put(n, value):
        tables[n * BLK : (n + 1) * BLK, :] = splat(value).astype(jnp.int32)

    values = [eff[:, tile(m)] for m in range(TILES)]
    packed = pack_faces(values, lane)
    emit_planes(values[:2], values[-2:], even, 0, first, second)

    row = jnp.broadcast_to(face_owner[...].astype(F32), (BLK, 4 * BLK))
    wanted = jnp.zeros((BLK, members * cap), F32)
    for d in range(4):
        place = 4 * sub32 + d
        owner = lane_sum(jnp.where(lane32 == place, row, 0.0))
        slot = lane_sum(jnp.where((lane32 < place) & (row == owner), 1.0, 0.0))
        block = column(face_block[d : d + 1, :])
        put(Table.OWNER + d, owner)
        at = (Table.APART + d) * BLK
        tables[at : at + BLK, :] = splat(owner).astype(jnp.int32) ^ jnp.full((BLK, LANES), member, jnp.int32)
        put(Table.SLOT + d, slot)
        put(Table.BLOCK + d, block)
        target = jnp.broadcast_to(owner * cap + slot, (BLK, members * cap))
        want = jnp.broadcast_to(block + (d ^ 1) * BLK, (BLK, members * cap))
        wanted = wanted + jnp.where(lane64.astype(F32) == target, want, 0.0)
    wanted = jnp.broadcast_to(jnp.sum(wanted, axis=0, keepdims=True), (BLK, members * cap))
    for d in range(2):
        put(Table.PLANE + d, column(plane_block[d : d + 1, :]))
    for n, flag in ((Table.EVEN, even), (Table.LOWER, group > 0), (Table.UPPER, group < groups - 1)):
        tables[n * BLK : (n + 1) * BLK, :] = jnp.full((BLK, LANES), jnp.where(flag, 1, 0), jnp.int32)
    for d in range(6):
        put(Table.HANG + d, hanging[:, d : d + 1])

    def coarse_tile(rows, at):
        have = coarse_rows[rows, at * LANES : min((at + 1) * LANES, coarse_rows.shape[1])]
        missing = LANES - have.shape[1]
        return have if missing == 0 else jnp.concatenate([have, jnp.zeros((BLK, missing), F32)], axis=1)

    columns = BLK * 3
    for n in range(members):
        for f in range(4):
            for p in range(2):
                at = (f * 2 + p) * BLK
                (mine, other)[n % 2][n // 2, at : at + BLK, :] = packed[f][p]
        request = lane_sum(jnp.where(lane64 == n * cap + sub64 % cap, wanted, 0.0))
        last = splat(request)
        at, off = divmod(n * columns, LANES)
        for v in range(3):
            rows = slice(v * BLK, (v + 1) * BLK)
            part = roll(coarse_tile(rows, at), v * columns - off)
            if off + columns > LANES:
                more = roll(coarse_tile(rows, at + 1), v * columns - off)
                part = jnp.where(lane < v * columns + LANES - off, part, more)
            last = jnp.where((lane >= v * columns) & (lane < (v + 1) * columns), part, last)
        special[member ^ n, :, :] = last
    for n in range(members):
        (mine, other)[n % 2][n // 2, 8 * BLK : 9 * BLK, :] = special[n, :, :]


def weights_kernel(
    members, cap, near, from_first, from_second, eff, forcing, tables,
    state, mine, other, first, second, wi, gk, gj, gi, diagonal, inverse, chosen, coarse, ghosts,
):
    lane = lane_id()
    k, g = lane & 15, lane >> 4
    table = Table(tables)
    for n in range(members):
        last = sent_by(near, n, slice(8 * BLK, 9 * BLK))
        chosen[n * BLK : (n + 1) * BLK, :] = splat(last[:, LANES - 1 :]).astype(jnp.int32)
        coarse[lax.axis_index("mem") ^ n, :, :] = last

    def near_tile(m, d, n):
        at = ((d ^ 1) * 2 + n) * BLK
        return sent_by(near, m, slice(at, at + BLK)), table(Table.BLOCK + d)

    ghost = gather_ghosts(near_tile, members, Table.APART, from_first, from_second, table, ghosts, lane, 2)
    values = [eff[:, tile(m)] for m in range(TILES)]
    start = [[], [], []]
    for m in range(TILES):
        i, h = divmod(m, 2)
        e = values[m]
        side_k = unpack_k(ghost[0], ghost[1], lane, m)
        side_j = unpack_j(ghost[2], ghost[3], m)
        ends_j = (g == 0) if h == 0 else (g == 7)
        n0 = jnp.where(k == 0, side_k, roll(e, 1))
        n1 = jnp.where(k == 15, side_k, roll(e, -1))
        n2 = jnp.where(g == 0, side_j if h == 0 else roll(values[m - 1], 16), roll(e, 16))
        n3 = jnp.where(g == 7, side_j if h == 1 else roll(values[m + 1], -16), roll(e, -16))
        n4 = ghost[4][h] if i == 0 else values[m - 2]
        n5 = ghost[5][h] if i == EDGE - 1 else values[m + 2]
        w = [0.5 * (e + n) for n in (n0, n1, n2, n3, n4, n5)]
        diag = MASS_TERM * e
        for d in range(6):
            diag = diag + w[d]
        inv = 1.0 / diag
        diagonal[:, tile(m)] = diag
        inverse[:, tile(m)] = inv
        wi[0, :, tile(m)] = jnp.where(k == 0, 0.0, w[0])
        wi[1, :, tile(m)] = jnp.where(k == 15, 0.0, w[1])
        wi[2, :, tile(m)] = jnp.where(ends_j, 0.0, w[2]) if h == 0 else w[2]
        wi[3, :, tile(m)] = jnp.where(ends_j, 0.0, w[3]) if h == 1 else w[3]
        wi[4, :, tile(m)] = w[4]
        gk[:, tile(m)] = jnp.where(k == 0, w[0], jnp.where(k == 15, w[1], 0.0))
        gj[:, tile(m)] = jnp.where(ends_j, w[2 + h], 0.0)
        if i == 0:
            gi[:, tile(h)] = w[4]
        if i == EDGE - 1:
            gi[:, tile(2 + h)] = w[5]
        scale = inv * (1.0 / THETA)
        for c in range(3):
            f = forcing[c, :, tile(m)]
            s = f * scale
            state[R + c, :, tile(m)] = f
            state[S + c, :, tile(m)] = s
            start[c].append(s)
    for c in range(3):
        emit_channel(c, start[c], chosen, table, mine, other, first, second, lane, members, cap)


def merge_kernel(mine, got, *pairs):
    for n, pair in enumerate(pairs):
        pair[0, :, :] = mine[n + 1, :, :]
        pair[1, :, :] = got[n + 1, :, :]


def inside_kernel(first_step, lifted, final, members, *refs):
    refs = list(refs)
    state, wi, diagonal = refs[:3]
    refs = refs[3:]
    lane = lane_id()
    lift, fixed = None, {}
    x = None if first_step else refs.pop(0)
    if lifted:
        lift = refs.pop(0)
        fixed = lift_inside(members, refs[0], refs[1], state, *refs[2:5])
        refs = refs[5:]
    out, new_x = refs[:2]
    if final:
        staged, sems = refs[2:]
    g = lane >> 4
    copies = []

    def get(row, m):
        return fixed[row, m] if (row, m) in fixed else state[row, :, tile(m)]

    for c in range(3):
        up = lift[c * BLK : (c + 1) * BLK, :] if lifted else None
        for m in range(TILES):
            i, h = divmod(m, 2)
            s = get(S + c, m)
            n2, n3 = roll(s, 16), roll(s, -16)
            if h == 1:
                n2 = jnp.where(g == 0, roll(get(S + c, m - 1), 16), n2)
            else:
                n3 = jnp.where(g == 7, roll(get(S + c, m + 1), -16), n3)
            acc = get(R + c, m) - diagonal[:, tile(m)] * s
            acc = acc + wi[0, :, tile(m)] * roll(s, 1)
            acc = acc + wi[1, :, tile(m)] * roll(s, -1)
            acc = acc + wi[2, :, tile(m)] * n2
            acc = acc + wi[3, :, tile(m)] * n3
            if i > 0:
                acc = acc + wi[4, :, tile(m)] * get(S + c, m - 2)
            if i < EDGE - 1:
                acc = acc + wi[4, :, tile(m + 2)] * get(S + c, m + 2)
            out[R + c, :, tile(m)] = acc
            total = s if first_step else x[c, :, tile(m)] + s
            if lifted:
                total = total + up
            if final:
                staged[c, :, tile(m)] = total
            else:
                new_x[c, :, tile(m)] = total
        if final:
            copies.append(pltpu.make_async_copy(staged.at[c], new_x.at[c], sems.at[c]))
            copies[c].start()
    for row in range(S, S + 3):
        for m in range(TILES):
            out[row, :, tile(m)] = get(row, m)
    for copy in copies:
        copy.wait()


def add_side(c, m, value, ghost, gk, gj, lane):
    pair = slice(2 * c, 2 * c + 2)
    value = value + gk[:, tile(m)] * unpack_k(ghost[0][pair], ghost[1][pair], lane, m)
    return value + gj[:, tile(m)] * unpack_j(ghost[2][pair], ghost[3][pair], m)


def add_ends(c, m, value, ghost, gi):
    i, h = divmod(m, 2)
    if i == 0:
        value = value + gi[:, tile(h)] * ghost[4][2 * c + h]
    if i == EDGE - 1:
        value = value + gi[:, tile(2 + h)] * ghost[5][2 * c + h]
    return value


def side_kernel(members, cap, near, state, gk, gj, tables, out, ghosts):
    lane = lane_id()
    ghost = step_ghosts(members, cap, near, None, None, Table(tables), ghosts, lane, None, range(4))
    for c in range(3):
        for batch in BATCHES:
            done = [(m, add_side(c, m, state[R + c, :, tile(m)], ghost, gk, gj, lane)) for m in batch]
            for m, r in done:
                out[R + c, :, tile(m)] = r
    out[S : S + 3, :, :] = state[S : S + 3, :, :]


def outside_kernel(
    members, cap, old, new, from_first, from_second, state, inverse, gi, tables, chosen, x, *refs,
):
    out, mine, other, first, second, same_x, ghosts = refs[-7:]
    lane = lane_id()
    table = Table(tables)
    lifted = len(refs) > 7
    if lifted:
        near, (unknowns, gk, gj) = refs[:-10], refs[-10:-7]
        amend = lift_outside(members, cap, near, from_first, from_second, unknowns, tables)
        ghost = step_ghosts(members, cap, near, from_first, from_second, table, ghosts, lane, amend)
    else:
        ghost = step_ghosts(members, cap, None, from_first, from_second, table, ghosts, lane, None, (4, 5))
    for c in range(3):
        values = []
        for batch in BATCHES:
            done = []
            for m in batch:
                r = add_ends(c, m, state[R + c, :, tile(m)], ghost, gi)
                if lifted:
                    r = add_side(c, m, r, ghost, gk, gj, lane)
                done.append((m, r, old * state[S + c, :, tile(m)] + new * (r * inverse[:, tile(m)])))
            for m, r, s in done:
                out[R + c, :, tile(m)] = r
                out[S + c, :, tile(m)] = s
                values.append(s)
        emit_channel(c, values, chosen, table, mine, other, first, second, lane, members, cap)


def last_kernel(
    members, cap, near, from_first, from_second, state, gk, gj, gi, tables, residual, ghosts, staged, sems,
):
    lane = lane_id()
    ghost = step_ghosts(members, cap, near, from_first, from_second, Table(tables), ghosts, lane)
    copies = []
    for c in range(3):
        for m in range(TILES):
            r = add_ends(c, m, state[R + c, :, tile(m)], ghost, gi)
            staged[c, :, tile(m)] = add_side(c, m, r, ghost, gk, gj, lane)
        copies.append(pltpu.make_async_copy(staged.at[c], residual.at[c], sems.at[c]))
        copies[c].start()
    for copy in copies:
        copy.wait()


def coarse_kernel(
    members, cap, from_first, from_second, state, gi, tables, coarse, x,
    out_state, payload, same_x, ghosts,
):
    lane, sub = lane_id(), sub_id()
    ghost = step_ghosts(members, cap, None, from_first, from_second, Table(tables), ghosts, lane, None, (4, 5))
    placed = jnp.zeros((BLK, LANES), F32)
    for c in range(3):
        sums = [None] * 4
        for batch in BATCHES:
            done = [(m, add_ends(c, m, state[R + c, :, tile(m)], ghost, gi)) for m in batch]
            for m, r in done:
                out_state[R + c, :, tile(m)] = r
                sums[m % 4] = r if sums[m % 4] is None else sums[m % 4] + r
        total = splat(lane_sum((sums[0] + sums[1]) + (sums[2] + sums[3])))
        placed = jnp.where(lane == 3 * sub + c, total, placed)
    own = jnp.sum(placed, axis=0, keepdims=True) * (1.0 / math.sqrt(CELLS))
    own = jnp.broadcast_to(own, (BLK, LANES))
    columns = BLK * 3
    wide = -(-members * columns // LANES)
    rows = [jnp.zeros((BLK, LANES), F32) for _ in range(wide)]
    for n in range(members):
        for v in range(3):
            have = jnp.where(lane < columns, roll(coarse[n, :, :], -v * columns), 0.0)
            part = splat(lane_sum(have * own))
            place = n * columns + v * BLK
            for t in range(place // LANES, (place + BLK - 1) // LANES + 1):
                rows[t] = jnp.where(lane + t * LANES == place + sub, part, rows[t])
    out = jnp.zeros((BLK, LANES), F32)
    for t in range(wide):
        out = jnp.where(sub == t, jnp.sum(rows[t], axis=0, keepdims=True), out)
    for n in range(members):
        payload[n, :, :] = out


def lift_kernel(
    members, cap, arrived, state, eff, inverse, gk, gj, gi, tables, chosen, x,
    out, lift, unknowns, mine, other, first, second, same_x,
):
    lane, sub = lane_id(), sub_id()
    k, g = lane & 15, lane >> 4
    table = Table(tables)
    wide = -(-members * BLK * 3 // LANES)
    member = lax.axis_index("mem")
    total = arrived[0, :, :]
    for n in range(1, members):
        total = total + arrived[n, :, :]
    unknowns[...] = total
    known = rows_of(total, wide)
    own = look_up(known, member * BLK + sub, lane)
    side = [look_up(known, table(Table.OWNER + d) * BLK + table(Table.BLOCK + d), lane) for d in range(4)]
    for c in range(3):
        values = []
        lift[c * BLK : (c + 1) * BLK, :] = own[c]
        drop_k = own[c] - jnp.where(k == 0, side[0][c], side[1][c])
        drop_j = [own[c] - side[2][c], own[c] - side[3][c]]
        for batch in BATCHES:
            done = []
            for m in batch:
                i, h = divmod(m, 2)
                applied = (MASS_TERM * eff[:, tile(m)]) * own[c]
                applied = applied + gk[:, tile(m)] * drop_k + gj[:, tile(m)] * drop_j[h]
                if i == 0:
                    applied = applied + gi[:, tile(h)] * own[c]
                if i == EDGE - 1:
                    applied = applied + gi[:, tile(2 + h)] * own[c]
                r = state[R + c, :, tile(m)] - applied
                done.append((m, r, r * (inverse[:, tile(m)] * (1.0 / THETA))))
            for m, r, s in done:
                out[R + c, :, tile(m)] = r
                out[S + c, :, tile(m)] = s
                values.append(s)
        emit_channel(c, values, chosen, table, mine, other, first, second, lane, members, cap)

    ends = end_weights(inverse, gi)
    planes = [table(Table.PLANE + d).astype(F32) for d in range(2)]
    emit_planes(ends[:2] + planes[:1], ends[2:] + planes[1:], table(Table.EVEN) == 1, 6, first, second)
    for ref in (first, second):
        ref[9 * BLK : 10 * BLK, :] = total
    edges = []
    for f in range(2):
        v = jnp.zeros((BLK, LANES), F32)
        for t, end in zip((0, 1, 14, 15), ends):
            v = jnp.where(k == t, roll(end, t - 15 * f), v)
        edges.append(v)
    edges.append(jnp.where(g == 0, ends[0], jnp.where(g == 7, roll(ends[2], 112), 0.0)))
    edges.append(jnp.where(g == 0, roll(ends[1], 16), jnp.where(g == 7, ends[3], 0.0)))
    edges = [jnp.where(lane == 18, planes[0], jnp.where(lane == 19, planes[1], v)) for v in edges]
    for m in range(members):
        want = chosen[m * BLK : (m + 1) * BLK, :]
        face, block = want >> 3, want & 7
        v = None
        for f in range(4):
            found = pick(edges[f], block)
            v = found if f == 0 else jnp.where(face == f, found, v)
        (mine, other)[m % 2][m // 2, 6 * cap : 6 * cap + BLK, :] = v


def end_weights(inverse, gi):
    return [
        gi[:, tile(n)] * (inverse[:, tile(m)] * (1.0 / THETA)) for n, m in enumerate((0, 1, TILES - 2, TILES - 1))
    ]


def lift_inside(members, from_first, from_second, state, inverse, gi, tables):
    lane = lane_id()
    table = Table(tables)
    wide = -(-members * BLK * 3 // LANES)
    member = lax.axis_index("mem")
    ends = end_weights(inverse, gi)
    fixed = {}
    for upper in range(2):
        rows = rows_of(from_side(from_first, from_second, table, 9, upper == 1), wide)
        beyond = look_up(rows, member * BLK + table(Table.PLANE + upper), lane)
        for c in range(3):
            for h in range(2):
                n, m = 2 * upper + h, upper * (TILES - 2) + h
                fixed[R + c, m] = state[R + c, :, tile(m)] + gi[:, tile(n)] * beyond[c]
                fixed[S + c, m] = state[S + c, :, tile(m)] + ends[n] * beyond[c]
    return fixed


def lift_outside(members, cap, near, from_first, from_second, unknowns, tables):
    lane = lane_id()
    k, g = lane & 15, lane >> 4
    table = Table(tables)
    wide = -(-members * BLK * 3 // LANES)
    member = lax.axis_index("mem")
    below, above = [
        rows_of(from_side(from_first, from_second, table, 9, upper), wide) for upper in (False, True)
    ]
    known = rows_of(unknowns[...], wide)
    parts = []
    for d in range(4):
        v = None
        for m in range(members):
            found = pick(sent_by(near, m, slice(6 * cap, 6 * cap + BLK)), table(Table.SLOT + d))
            v = found if m == 0 else jnp.where(table(Table.APART + d) == m, found, v)
        base = table(Table.OWNER + d) * BLK
        low = look_up(below, base + splat(v[:, 18:19]).astype(jnp.int32), lane)
        high = look_up(above, base + splat(v[:, 19:20]).astype(jnp.int32), lane)
        at_low, at_high = (k < 2, k > 13) if d < 2 else (g == 0, g == 7)
        weights = [jnp.where(at_low, v, 0.0), jnp.where(at_high, v, 0.0)]
        parts.append([weights[n % 2] * (low, high)[n % 2][n // 2] for n in range(6)])
    for upper in (False, True):
        index = from_side(from_first, from_second, table, 8, upper).astype(jnp.int32)
        own = look_up(known, member * BLK + index, lane)
        weights = [from_side(from_first, from_second, table, 6 + p, upper) for p in range(2)]
        parts.append([weights[n % 2] * own[n // 2] for n in range(6)])
    return lambda d, n, v: v + parts[d][n]


def local(
    forcing, viscosity, refinement, face_owner, face_block, plane_block, hanging, coarse_solver
):
    groups, members = lax.axis_size("grp"), lax.axis_size("mem")
    cap = 8 * BLK // members
    field = jax.ShapeDtypeStruct(forcing.shape, F32)
    scalar_field = jax.ShapeDtypeStruct(viscosity.shape, F32)
    states = jax.ShapeDtypeStruct((6, BLK, CELLS), F32)

    def array(*shape):
        return jax.ShapeDtypeStruct(shape, F32)

    def ints(*shape):
        return jax.ShapeDtypeStruct(shape, jnp.int32)

    def scratch(*shape):
        return pltpu.VMEM(shape, F32)

    def call(body, in_specs, out_shape, out_specs, scratch_shapes, name, aliases=None, moved=2_000_000):
        return pl.pallas_call(
            body,
            out_shape=out_shape,
            in_specs=in_specs,
            out_specs=out_specs,
            scratch_shapes=scratch_shapes,
            compiler_params=PARAMS,
            input_output_aliases=aliases or {},
            cost_estimate=pl.CostEstimate(flops=2_000_000, bytes_accessed=moved, transcendentals=0),
            name=name,
        )

    first_route = [(q * members + m, (q ^ 1) * members + m) for q in range(groups) for m in range(members)]
    second_route = []
    for q in range(groups):
        for m in range(members):
            if q == 0 or q == groups - 1:
                second_route.append((q * members + m, q * members + (m ^ 1)))
            else:
                second_route.append((q * members + m, (q + 1 if q % 2 else q - 1) * members + m))

    def swap(a, bits):
        return lax.ppermute(a, "mem", [(m, m ^ bits) for m in range(members)])

    def spread(mine, other, first, second):
        first = lax.ppermute(first, ("grp", "mem"), first_route)
        second = lax.ppermute(second, ("grp", "mem"), second_route)
        got = swap(other, 1)
        pairs = members // 2 - 1
        sent = call(
            merge_kernel, [VMEM] * 2, [array(2, *mine.shape[1:])] * pairs, [VMEM] * pairs, [], "merge", moved=200_000
        )(mine, got)
        return [mine, got] + [swap(a, 2 * n + 2) for n, a in enumerate(sent)], first, second

    per = 9 * BLK
    half = array(members // 2, per, LANES)
    eff = viscosity * jnp.exp2(-refinement.astype(F32))[:, None]
    mine, other, first, second, tables = call(
        functools.partial(prepare_kernel, members, groups, cap),
        [VMEM] + [HBM] * 4 + [VMEM],
        [half, half, array(16, LANES), array(16, LANES), ints(Table.SIZE * BLK, LANES)],
        [VMEM] * 5,
        [
            pltpu.VMEM((1, 4 * BLK), jnp.int32), pltpu.VMEM((4, BLK), jnp.int32),
            pltpu.VMEM((2, BLK), jnp.int32), pltpu.VMEM((BLK, 6), jnp.int32), scratch(members, BLK, LANES),
            pltpu.SemaphoreType.DMA((4,)),
        ],
        "prepare",
        moved=0,
    )(eff, face_owner.T, face_block.T, plane_block.T, hanging, jnp.pad(coarse_solver[0], ((0, 0), (0, -coarse_solver.shape[2] % LANES))))
    near, from_first, from_second = spread(mine, other, first, second)

    half = array(members // 2, 6 * cap, LANES)
    sent_out = [half, half, array(48, LANES), array(48, LANES)]
    near_refs = members // 2 + 1
    ghost_scratch = [scratch(3, 6 * 48, LANES)]

    def gathered(body, *fixed):
        return lambda *refs: body(*fixed, refs[:near_refs], *refs[near_refs:])

    state, mine, other, first, second, wi, gk, gj, gi, diagonal, inverse, chosen, coarse = call(
        gathered(weights_kernel, members, cap),
        [VMEM] * (near_refs + 5),
        [states] + sent_out
        + [array(5, BLK, CELLS), scalar_field, scalar_field, array(BLK, 4 * LANES), scalar_field, scalar_field]
        + [ints(members * BLK, LANES), array(members, BLK, LANES)],
        [VMEM] * 13,
        [scratch(3, 6 * 16, LANES)],
        "weights",
    )(*near, from_first, from_second, eff, forcing, tables)

    field_scratch = [scratch(3, BLK, CELLS), pltpu.SemaphoreType.DMA((3,))]

    def inside(state, x=None, lift=(), final=False):
        operands = [state, wi, diagonal] + ([] if x is None else [x]) + list(lift)
        return call(
            functools.partial(inside_kernel, x is None, bool(lift), final, members),
            [VMEM] * len(operands),
            [states, field],
            [VMEM, HBM if final else VMEM],
            field_scratch * final,
            "inside",
            {0: 0} if x is None or final else {0: 0, 3: 1},
        )(*operands)

    def side(near, state):
        return call(
            gathered(side_kernel, members, cap),
            [VMEM] * (near_refs + 4),
            [states],
            [VMEM],
            ghost_scratch,
            "side",
            {near_refs: 0},
        )(*near, state, gk, gj, tables)[0]

    def outside(from_first, from_second, state, x, old, new, more=()):
        return call(
            functools.partial(outside_kernel, members, cap, old, new),
            [VMEM] * 7 + [ANY] + [VMEM] * len(more),
            [states] + sent_out + [field],
            [VMEM] * 5 + [ANY],
            ghost_scratch,
            "outside",
            {2: 0, 7: 5},
        )(from_first, from_second, state, inverse, gi, tables, chosen, x, *more)

    rho = 1.0 / SIGMA
    factors = []
    for _ in range(DEG - 1):
        rho_next = 1.0 / (2.0 * SIGMA - rho)
        factors.append((rho_next * rho, 2.0 * rho_next / DELTA))
        rho = rho_next

    def steps(state, sent, x, lift=None, unknowns=None):
        for n, (old, new) in enumerate(factors):
            near, from_first, from_second = spread(*sent)
            more = ()
            if n == 0 and lift is not None:
                state, x = inside(state, x, (lift, from_first, from_second, inverse, gi, tables))
                more = (*near, unknowns, gk, gj)
            else:
                state, x = inside(state, x)
                state = side(near, state)
            state, *sent, x = outside(from_first, from_second, state, x, old, new, more)
        return state, x, spread(*sent)

    state, x, (near, from_first, from_second) = steps(state, (mine, other, first, second), None)
    state, x = inside(state, x)
    state = side(near, state)
    state, payload, x = call(
        functools.partial(coarse_kernel, members, cap),
        [VMEM] * 6 + [ANY],
        [states, array(members, BLK, LANES), field],
        [VMEM, VMEM, ANY],
        ghost_scratch,
        "coarse",
        {2: 0, 6: 2},
    )(from_first, from_second, state, gi, tables, coarse, x)
    sums = lax.all_to_all(payload, "mem", split_axis=0, concat_axis=0, tiled=True)
    half = array(members // 2, 6 * cap + BLK, LANES)
    state, lift, unknowns, *sent, x = call(
        functools.partial(lift_kernel, members, cap),
        [VMEM] * 9 + [ANY],
        [states, array(3 * BLK, LANES), array(BLK, LANES), half, half, array(80, LANES), array(80, LANES), field],
        [VMEM] * 7 + [ANY],
        [],
        "lift",
        {1: 0, 9: 7},
    )(sums, state, eff, inverse, gk, gj, gi, tables, chosen, x)
    state, x, (near, from_first, from_second) = steps(state, sent, x, lift, unknowns)
    state, velocity = inside(state, x, final=True)
    residual = call(
        gathered(last_kernel, members, cap),
        [VMEM] * (near_refs + 7),
        [field],
        [HBM],
        ghost_scratch + field_scratch,
        "last",
    )(*near, from_first, from_second, state, gk, gj, gi, tables)[0]
    return velocity, residual


def solution(mesh):
    in_specs = (
        P(None, ("grp", "mem"), None),
        P(("grp", "mem"), None),
        P(("grp", "mem")),
        P(("grp", "mem"), None),
        P(("grp", "mem"), None),
        P(("grp", "mem"), None),
        P(("grp", "mem"), None),
        P("grp", "mem", None),
    )
    out_specs = (P(None, ("grp", "mem"), None), P(None, ("grp", "mem"), None))
    return jax.shard_map(local, mesh=mesh, in_specs=in_specs, out_specs=out_specs, check_vma=False)
```

```python
import functools
import math

import jax
import jax.numpy as jnp
from jax import lax
from jax.experimental import pallas as pl
from jax.experimental.pallas import tpu as pltpu
from jax.sharding import PartitionSpec as P

EDGE = 16
DEG = 3
CELLS = 4096
MASS_TERM = 1.0
LOWER_BOUND = 0.25
UPPER_BOUND = 2.0
THETA = 0.5 * (UPPER_BOUND + LOWER_BOUND)
DELTA = 0.5 * (UPPER_BOUND - LOWER_BOUND)
SIGMA = THETA / DELTA

LANES = 128
BLK = 8
TILES = CELLS // LANES
BATCHES = [range(m, m + 8) for m in range(0, TILES, 8)]
F32 = jnp.float32
R, S = 0, 3
VMEM = pl.BlockSpec(memory_space=pltpu.VMEM)
ANY = pl.BlockSpec(memory_space=pl.ANY)
HBM = pl.BlockSpec(memory_space=pltpu.HBM)
PARAMS = pltpu.CompilerParams(vmem_limit_bytes=8 * 1024 * 1024)


def lane_id():
    return lax.broadcasted_iota(jnp.int32, (BLK, LANES), 1)


def sub_id():
    return lax.broadcasted_iota(jnp.int32, (BLK, LANES), 0)


def roll(v, shift):
    shift = shift % LANES
    return v if shift == 0 else pltpu.roll(v, shift, 1)


def tile(m):
    return slice(m * LANES, (m + 1) * LANES)


def pack_faces(values, lane):
    k, g = lane & 15, lane >> 4
    faces = [[], [], [], []]
    for p in range(2):
        low = high = None
        for t in range(16):
            moved = roll(values[16 * p + t], t)
            low = moved if t == 0 else jnp.where(k == t, moved, low)
            high = moved if t == 0 else jnp.where(k == (15 + t) % 16, moved, high)
        faces[0].append(low)
        faces[1].append(roll(high, -15))
        low = high = None
        for t in range(8):
            i = 8 * p + t
            first = roll(values[2 * i], 16 * t)
            last = roll(values[2 * i + 1], 16 * t + 16)
            low = first if t == 0 else jnp.where(g == t, first, low)
            high = last if t == 0 else jnp.where(g == t, last, high)
        faces[2].append(low)
        faces[3].append(high)
    return faces


def unpack_k(low, high, lane, m):
    t = m % 16
    return jnp.where((lane & 15) == 0, roll(low[m // 16], -t), roll(high[m // 16], 15 - t))


def unpack_j(low, high, m):
    i = m // 2
    if m % 2 == 0:
        return roll(low[i // 8], -16 * (i % 8))
    return roll(high[i // 8], 112 - 16 * (i % 8))


def pick(values, index):
    return jnp.take_along_axis(values, index, axis=0, mode="promise_in_bounds")


def lane_sum(v):
    return jnp.sum(v, axis=1, keepdims=True)


def splat(column):
    return jnp.broadcast_to(column, (BLK, LANES))


class Table:
    OWNER, SLOT, BLOCK, PLANE, EVEN, LOWER, UPPER, HANG, APART = 0, 4, 8, 12, 14, 15, 16, 17, 23
    SIZE = 27

    def __init__(self, ref):
        self.ref = ref

    def __call__(self, n):
        return self.ref[n * BLK : (n + 1) * BLK, :]


def gather_ghosts(near_tile, members, who, first, second, table, ghosts, lane, rows, amend=None, faces=range(6)):
    even = table(Table.EVEN) == 1
    for d in faces:
        for n in range(rows):
            if d < 4:
                v = None
                for m in range(members):
                    source, index = near_tile(m, d, n)
                    found = pick(source, index)
                    v = found if m == 0 else jnp.where(table(who + d) == m, found, v)
                if amend:
                    v = amend(d, n, v)
            else:
                a, b = first[n * BLK : (n + 1) * BLK, :], second[n * BLK : (n + 1) * BLK, :]
                v = jnp.where(even, b, a) if d == 4 else jnp.where(even, a, b)
                if amend:
                    v = amend(d, n, v)
                inside = table(Table.LOWER if d == 4 else Table.UPPER) == 1
                v = jnp.where(inside, pick(v, table(Table.PLANE + d - 4)), 0.0)
            at = (d * rows + n) * BLK
            ghosts[0, at : at + BLK, :] = v
    for stage in range(2):
        for d in faces:
            bit = 16 if stage else (2 if d < 2 else 1)
            low = (lane & bit) == 0
            for n in range(rows):
                at = (d * rows + n) * BLK
                v = ghosts[stage, at : at + BLK, :]
                ghosts[stage + 1, at : at + BLK, :] = v + jnp.where(low, roll(v, -bit), roll(v, bit))
    result = {}
    for d in faces:
        hang = table(Table.HANG + d) == 1
        tiles = []
        for n in range(rows):
            at = (d * rows + n) * BLK
            tiles.append(jnp.where(hang, ghosts[2, at : at + BLK, :] * 0.25, ghosts[0, at : at + BLK, :]))
        result[d] = tiles
    return result


def sent_by(near, apart, rows):
    pair, bit = divmod(apart, 2)
    return near[bit][0, rows, :] if pair == 0 else near[1 + pair][bit, rows, :]


def step_ghosts(members, cap, near, first, second, table, ghosts, lane, amend=None, faces=range(6)):
    def near_tile(m, d, n):
        start = n * cap
        at = start // BLK * BLK
        return sent_by(near, m, slice(at, at + BLK)), table(Table.SLOT + d) + (start - at)

    return gather_ghosts(near_tile, members, Table.APART, first, second, table, ghosts, lane, 6, amend, faces)


def look_up(rows, block, lane):
    found = []
    for c in range(3):
        total = jnp.zeros((BLK, LANES), F32)
        for t, values in enumerate(rows):
            total = total + jnp.where(lane + t * LANES == 3 * block + c, values, 0.0)
        found.append(splat(lane_sum(total)))
    return found


def rows_of(v, wide):
    return [jnp.broadcast_to(v[t : t + 1, :], (BLK, LANES)) for t in range(wide)]


def from_side(first, second, table, n, upper):
    a, b = first[n * BLK : (n + 1) * BLK, :], second[n * BLK : (n + 1) * BLK, :]
    even = table(Table.EVEN) == 1
    v = jnp.where(even, a, b) if upper else jnp.where(even, b, a)
    return jnp.where(table(Table.UPPER if upper else Table.LOWER) == 1, v, 0.0)


def emit_planes(low, high, even, at, first, second):
    for n in range(len(low)):
        span = slice((at + n) * BLK, (at + n + 1) * BLK)
        first[span, :] = jnp.where(even, high[n], low[n])
        second[span, :] = jnp.where(even, low[n], high[n])


def emit_channel(c, values, chosen, table, mine, other, first, second, lane, members, cap):
    packed = pack_faces(values, lane)
    emit_planes(values[:2], values[-2:], table(Table.EVEN) == 1, 2 * c, first, second)
    sub = sub_id()
    for m in range(members):
        want = chosen[m * BLK : (m + 1) * BLK, :]
        face, block = want >> 3, want & 7
        for u in range(2 * cap // BLK):
            out = None
            for p in range(2):
                if not u * BLK <= p * cap < (u + 1) * BLK:
                    continue
                v = None
                for f in range(4):
                    found = pick(packed[f][p], block)
                    v = found if f == 0 else jnp.where(face == f, found, v)
                out = v if out is None else jnp.where(sub < p * cap - u * BLK, out, v)
            at = c * 2 * cap + u * BLK
            (mine, other)[m % 2][m // 2, at : at + BLK, :] = out


def prepare_kernel(
    members, groups, cap, eff, owner_hbm, block_hbm, plane_hbm, hanging_hbm, coarse_rows,
    mine, other, first, second, tables,
    face_owner, face_block, plane_block, hanging, special, sems,
):
    copies = [
        pltpu.make_async_copy(source, target, sems.at[n])
        for n, (source, target) in enumerate(
            [
                (owner_hbm, face_owner), (block_hbm, face_block), (plane_hbm, plane_block), (hanging_hbm, hanging),
            ]
        )
    ]
    for copy in copies:
        copy.start()
    lane, sub = lane_id(), sub_id()
    group, member = lax.axis_index("grp"), lax.axis_index("mem")
    even = group % 2 == 0
    for copy in copies:
        copy.wait()

    def iotas(width):
        return (
            lax.broadcasted_iota(jnp.int32, (BLK, width), 1), lax.broadcasted_iota(jnp.int32, (BLK, width), 0)
        )

    lane8, sub8 = iotas(BLK)
    lane32, sub32 = iotas(4 * BLK)
    lane64, sub64 = iotas(members * cap)

    def column(row):
        wide = jnp.broadcast_to(row.astype(F32), (BLK, BLK))
        return lane_sum(jnp.where(lane8 == sub8, wide, 0.0))

    def put(n, value):
        tables[n * BLK : (n + 1) * BLK, :] = splat(value).astype(jnp.int32)

    values = [eff[:, tile(m)] for m in range(TILES)]
    packed = pack_faces(values, lane)
    emit_planes(values[:2], values[-2:], even, 0, first, second)

    row = jnp.broadcast_to(face_owner[...].astype(F32), (BLK, 4 * BLK))
    wanted = jnp.zeros((BLK, members * cap), F32)
    for d in range(4):
        place = 4 * sub32 + d
        owner = lane_sum(jnp.where(lane32 == place, row, 0.0))
        slot = lane_sum(jnp.where((lane32 < place) & (row == owner), 1.0, 0.0))
        block = column(face_block[d : d + 1, :])
        put(Table.OWNER + d, owner)
        at = (Table.APART + d) * BLK
        tables[at : at + BLK, :] = splat(owner).astype(jnp.int32) ^ jnp.full((BLK, LANES), member, jnp.int32)
        put(Table.SLOT + d, slot)
        put(Table.BLOCK + d, block)
        target = jnp.broadcast_to(owner * cap + slot, (BLK, members * cap))
        want = jnp.broadcast_to(block + (d ^ 1) * BLK, (BLK, members * cap))
        wanted = wanted + jnp.where(lane64.astype(F32) == target, want, 0.0)
    wanted = jnp.broadcast_to(jnp.sum(wanted, axis=0, keepdims=True), (BLK, members * cap))
    for d in range(2):
        put(Table.PLANE + d, column(plane_block[d : d + 1, :]))
    for n, flag in ((Table.EVEN, even), (Table.LOWER, group > 0), (Table.UPPER, group < groups - 1)):
        tables[n * BLK : (n + 1) * BLK, :] = jnp.full((BLK, LANES), jnp.where(flag, 1, 0), jnp.int32)
    for d in range(6):
        put(Table.HANG + d, hanging[:, d : d + 1])

    def coarse_tile(rows, at):
        have = coarse_rows[rows, at * LANES : min((at + 1) * LANES, coarse_rows.shape[1])]
        missing = LANES - have.shape[1]
        return have if missing == 0 else jnp.concatenate([have, jnp.zeros((BLK, missing), F32)], axis=1)

    columns = BLK * 3
    for n in range(members):
        for f in range(4):
            for p in range(2):
                at = (f * 2 + p) * BLK
                (mine, other)[n % 2][n // 2, at : at + BLK, :] = packed[f][p]
        request = lane_sum(jnp.where(lane64 == n * cap + sub64 % cap, wanted, 0.0))
        last = splat(request)
        at, off = divmod(n * columns, LANES)
        for v in range(3):
            rows = slice(v * BLK, (v + 1) * BLK)
            part = roll(coarse_tile(rows, at), v * columns - off)
            if off + columns > LANES:
                more = roll(coarse_tile(rows, at + 1), v * columns - off)
                part = jnp.where(lane < v * columns + LANES - off, part, more)
            last = jnp.where((lane >= v * columns) & (lane < (v + 1) * columns), part, last)
        special[member ^ n, :, :] = last
    for n in range(members):
        (mine, other)[n % 2][n // 2, 8 * BLK : 9 * BLK, :] = special[n, :, :]


def weights_kernel(
    members, cap, near, from_first, from_second, eff, forcing, tables,
    state, mine, other, first, second, wi, gk, gj, gi, diagonal, inverse, chosen, coarse, ghosts,
):
    lane = lane_id()
    k, g = lane & 15, lane >> 4
    table = Table(tables)
    for n in range(members):
        last = sent_by(near, n, slice(8 * BLK, 9 * BLK))
        chosen[n * BLK : (n + 1) * BLK, :] = splat(last[:, LANES - 1 :]).astype(jnp.int32)
        coarse[lax.axis_index("mem") ^ n, :, :] = last

    def near_tile(m, d, n):
        at = ((d ^ 1) * 2 + n) * BLK
        return sent_by(near, m, slice(at, at + BLK)), table(Table.BLOCK + d)

    ghost = gather_ghosts(near_tile, members, Table.APART, from_first, from_second, table, ghosts, lane, 2)
    values = [eff[:, tile(m)] for m in range(TILES)]
    start = [[], [], []]
    for m in range(TILES):
        i, h = divmod(m, 2)
        e = values[m]
        side_k = unpack_k(ghost[0], ghost[1], lane, m)
        side_j = unpack_j(ghost[2], ghost[3], m)
        ends_j = (g == 0) if h == 0 else (g == 7)
        n0 = jnp.where(k == 0, side_k, roll(e, 1))
        n1 = jnp.where(k == 15, side_k, roll(e, -1))
        n2 = jnp.where(g == 0, side_j if h == 0 else roll(values[m - 1], 16), roll(e, 16))
        n3 = jnp.where(g == 7, side_j if h == 1 else roll(values[m + 1], -16), roll(e, -16))
        n4 = ghost[4][h] if i == 0 else values[m - 2]
        n5 = ghost[5][h] if i == EDGE - 1 else values[m + 2]
        w = [0.5 * (e + n) for n in (n0, n1, n2, n3, n4, n5)]
        diag = MASS_TERM * e
        for d in range(6):
            diag = diag + w[d]
        inv = 1.0 / diag
        diagonal[:, tile(m)] = diag
        inverse[:, tile(m)] = inv
        wi[0, :, tile(m)] = jnp.where(k == 0, 0.0, w[0])
        wi[1, :, tile(m)] = jnp.where(k == 15, 0.0, w[1])
        wi[2, :, tile(m)] = jnp.where(ends_j, 0.0, w[2]) if h == 0 else w[2]
        wi[3, :, tile(m)] = jnp.where(ends_j, 0.0, w[3]) if h == 1 else w[3]
        wi[4, :, tile(m)] = w[4]
        gk[:, tile(m)] = jnp.where(k == 0, w[0], jnp.where(k == 15, w[1], 0.0))
        gj[:, tile(m)] = jnp.where(ends_j, w[2 + h], 0.0)
        if i == 0:
            gi[:, tile(h)] = w[4]
        if i == EDGE - 1:
            gi[:, tile(2 + h)] = w[5]
        scale = inv * (1.0 / THETA)
        for c in range(3):
            f = forcing[c, :, tile(m)]
            s = f * scale
            state[R + c, :, tile(m)] = f
            state[S + c, :, tile(m)] = s
            start[c].append(s)
    for c in range(3):
        emit_channel(c, start[c], chosen, table, mine, other, first, second, lane, members, cap)


def merge_kernel(mine, got, *pairs):
    for n, pair in enumerate(pairs):
        pair[0, :, :] = mine[n + 1, :, :]
        pair[1, :, :] = got[n + 1, :, :]


def add_kernel(mine, got, total):
    total[...] = mine[...] + got[...]


def inside_kernel(first_step, lifted, final, members, *refs):
    refs = list(refs)
    state, wi, diagonal = refs[:3]
    refs = refs[3:]
    lane = lane_id()
    lift, fixed = None, {}
    x = None if first_step else refs.pop(0)
    if lifted:
        lift = refs.pop(0)
        fixed = lift_inside(members, refs[0], refs[1], state, *refs[2:5])
        refs = refs[5:]
    out, new_x = refs[:2]
    if final:
        staged, sems = refs[2:]
    g = lane >> 4
    copies = []

    def get(row, m):
        return fixed[row, m] if (row, m) in fixed else state[row, :, tile(m)]

    for c in range(3):
        up = lift[c * BLK : (c + 1) * BLK, :] if lifted else None
        for m in range(TILES):
            i, h = divmod(m, 2)
            s = get(S + c, m)
            n2, n3 = roll(s, 16), roll(s, -16)
            if h == 1:
                n2 = jnp.where(g == 0, roll(get(S + c, m - 1), 16), n2)
            else:
                n3 = jnp.where(g == 7, roll(get(S + c, m + 1), -16), n3)
            acc = get(R + c, m) - diagonal[:, tile(m)] * s
            acc = acc + wi[0, :, tile(m)] * roll(s, 1)
            acc = acc + wi[1, :, tile(m)] * roll(s, -1)
            acc = acc + wi[2, :, tile(m)] * n2
            acc = acc + wi[3, :, tile(m)] * n3
            if i > 0:
                acc = acc + wi[4, :, tile(m)] * get(S + c, m - 2)
            if i < EDGE - 1:
                acc = acc + wi[4, :, tile(m + 2)] * get(S + c, m + 2)
            out[R + c, :, tile(m)] = acc
            total = s if first_step else x[c, :, tile(m)] + s
            if lifted:
                total = total + up
            if final:
                staged[c, :, tile(m)] = total
            else:
                new_x[c, :, tile(m)] = total
        if final:
            copies.append(pltpu.make_async_copy(staged.at[c], new_x.at[c], sems.at[c]))
            copies[c].start()
    for row in range(S, S + 3):
        for m in range(TILES):
            out[row, :, tile(m)] = get(row, m)
    for copy in copies:
        copy.wait()


def add_side(c, m, value, ghost, gk, gj, lane):
    pair = slice(2 * c, 2 * c + 2)
    value = value + gk[:, tile(m)] * unpack_k(ghost[0][pair], ghost[1][pair], lane, m)
    return value + gj[:, tile(m)] * unpack_j(ghost[2][pair], ghost[3][pair], m)


def add_ends(c, m, value, ghost, gi):
    i, h = divmod(m, 2)
    if i == 0:
        value = value + gi[:, tile(h)] * ghost[4][2 * c + h]
    if i == EDGE - 1:
        value = value + gi[:, tile(2 + h)] * ghost[5][2 * c + h]
    return value


def side_kernel(members, cap, near, state, gk, gj, tables, out, ghosts):
    lane = lane_id()
    ghost = step_ghosts(members, cap, near, None, None, Table(tables), ghosts, lane, None, range(4))
    for c in range(3):
        for batch in BATCHES:
            done = [(m, add_side(c, m, state[R + c, :, tile(m)], ghost, gk, gj, lane)) for m in batch]
            for m, r in done:
                out[R + c, :, tile(m)] = r
    out[S : S + 3, :, :] = state[S : S + 3, :, :]


def outside_kernel(
    members, cap, old, new, from_first, from_second, state, inverse, gi, tables, chosen, x, *refs,
):
    out, mine, other, first, second, same_x, ghosts = refs[-7:]
    lane = lane_id()
    table = Table(tables)
    lifted = len(refs) > 7
    if lifted:
        near, (unknowns, gk, gj) = refs[:-10], refs[-10:-7]
        amend = lift_outside(members, cap, near, from_first, from_second, unknowns, tables)
        ghost = step_ghosts(members, cap, near, from_first, from_second, table, ghosts, lane, amend)
    else:
        ghost = step_ghosts(members, cap, None, from_first, from_second, table, ghosts, lane, None, (4, 5))
    for c in range(3):
        values = []
        for batch in BATCHES:
            done = []
            for m in batch:
                r = add_ends(c, m, state[R + c, :, tile(m)], ghost, gi)
                if lifted:
                    r = add_side(c, m, r, ghost, gk, gj, lane)
                done.append((m, r, old * state[S + c, :, tile(m)] + new * (r * inverse[:, tile(m)])))
            for m, r, s in done:
                out[R + c, :, tile(m)] = r
                out[S + c, :, tile(m)] = s
                values.append(s)
        emit_channel(c, values, chosen, table, mine, other, first, second, lane, members, cap)


def last_kernel(
    members, cap, near, from_first, from_second, state, gk, gj, gi, tables, residual, ghosts, staged, sems,
):
    lane = lane_id()
    ghost = step_ghosts(members, cap, near, from_first, from_second, Table(tables), ghosts, lane)
    copies = []
    for c in range(3):
        for m in range(TILES):
            r = add_ends(c, m, state[R + c, :, tile(m)], ghost, gi)
            staged[c, :, tile(m)] = add_side(c, m, r, ghost, gk, gj, lane)
        copies.append(pltpu.make_async_copy(staged.at[c], residual.at[c], sems.at[c]))
        copies[c].start()
    for copy in copies:
        copy.wait()


def coarse_kernel(
    members, cap, from_first, from_second, state, gi, tables, coarse, x,
    out_state, payload, same_x, ghosts,
):
    lane, sub = lane_id(), sub_id()
    ghost = step_ghosts(members, cap, None, from_first, from_second, Table(tables), ghosts, lane, None, (4, 5))
    placed = jnp.zeros((BLK, LANES), F32)
    for c in range(3):
        sums = [None] * 4
        for batch in BATCHES:
            done = [(m, add_ends(c, m, state[R + c, :, tile(m)], ghost, gi)) for m in batch]
            for m, r in done:
                out_state[R + c, :, tile(m)] = r
                sums[m % 4] = r if sums[m % 4] is None else sums[m % 4] + r
        total = splat(lane_sum((sums[0] + sums[1]) + (sums[2] + sums[3])))
        placed = jnp.where(lane == 3 * sub + c, total, placed)
    own = jnp.sum(placed, axis=0, keepdims=True) * (1.0 / math.sqrt(CELLS))
    own = jnp.broadcast_to(own, (BLK, LANES))
    columns = BLK * 3
    wide = -(-members * columns // LANES)
    rows = [jnp.zeros((BLK, LANES), F32) for _ in range(wide)]
    for n in range(members):
        for v in range(3):
            have = jnp.where(lane < columns, roll(coarse[n, :, :], -v * columns), 0.0)
            part = splat(lane_sum(have * own))
            place = n * columns + v * BLK
            for t in range(place // LANES, (place + BLK - 1) // LANES + 1):
                rows[t] = jnp.where(lane + t * LANES == place + sub, part, rows[t])
    out = jnp.zeros((BLK, LANES), F32)
    for t in range(wide):
        out = jnp.where(sub == t, jnp.sum(rows[t], axis=0, keepdims=True), out)
    payload[...] = out


def lift_kernel(
    members, cap, parts, state, eff, inverse, gk, gj, gi, tables, chosen, x,
    out, lift, unknowns, mine, other, first, second, same_x,
):
    lane, sub = lane_id(), sub_id()
    k, g = lane & 15, lane >> 4
    table = Table(tables)
    wide = -(-members * BLK * 3 // LANES)
    member = lax.axis_index("mem")
    total = parts[0][...]
    for part in parts[1:]:
        total = total + part[...]
    unknowns[...] = total
    known = rows_of(total, wide)
    own = look_up(known, member * BLK + sub, lane)
    side = [look_up(known, table(Table.OWNER + d) * BLK + table(Table.BLOCK + d), lane) for d in range(4)]
    for c in range(3):
        values = []
        lift[c * BLK : (c + 1) * BLK, :] = own[c]
        drop_k = own[c] - jnp.where(k == 0, side[0][c], side[1][c])
        drop_j = [own[c] - side[2][c], own[c] - side[3][c]]
        for batch in BATCHES:
            done = []
            for m in batch:
                i, h = divmod(m, 2)
                applied = (MASS_TERM * eff[:, tile(m)]) * own[c]
                applied = applied + gk[:, tile(m)] * drop_k + gj[:, tile(m)] * drop_j[h]
                if i == 0:
                    applied = applied + gi[:, tile(h)] * own[c]
                if i == EDGE - 1:
                    applied = applied + gi[:, tile(2 + h)] * own[c]
                r = state[R + c, :, tile(m)] - applied
                done.append((m, r, r * (inverse[:, tile(m)] * (1.0 / THETA))))
            for m, r, s in done:
                out[R + c, :, tile(m)] = r
                out[S + c, :, tile(m)] = s
                values.append(s)
        emit_channel(c, values, chosen, table, mine, other, first, second, lane, members, cap)

    ends = end_weights(inverse, gi)
    planes = [table(Table.PLANE + d).astype(F32) for d in range(2)]
    emit_planes(ends[:2] + planes[:1], ends[2:] + planes[1:], table(Table.EVEN) == 1, 6, first, second)
    for ref in (first, second):
        ref[9 * BLK : 10 * BLK, :] = total
    edges = []
    for f in range(2):
        v = jnp.zeros((BLK, LANES), F32)
        for t, end in zip((0, 1, 14, 15), ends):
            v = jnp.where(k == t, roll(end, t - 15 * f), v)
        edges.append(v)
    edges.append(jnp.where(g == 0, ends[0], jnp.where(g == 7, roll(ends[2], 112), 0.0)))
    edges.append(jnp.where(g == 0, roll(ends[1], 16), jnp.where(g == 7, ends[3], 0.0)))
    edges = [jnp.where(lane == 18, planes[0], jnp.where(lane == 19, planes[1], v)) for v in edges]
    for m in range(members):
        want = chosen[m * BLK : (m + 1) * BLK, :]
        face, block = want >> 3, want & 7
        v = None
        for f in range(4):
            found = pick(edges[f], block)
            v = found if f == 0 else jnp.where(face == f, found, v)
        (mine, other)[m % 2][m // 2, 6 * cap : 6 * cap + BLK, :] = v


def end_weights(inverse, gi):
    return [
        gi[:, tile(n)] * (inverse[:, tile(m)] * (1.0 / THETA)) for n, m in enumerate((0, 1, TILES - 2, TILES - 1))
    ]


def lift_inside(members, from_first, from_second, state, inverse, gi, tables):
    lane = lane_id()
    table = Table(tables)
    wide = -(-members * BLK * 3 // LANES)
    member = lax.axis_index("mem")
    ends = end_weights(inverse, gi)
    fixed = {}
    for upper in range(2):
        rows = rows_of(from_side(from_first, from_second, table, 9, upper == 1), wide)
        beyond = look_up(rows, member * BLK + table(Table.PLANE + upper), lane)
        for c in range(3):
            for h in range(2):
                n, m = 2 * upper + h, upper * (TILES - 2) + h
                fixed[R + c, m] = state[R + c, :, tile(m)] + gi[:, tile(n)] * beyond[c]
                fixed[S + c, m] = state[S + c, :, tile(m)] + ends[n] * beyond[c]
    return fixed


def lift_outside(members, cap, near, from_first, from_second, unknowns, tables):
    lane = lane_id()
    k, g = lane & 15, lane >> 4
    table = Table(tables)
    wide = -(-members * BLK * 3 // LANES)
    member = lax.axis_index("mem")
    below, above = [
        rows_of(from_side(from_first, from_second, table, 9, upper), wide) for upper in (False, True)
    ]
    known = rows_of(unknowns[...], wide)
    parts = []
    for d in range(4):
        v = None
        for m in range(members):
            found = pick(sent_by(near, m, slice(6 * cap, 6 * cap + BLK)), table(Table.SLOT + d))
            v = found if m == 0 else jnp.where(table(Table.APART + d) == m, found, v)
        base = table(Table.OWNER + d) * BLK
        low = look_up(below, base + splat(v[:, 18:19]).astype(jnp.int32), lane)
        high = look_up(above, base + splat(v[:, 19:20]).astype(jnp.int32), lane)
        at_low, at_high = (k < 2, k > 13) if d < 2 else (g == 0, g == 7)
        weights = [jnp.where(at_low, v, 0.0), jnp.where(at_high, v, 0.0)]
        parts.append([weights[n % 2] * (low, high)[n % 2][n // 2] for n in range(6)])
    for upper in (False, True):
        index = from_side(from_first, from_second, table, 8, upper).astype(jnp.int32)
        own = look_up(known, member * BLK + index, lane)
        weights = [from_side(from_first, from_second, table, 6 + p, upper) for p in range(2)]
        parts.append([weights[n % 2] * own[n // 2] for n in range(6)])
    return lambda d, n, v: v + parts[d][n]


def local(
    forcing, viscosity, refinement, face_owner, face_block, plane_block, hanging, coarse_solver
):
    groups, members = lax.axis_size("grp"), lax.axis_size("mem")
    cap = 8 * BLK // members
    field = jax.ShapeDtypeStruct(forcing.shape, F32)
    scalar_field = jax.ShapeDtypeStruct(viscosity.shape, F32)
    states = jax.ShapeDtypeStruct((6, BLK, CELLS), F32)

    def array(*shape):
        return jax.ShapeDtypeStruct(shape, F32)

    def ints(*shape):
        return jax.ShapeDtypeStruct(shape, jnp.int32)

    def scratch(*shape):
        return pltpu.VMEM(shape, F32)

    def call(body, in_specs, out_shape, out_specs, scratch_shapes, name, aliases=None, moved=2_000_000):
        return pl.pallas_call(
            body,
            out_shape=out_shape,
            in_specs=in_specs,
            out_specs=out_specs,
            scratch_shapes=scratch_shapes,
            compiler_params=PARAMS,
            input_output_aliases=aliases or {},
            cost_estimate=pl.CostEstimate(flops=2_000_000, bytes_accessed=moved, transcendentals=0),
            name=name,
        )

    first_route = [(q * members + m, (q ^ 1) * members + m) for q in range(groups) for m in range(members)]
    second_route = []
    for q in range(groups):
        for m in range(members):
            if q == 0 or q == groups - 1:
                second_route.append((q * members + m, q * members + (m ^ 1)))
            else:
                second_route.append((q * members + m, (q + 1 if q % 2 else q - 1) * members + m))

    def swap(a, bits):
        return lax.ppermute(a, "mem", [(m, m ^ bits) for m in range(members)])

    def spread(mine, other, first, second):
        first = lax.ppermute(first, ("grp", "mem"), first_route)
        second = lax.ppermute(second, ("grp", "mem"), second_route)
        got = swap(other, 1)
        pairs = members // 2 - 1
        sent = call(
            merge_kernel, [VMEM] * 2, [array(2, *mine.shape[1:])] * pairs, [VMEM] * pairs, [], "merge", moved=200_000
        )(mine, got)
        return [mine, got] + [swap(a, 2 * n + 2) for n, a in enumerate(sent)], first, second

    per = 9 * BLK
    half = array(members // 2, per, LANES)
    solver_rows = jnp.pad(coarse_solver[0], ((0, 0), (0, -coarse_solver.shape[2] % LANES)))
    eff = viscosity * jnp.exp2(-refinement.astype(F32))[:, None]
    mine, other, first, second, tables = call(
        functools.partial(prepare_kernel, members, groups, cap),
        [VMEM] + [HBM] * 4 + [VMEM],
        [half, half, array(16, LANES), array(16, LANES), ints(Table.SIZE * BLK, LANES)],
        [VMEM] * 5,
        [
            pltpu.VMEM((1, 4 * BLK), jnp.int32), pltpu.VMEM((4, BLK), jnp.int32),
            pltpu.VMEM((2, BLK), jnp.int32), pltpu.VMEM((BLK, 6), jnp.int32), scratch(members, BLK, LANES),
            pltpu.SemaphoreType.DMA((4,)),
        ],
        "prepare",
        moved=0,
    )(eff, face_owner.T, face_block.T, plane_block.T, hanging, solver_rows)
    near, from_first, from_second = spread(mine, other, first, second)

    half = array(members // 2, 6 * cap, LANES)
    sent_out = [half, half, array(48, LANES), array(48, LANES)]
    near_refs = members // 2 + 1
    ghost_scratch = [scratch(3, 6 * 48, LANES)]

    def gathered(body, *fixed):
        return lambda *refs: body(*fixed, refs[:near_refs], *refs[near_refs:])

    state, mine, other, first, second, wi, gk, gj, gi, diagonal, inverse, chosen, coarse = call(
        gathered(weights_kernel, members, cap),
        [VMEM] * (near_refs + 5),
        [states] + sent_out
        + [array(5, BLK, CELLS), scalar_field, scalar_field, array(BLK, 4 * LANES), scalar_field, scalar_field]
        + [ints(members * BLK, LANES), array(members, BLK, LANES)],
        [VMEM] * 13,
        [scratch(3, 6 * 16, LANES)],
        "weights",
    )(*near, from_first, from_second, eff, forcing, tables)

    field_scratch = [scratch(3, BLK, CELLS), pltpu.SemaphoreType.DMA((3,))]

    def inside(state, x=None, lift=(), final=False):
        operands = [state, wi, diagonal] + ([] if x is None else [x]) + list(lift)
        return call(
            functools.partial(inside_kernel, x is None, bool(lift), final, members),
            [VMEM] * len(operands),
            [states, field],
            [VMEM, HBM if final else VMEM],
            field_scratch * final,
            "inside",
            {0: 0} if x is None or final else {0: 0, 3: 1},
        )(*operands)

    def side(near, state):
        return call(
            gathered(side_kernel, members, cap),
            [VMEM] * (near_refs + 4),
            [states],
            [VMEM],
            ghost_scratch,
            "side",
            {near_refs: 0},
        )(*near, state, gk, gj, tables)[0]

    def outside(from_first, from_second, state, x, old, new, more=()):
        return call(
            functools.partial(outside_kernel, members, cap, old, new),
            [VMEM] * 7 + [ANY] + [VMEM] * len(more),
            [states] + sent_out + [field],
            [VMEM] * 5 + [ANY],
            ghost_scratch,
            "outside",
            {2: 0, 7: 5},
        )(from_first, from_second, state, inverse, gi, tables, chosen, x, *more)

    rho = 1.0 / SIGMA
    factors = []
    for _ in range(DEG - 1):
        rho_next = 1.0 / (2.0 * SIGMA - rho)
        factors.append((rho_next * rho, 2.0 * rho_next / DELTA))
        rho = rho_next

    def steps(state, sent, x, lift=None, unknowns=None):
        for n, (old, new) in enumerate(factors):
            near, from_first, from_second = spread(*sent)
            more = ()
            if n == 0 and lift is not None:
                state, x = inside(state, x, (lift, from_first, from_second, inverse, gi, tables))
                more = (*near, unknowns, gk, gj)
            else:
                state, x = inside(state, x)
                state = side(near, state)
            state, *sent, x = outside(from_first, from_second, state, x, old, new, more)
        return state, x, spread(*sent)

    state, x, (near, from_first, from_second) = steps(state, (mine, other, first, second), None)
    state, x = inside(state, x)
    state = side(near, state)
    state, payload, x = call(
        functools.partial(coarse_kernel, members, cap),
        [VMEM] * 6 + [ANY],
        [states, array(BLK, LANES), field],
        [VMEM, VMEM, ANY],
        ghost_scratch,
        "coarse",
        {2: 0, 6: 2},
    )(from_first, from_second, state, gi, tables, coarse, x)
    pair = call(add_kernel, [VMEM] * 2, [array(BLK, LANES)], [VMEM], [], "add")(payload, swap(payload, 1))[0]
    parts = [pair] + [swap(pair, 2 * n) for n in range(1, members // 2)]
    half = array(members // 2, 6 * cap + BLK, LANES)
    state, lift, unknowns, *sent, x = call(
        lambda *refs: lift_kernel(members, cap, refs[: len(parts)], *refs[len(parts) :]),
        [VMEM] * (len(parts) + 8) + [ANY],
        [states, array(3 * BLK, LANES), array(BLK, LANES), half, half, array(80, LANES), array(80, LANES), field],
        [VMEM] * 7 + [ANY],
        [],
        "lift",
        {len(parts): 0, len(parts) + 8: 7},
    )(*parts, state, eff, inverse, gk, gj, gi, tables, chosen, x)
    state, x, (near, from_first, from_second) = steps(state, sent, x, lift, unknowns)
    state, velocity = inside(state, x, final=True)
    residual = call(
        gathered(last_kernel, members, cap),
        [VMEM] * (near_refs + 7),
        [field],
        [HBM],
        ghost_scratch + field_scratch,
        "last",
    )(*near, from_first, from_second, state, gk, gj, gi, tables)[0]
    return velocity, residual


def solution(mesh):
    in_specs = (
        P(None, ("grp", "mem"), None),
        P(("grp", "mem"), None),
        P(("grp", "mem")),
        P(("grp", "mem"), None),
        P(("grp", "mem"), None),
        P(("grp", "mem"), None),
        P(("grp", "mem"), None),
        P("grp", "mem", None),
    )
    out_specs = (P(None, ("grp", "mem"), None), P(None, ("grp", "mem"), None))
    return jax.shard_map(local, mesh=mesh, in_specs=in_specs, out_specs=out_specs, check_vma=False)
```

```python
import functools
import math

import jax
import jax.numpy as jnp
from jax import lax
from jax.experimental import pallas as pl
from jax.experimental.pallas import tpu as pltpu
from jax.sharding import PartitionSpec as P

EDGE = 16
DEG = 3
CELLS = 4096
MASS_TERM = 1.0
LOWER_BOUND = 0.25
UPPER_BOUND = 2.0
THETA = 0.5 * (UPPER_BOUND + LOWER_BOUND)
DELTA = 0.5 * (UPPER_BOUND - LOWER_BOUND)
SIGMA = THETA / DELTA

LANES = 128
BLK = 8
TILES = CELLS // LANES
BATCHES = [range(m, m + 8) for m in range(0, TILES, 8)]
F32 = jnp.float32
R, S = 0, 3
VMEM = pl.BlockSpec(memory_space=pltpu.VMEM)
ANY = pl.BlockSpec(memory_space=pl.ANY)
HBM = pl.BlockSpec(memory_space=pltpu.HBM)
PARAMS = pltpu.CompilerParams(vmem_limit_bytes=8 * 1024 * 1024)


def lane_id():
    return lax.broadcasted_iota(jnp.int32, (BLK, LANES), 1)


def sub_id():
    return lax.broadcasted_iota(jnp.int32, (BLK, LANES), 0)


def roll(v, shift):
    shift = shift % LANES
    return v if shift == 0 else pltpu.roll(v, shift, 1)


def tile(m):
    return slice(m * LANES, (m + 1) * LANES)


def pack_faces(values, lane):
    k, g = lane & 15, lane >> 4
    faces = [[], [], [], []]
    for p in range(2):
        low = high = None
        for t in range(16):
            moved = roll(values[16 * p + t], t)
            low = moved if t == 0 else jnp.where(k == t, moved, low)
            high = moved if t == 0 else jnp.where(k == (15 + t) % 16, moved, high)
        faces[0].append(low)
        faces[1].append(roll(high, -15))
        low = high = None
        for t in range(8):
            i = 8 * p + t
            first = roll(values[2 * i], 16 * t)
            last = roll(values[2 * i + 1], 16 * t + 16)
            low = first if t == 0 else jnp.where(g == t, first, low)
            high = last if t == 0 else jnp.where(g == t, last, high)
        faces[2].append(low)
        faces[3].append(high)
    return faces


def unpack_k(low, high, lane, m):
    t = m % 16
    return jnp.where((lane & 15) == 0, roll(low[m // 16], -t), roll(high[m // 16], 15 - t))


def unpack_j(low, high, m):
    i = m // 2
    if m % 2 == 0:
        return roll(low[i // 8], -16 * (i % 8))
    return roll(high[i // 8], 112 - 16 * (i % 8))


def pick(values, index):
    return jnp.take_along_axis(values, index, axis=0, mode="promise_in_bounds")


def lane_sum(v):
    return jnp.sum(v, axis=1, keepdims=True)


def splat(column):
    return jnp.broadcast_to(column, (BLK, LANES))


class Table:
    OWNER, SLOT, BLOCK, PLANE, EVEN, LOWER, UPPER, HANG, APART = 0, 4, 8, 12, 14, 15, 16, 17, 23
    SIZE = 27

    def __init__(self, ref):
        self.ref = ref

    def __call__(self, n):
        return self.ref[n * BLK : (n + 1) * BLK, :]


def gather_ghosts(near_tile, members, who, first, second, table, ghosts, lane, rows, amend=None, faces=range(6)):
    even = table(Table.EVEN) == 1
    for d in faces:
        for n in range(rows):
            if d < 4:
                v = None
                for m in range(members):
                    source, index = near_tile(m, d, n)
                    found = pick(source, index)
                    v = found if m == 0 else jnp.where(table(who + d) == m, found, v)
                if amend:
                    v = amend(d, n, v)
            else:
                a, b = first[n * BLK : (n + 1) * BLK, :], second[n * BLK : (n + 1) * BLK, :]
                v = jnp.where(even, b, a) if d == 4 else jnp.where(even, a, b)
                if amend:
                    v = amend(d, n, v)
                inside = table(Table.LOWER if d == 4 else Table.UPPER) == 1
                v = jnp.where(inside, pick(v, table(Table.PLANE + d - 4)), 0.0)
            at = (d * rows + n) * BLK
            ghosts[0, at : at + BLK, :] = v
    for stage in range(2):
        for d in faces:
            bit = 16 if stage else (2 if d < 2 else 1)
            low = (lane & bit) == 0
            for n in range(rows):
                at = (d * rows + n) * BLK
                v = ghosts[stage, at : at + BLK, :]
                ghosts[stage + 1, at : at + BLK, :] = v + jnp.where(low, roll(v, -bit), roll(v, bit))
    result = {}
    for d in faces:
        hang = table(Table.HANG + d) == 1
        tiles = []
        for n in range(rows):
            at = (d * rows + n) * BLK
            tiles.append(jnp.where(hang, ghosts[2, at : at + BLK, :] * 0.25, ghosts[0, at : at + BLK, :]))
        result[d] = tiles
    return result


def sent_by(near, apart, rows):
    pair, bit = divmod(apart, 2)
    return near[bit][0, rows, :] if pair == 0 else near[1 + pair][bit, rows, :]


def step_ghosts(members, cap, near, first, second, table, ghosts, lane, amend=None, faces=range(6)):
    def near_tile(m, d, n):
        start = n * cap
        at = start // BLK * BLK
        return sent_by(near, m, slice(at, at + BLK)), table(Table.SLOT + d) + (start - at)

    return gather_ghosts(near_tile, members, Table.APART, first, second, table, ghosts, lane, 6, amend, faces)


def look_up(rows, block, lane):
    found = []
    for c in range(3):
        total = jnp.zeros((BLK, LANES), F32)
        for t, values in enumerate(rows):
            total = total + jnp.where(lane + t * LANES == 3 * block + c, values, 0.0)
        found.append(splat(lane_sum(total)))
    return found


def rows_of(v, wide):
    return [jnp.broadcast_to(v[t : t + 1, :], (BLK, LANES)) for t in range(wide)]


def from_side(first, second, table, n, upper):
    a, b = first[n * BLK : (n + 1) * BLK, :], second[n * BLK : (n + 1) * BLK, :]
    even = table(Table.EVEN) == 1
    v = jnp.where(even, a, b) if upper else jnp.where(even, b, a)
    return jnp.where(table(Table.UPPER if upper else Table.LOWER) == 1, v, 0.0)


def emit_planes(low, high, even, at, first, second):
    for n in range(len(low)):
        span = slice((at + n) * BLK, (at + n + 1) * BLK)
        first[span, :] = jnp.where(even, high[n], low[n])
        second[span, :] = jnp.where(even, low[n], high[n])


def emit_channel(c, values, chosen, table, mine, other, first, second, lane, members, cap):
    packed = pack_faces(values, lane)
    emit_planes(values[:2], values[-2:], table(Table.EVEN) == 1, 2 * c, first, second)
    sub = sub_id()
    for m in range(members):
        want = chosen[m * BLK : (m + 1) * BLK, :]
        face, block = want >> 3, want & 7
        for u in range(2 * cap // BLK):
            out = None
            for p in range(2):
                if not u * BLK <= p * cap < (u + 1) * BLK:
                    continue
                v = None
                for f in range(4):
                    found = pick(packed[f][p], block)
                    v = found if f == 0 else jnp.where(face == f, found, v)
                out = v if out is None else jnp.where(sub < p * cap - u * BLK, out, v)
            at = c * 2 * cap + u * BLK
            (mine, other)[m % 2][m // 2, at : at + BLK, :] = out


def prepare_kernel(
    members, groups, cap, eff, owner_hbm, block_hbm, plane_hbm, hanging_hbm, coarse_rows,
    mine, other, first, second, tables,
    face_owner, face_block, plane_block, hanging, special, sems,
):
    copies = [
        pltpu.make_async_copy(source, target, sems.at[n])
        for n, (source, target) in enumerate(
            [
                (owner_hbm, face_owner), (block_hbm, face_block), (plane_hbm, plane_block), (hanging_hbm, hanging),
            ]
        )
    ]
    for copy in copies:
        copy.start()
    lane, sub = lane_id(), sub_id()
    group, member = lax.axis_index("grp"), lax.axis_index("mem")
    even = group % 2 == 0
    for copy in copies:
        copy.wait()

    def iotas(width):
        return (
            lax.broadcasted_iota(jnp.int32, (BLK, width), 1), lax.broadcasted_iota(jnp.int32, (BLK, width), 0)
        )

    lane8, sub8 = iotas(BLK)
    lane32, sub32 = iotas(4 * BLK)
    lane64, sub64 = iotas(members * cap)

    def column(row):
        wide = jnp.broadcast_to(row.astype(F32), (BLK, BLK))
        return lane_sum(jnp.where(lane8 == sub8, wide, 0.0))

    def put(n, value):
        tables[n * BLK : (n + 1) * BLK, :] = splat(value).astype(jnp.int32)

    values = [eff[:, tile(m)] for m in range(TILES)]
    packed = pack_faces(values, lane)
    emit_planes(values[:2], values[-2:], even, 0, first, second)

    row = jnp.broadcast_to(face_owner[...].astype(F32), (BLK, 4 * BLK))
    wanted = jnp.zeros((BLK, members * cap), F32)
    for d in range(4):
        place = 4 * sub32 + d
        owner = lane_sum(jnp.where(lane32 == place, row, 0.0))
        slot = lane_sum(jnp.where((lane32 < place) & (row == owner), 1.0, 0.0))
        block = column(face_block[d : d + 1, :])
        put(Table.OWNER + d, owner)
        at = (Table.APART + d) * BLK
        tables[at : at + BLK, :] = splat(owner).astype(jnp.int32) ^ jnp.full((BLK, LANES), member, jnp.int32)
        put(Table.SLOT + d, slot)
        put(Table.BLOCK + d, block)
        target = jnp.broadcast_to(owner * cap + slot, (BLK, members * cap))
        want = jnp.broadcast_to(block + (d ^ 1) * BLK, (BLK, members * cap))
        wanted = wanted + jnp.where(lane64.astype(F32) == target, want, 0.0)
    wanted = jnp.broadcast_to(jnp.sum(wanted, axis=0, keepdims=True), (BLK, members * cap))
    for d in range(2):
        put(Table.PLANE + d, column(plane_block[d : d + 1, :]))
    for n, flag in ((Table.EVEN, even), (Table.LOWER, group > 0), (Table.UPPER, group < groups - 1)):
        tables[n * BLK : (n + 1) * BLK, :] = jnp.full((BLK, LANES), jnp.where(flag, 1, 0), jnp.int32)
    for d in range(6):
        put(Table.HANG + d, hanging[:, d : d + 1])

    def coarse_tile(rows, at):
        have = coarse_rows[rows, at * LANES : min((at + 1) * LANES, coarse_rows.shape[1])]
        missing = LANES - have.shape[1]
        return have if missing == 0 else jnp.concatenate([have, jnp.zeros((BLK, missing), F32)], axis=1)

    columns = BLK * 3
    for n in range(members):
        for f in range(4):
            for p in range(2):
                at = (f * 2 + p) * BLK
                (mine, other)[n % 2][n // 2, at : at + BLK, :] = packed[f][p]
        request = lane_sum(jnp.where(lane64 == n * cap + sub64 % cap, wanted, 0.0))
        last = splat(request)
        at, off = divmod(n * columns, LANES)
        for v in range(3):
            rows = slice(v * BLK, (v + 1) * BLK)
            part = roll(coarse_tile(rows, at), v * columns - off)
            if off + columns > LANES:
                more = roll(coarse_tile(rows, at + 1), v * columns - off)
                part = jnp.where(lane < v * columns + LANES - off, part, more)
            last = jnp.where((lane >= v * columns) & (lane < (v + 1) * columns), part, last)
        special[member ^ n, :, :] = last
    for n in range(members):
        (mine, other)[n % 2][n // 2, 8 * BLK : 9 * BLK, :] = special[n, :, :]


def weights_kernel(
    members, cap, near, from_first, from_second, eff, forcing, tables,
    state, mine, other, first, second, wi, gk, gj, gi, diagonal, inverse, chosen, coarse, ghosts,
):
    lane = lane_id()
    k, g = lane & 15, lane >> 4
    table = Table(tables)
    for n in range(members):
        last = sent_by(near, n, slice(8 * BLK, 9 * BLK))
        chosen[n * BLK : (n + 1) * BLK, :] = splat(last[:, LANES - 1 :]).astype(jnp.int32)
        coarse[lax.axis_index("mem") ^ n, :, :] = last

    def near_tile(m, d, n):
        at = ((d ^ 1) * 2 + n) * BLK
        return sent_by(near, m, slice(at, at + BLK)), table(Table.BLOCK + d)

    ghost = gather_ghosts(near_tile, members, Table.APART, from_first, from_second, table, ghosts, lane, 2)
    values = [eff[:, tile(m)] for m in range(TILES)]
    start = [[], [], []]
    for m in range(TILES):
        i, h = divmod(m, 2)
        e = values[m]
        side_k = unpack_k(ghost[0], ghost[1], lane, m)
        side_j = unpack_j(ghost[2], ghost[3], m)
        ends_j = (g == 0) if h == 0 else (g == 7)
        n0 = jnp.where(k == 0, side_k, roll(e, 1))
        n1 = jnp.where(k == 15, side_k, roll(e, -1))
        n2 = jnp.where(g == 0, side_j if h == 0 else roll(values[m - 1], 16), roll(e, 16))
        n3 = jnp.where(g == 7, side_j if h == 1 else roll(values[m + 1], -16), roll(e, -16))
        n4 = ghost[4][h] if i == 0 else values[m - 2]
        n5 = ghost[5][h] if i == EDGE - 1 else values[m + 2]
        w = [0.5 * (e + n) for n in (n0, n1, n2, n3, n4, n5)]
        diag = MASS_TERM * e
        for d in range(6):
            diag = diag + w[d]
        inv = 1.0 / diag
        diagonal[:, tile(m)] = diag
        inverse[:, tile(m)] = inv
        wi[0, :, tile(m)] = jnp.where(k == 0, 0.0, w[0])
        wi[1, :, tile(m)] = jnp.where(k == 15, 0.0, w[1])
        wi[2, :, tile(m)] = jnp.where(ends_j, 0.0, w[2]) if h == 0 else w[2]
        wi[3, :, tile(m)] = jnp.where(ends_j, 0.0, w[3]) if h == 1 else w[3]
        wi[4, :, tile(m)] = w[4]
        gk[:, tile(m)] = jnp.where(k == 0, w[0], jnp.where(k == 15, w[1], 0.0))
        gj[:, tile(m)] = jnp.where(ends_j, w[2 + h], 0.0)
        if i == 0:
            gi[:, tile(h)] = w[4]
        if i == EDGE - 1:
            gi[:, tile(2 + h)] = w[5]
        scale = inv * (1.0 / THETA)
        for c in range(3):
            f = forcing[c, :, tile(m)]
            s = f * scale
            state[R + c, :, tile(m)] = f
            state[S + c, :, tile(m)] = s
            start[c].append(s)
    for c in range(3):
        emit_channel(c, start[c], chosen, table, mine, other, first, second, lane, members, cap)


def merge_kernel(mine, got, *pairs):
    for n, pair in enumerate(pairs):
        pair[0, :, :] = mine[n + 1, :, :]
        pair[1, :, :] = got[n + 1, :, :]


def add_kernel(mine, got, total):
    total[...] = mine[...] + got[...]


def inside_kernel(first_step, lifted, final, members, *refs):
    refs = list(refs)
    state, wi, diagonal = refs[:3]
    refs = refs[3:]
    lane = lane_id()
    lift, fixed = None, {}
    x = None if first_step else refs.pop(0)
    if lifted:
        lift = refs.pop(0)
        fixed = lift_inside(members, refs[0], refs[1], state, *refs[2:5])
        refs = refs[5:]
    out, new_x = refs[:2]
    if final:
        staged, sems = refs[2:]
    g = lane >> 4
    copies = []

    def get(row, m):
        return fixed[row, m] if (row, m) in fixed else state[row, :, tile(m)]

    for c in range(3):
        up = lift[c * BLK : (c + 1) * BLK, :] if lifted else None
        for m in range(TILES):
            i, h = divmod(m, 2)
            s = get(S + c, m)
            n2, n3 = roll(s, 16), roll(s, -16)
            if h == 1:
                n2 = jnp.where(g == 0, roll(get(S + c, m - 1), 16), n2)
            else:
                n3 = jnp.where(g == 7, roll(get(S + c, m + 1), -16), n3)
            acc = get(R + c, m) - diagonal[:, tile(m)] * s
            acc = acc + wi[0, :, tile(m)] * roll(s, 1)
            acc = acc + wi[1, :, tile(m)] * roll(s, -1)
            acc = acc + wi[2, :, tile(m)] * n2
            acc = acc + wi[3, :, tile(m)] * n3
            if i > 0:
                acc = acc + wi[4, :, tile(m)] * get(S + c, m - 2)
            if i < EDGE - 1:
                acc = acc + wi[4, :, tile(m + 2)] * get(S + c, m + 2)
            out[R + c, :, tile(m)] = acc
            total = s if first_step else x[c, :, tile(m)] + s
            if lifted:
                total = total + up
            if final:
                staged[c, :, tile(m)] = total
            else:
                new_x[c, :, tile(m)] = total
        if final:
            copies.append(pltpu.make_async_copy(staged.at[c], new_x.at[c], sems.at[c]))
            copies[c].start()
    for row in range(S, S + 3):
        for m in range(TILES):
            out[row, :, tile(m)] = get(row, m)
    for copy in copies:
        copy.wait()


def add_side(c, m, value, ghost, gk, gj, lane):
    pair = slice(2 * c, 2 * c + 2)
    value = value + gk[:, tile(m)] * unpack_k(ghost[0][pair], ghost[1][pair], lane, m)
    return value + gj[:, tile(m)] * unpack_j(ghost[2][pair], ghost[3][pair], m)


def add_ends(c, m, value, ghost, gi):
    i, h = divmod(m, 2)
    if i == 0:
        value = value + gi[:, tile(h)] * ghost[4][2 * c + h]
    if i == EDGE - 1:
        value = value + gi[:, tile(2 + h)] * ghost[5][2 * c + h]
    return value


def side_kernel(members, cap, near, state, gk, gj, tables, out, ghosts):
    lane = lane_id()
    ghost = step_ghosts(members, cap, near, None, None, Table(tables), ghosts, lane, None, range(4))
    for c in range(3):
        for batch in BATCHES:
            done = [(m, add_side(c, m, state[R + c, :, tile(m)], ghost, gk, gj, lane)) for m in batch]
            for m, r in done:
                out[R + c, :, tile(m)] = r
    out[S : S + 3, :, :] = state[S : S + 3, :, :]


def outside_kernel(
    members, cap, old, new, from_first, from_second, state, inverse, gi, tables, chosen, x, *refs,
):
    out, mine, other, first, second, same_x, ghosts = refs[-7:]
    lane = lane_id()
    table = Table(tables)
    lifted = len(refs) > 7
    if lifted:
        near, (unknowns, gk, gj) = refs[:-10], refs[-10:-7]
        amend = lift_outside(members, cap, near, from_first, from_second, unknowns, tables)
        ghost = step_ghosts(members, cap, near, from_first, from_second, table, ghosts, lane, amend)
    else:
        ghost = step_ghosts(members, cap, None, from_first, from_second, table, ghosts, lane, None, (4, 5))
    for c in range(3):
        values = []
        for batch in BATCHES:
            done = []
            for m in batch:
                r = add_ends(c, m, state[R + c, :, tile(m)], ghost, gi)
                if lifted:
                    r = add_side(c, m, r, ghost, gk, gj, lane)
                done.append((m, r, old * state[S + c, :, tile(m)] + new * (r * inverse[:, tile(m)])))
            for m, r, s in done:
                out[R + c, :, tile(m)] = r
                out[S + c, :, tile(m)] = s
                values.append(s)
        emit_channel(c, values, chosen, table, mine, other, first, second, lane, members, cap)


def last_kernel(
    members, cap, from_first, from_second, state, gi, tables, x, residual, velocity, ghosts, staged, sems,
):
    lane = lane_id()
    out = pltpu.make_async_copy(x, velocity, sems.at[3])
    out.start()
    ghost = step_ghosts(members, cap, None, from_first, from_second, Table(tables), ghosts, lane, None, (4, 5))
    copies = [out]
    for c in range(3):
        for m in range(TILES):
            staged[c, :, tile(m)] = add_ends(c, m, state[R + c, :, tile(m)], ghost, gi)
        copies.append(pltpu.make_async_copy(staged.at[c], residual.at[c], sems.at[c]))
        copies[-1].start()
    for copy in copies:
        copy.wait()


def coarse_kernel(
    members, cap, from_first, from_second, state, gi, tables, coarse, x,
    out_state, payload, same_x, ghosts,
):
    lane, sub = lane_id(), sub_id()
    ghost = step_ghosts(members, cap, None, from_first, from_second, Table(tables), ghosts, lane, None, (4, 5))
    placed = jnp.zeros((BLK, LANES), F32)
    for c in range(3):
        sums = [None] * 4
        for batch in BATCHES:
            done = [(m, add_ends(c, m, state[R + c, :, tile(m)], ghost, gi)) for m in batch]
            for m, r in done:
                out_state[R + c, :, tile(m)] = r
                sums[m % 4] = r if sums[m % 4] is None else sums[m % 4] + r
        total = splat(lane_sum((sums[0] + sums[1]) + (sums[2] + sums[3])))
        placed = jnp.where(lane == 3 * sub + c, total, placed)
    own = jnp.sum(placed, axis=0, keepdims=True) * (1.0 / math.sqrt(CELLS))
    own = jnp.broadcast_to(own, (BLK, LANES))
    columns = BLK * 3
    wide = -(-members * columns // LANES)
    rows = [jnp.zeros((BLK, LANES), F32) for _ in range(wide)]
    for n in range(members):
        for v in range(3):
            have = jnp.where(lane < columns, roll(coarse[n, :, :], -v * columns), 0.0)
            part = splat(lane_sum(have * own))
            place = n * columns + v * BLK
            for t in range(place // LANES, (place + BLK - 1) // LANES + 1):
                rows[t] = jnp.where(lane + t * LANES == place + sub, part, rows[t])
    out = jnp.zeros((BLK, LANES), F32)
    for t in range(wide):
        out = jnp.where(sub == t, jnp.sum(rows[t], axis=0, keepdims=True), out)
    payload[...] = out


def lift_kernel(
    members, cap, parts, state, eff, inverse, gk, gj, gi, tables, chosen, x,
    out, lift, unknowns, mine, other, first, second, same_x,
):
    lane, sub = lane_id(), sub_id()
    k, g = lane & 15, lane >> 4
    table = Table(tables)
    wide = -(-members * BLK * 3 // LANES)
    member = lax.axis_index("mem")
    total = parts[0][...]
    for part in parts[1:]:
        total = total + part[...]
    unknowns[...] = total
    known = rows_of(total, wide)
    own = look_up(known, member * BLK + sub, lane)
    side = [look_up(known, table(Table.OWNER + d) * BLK + table(Table.BLOCK + d), lane) for d in range(4)]
    for c in range(3):
        values = []
        lift[c * BLK : (c + 1) * BLK, :] = own[c]
        drop_k = own[c] - jnp.where(k == 0, side[0][c], side[1][c])
        drop_j = [own[c] - side[2][c], own[c] - side[3][c]]
        for batch in BATCHES:
            done = []
            for m in batch:
                i, h = divmod(m, 2)
                applied = (MASS_TERM * eff[:, tile(m)]) * own[c]
                applied = applied + gk[:, tile(m)] * drop_k + gj[:, tile(m)] * drop_j[h]
                if i == 0:
                    applied = applied + gi[:, tile(h)] * own[c]
                if i == EDGE - 1:
                    applied = applied + gi[:, tile(2 + h)] * own[c]
                r = state[R + c, :, tile(m)] - applied
                done.append((m, r, r * (inverse[:, tile(m)] * (1.0 / THETA))))
            for m, r, s in done:
                out[R + c, :, tile(m)] = r
                out[S + c, :, tile(m)] = s
                values.append(s)
        emit_channel(c, values, chosen, table, mine, other, first, second, lane, members, cap)

    ends = end_weights(inverse, gi)
    planes = [table(Table.PLANE + d).astype(F32) for d in range(2)]
    emit_planes(ends[:2] + planes[:1], ends[2:] + planes[1:], table(Table.EVEN) == 1, 6, first, second)
    for ref in (first, second):
        ref[9 * BLK : 10 * BLK, :] = total
    edges = []
    for f in range(2):
        v = jnp.zeros((BLK, LANES), F32)
        for t, end in zip((0, 1, 14, 15), ends):
            v = jnp.where(k == t, roll(end, t - 15 * f), v)
        edges.append(v)
    edges.append(jnp.where(g == 0, ends[0], jnp.where(g == 7, roll(ends[2], 112), 0.0)))
    edges.append(jnp.where(g == 0, roll(ends[1], 16), jnp.where(g == 7, ends[3], 0.0)))
    edges = [jnp.where(lane == 18, planes[0], jnp.where(lane == 19, planes[1], v)) for v in edges]
    for m in range(members):
        want = chosen[m * BLK : (m + 1) * BLK, :]
        face, block = want >> 3, want & 7
        v = None
        for f in range(4):
            found = pick(edges[f], block)
            v = found if f == 0 else jnp.where(face == f, found, v)
        (mine, other)[m % 2][m // 2, 6 * cap : 6 * cap + BLK, :] = v


def end_weights(inverse, gi):
    return [
        gi[:, tile(n)] * (inverse[:, tile(m)] * (1.0 / THETA)) for n, m in enumerate((0, 1, TILES - 2, TILES - 1))
    ]


def lift_inside(members, from_first, from_second, state, inverse, gi, tables):
    lane = lane_id()
    table = Table(tables)
    wide = -(-members * BLK * 3 // LANES)
    member = lax.axis_index("mem")
    ends = end_weights(inverse, gi)
    fixed = {}
    for upper in range(2):
        rows = rows_of(from_side(from_first, from_second, table, 9, upper == 1), wide)
        beyond = look_up(rows, member * BLK + table(Table.PLANE + upper), lane)
        for c in range(3):
            for h in range(2):
                n, m = 2 * upper + h, upper * (TILES - 2) + h
                fixed[R + c, m] = state[R + c, :, tile(m)] + gi[:, tile(n)] * beyond[c]
                fixed[S + c, m] = state[S + c, :, tile(m)] + ends[n] * beyond[c]
    return fixed


def lift_outside(members, cap, near, from_first, from_second, unknowns, tables):
    lane = lane_id()
    k, g = lane & 15, lane >> 4
    table = Table(tables)
    wide = -(-members * BLK * 3 // LANES)
    member = lax.axis_index("mem")
    below, above = [
        rows_of(from_side(from_first, from_second, table, 9, upper), wide) for upper in (False, True)
    ]
    known = rows_of(unknowns[...], wide)
    parts = []
    for d in range(4):
        v = None
        for m in range(members):
            found = pick(sent_by(near, m, slice(6 * cap, 6 * cap + BLK)), table(Table.SLOT + d))
            v = found if m == 0 else jnp.where(table(Table.APART + d) == m, found, v)
        base = table(Table.OWNER + d) * BLK
        low = look_up(below, base + splat(v[:, 18:19]).astype(jnp.int32), lane)
        high = look_up(above, base + splat(v[:, 19:20]).astype(jnp.int32), lane)
        at_low, at_high = (k < 2, k > 13) if d < 2 else (g == 0, g == 7)
        weights = [jnp.where(at_low, v, 0.0), jnp.where(at_high, v, 0.0)]
        parts.append([weights[n % 2] * (low, high)[n % 2][n // 2] for n in range(6)])
    for upper in (False, True):
        index = from_side(from_first, from_second, table, 8, upper).astype(jnp.int32)
        own = look_up(known, member * BLK + index, lane)
        weights = [from_side(from_first, from_second, table, 6 + p, upper) for p in range(2)]
        parts.append([weights[n % 2] * own[n // 2] for n in range(6)])
    return lambda d, n, v: v + parts[d][n]


def local(
    forcing, viscosity, refinement, face_owner, face_block, plane_block, hanging, coarse_solver
):
    groups, members = lax.axis_size("grp"), lax.axis_size("mem")
    cap = 8 * BLK // members
    field = jax.ShapeDtypeStruct(forcing.shape, F32)
    scalar_field = jax.ShapeDtypeStruct(viscosity.shape, F32)
    states = jax.ShapeDtypeStruct((6, BLK, CELLS), F32)

    def array(*shape):
        return jax.ShapeDtypeStruct(shape, F32)

    def ints(*shape):
        return jax.ShapeDtypeStruct(shape, jnp.int32)

    def scratch(*shape):
        return pltpu.VMEM(shape, F32)

    def call(body, in_specs, out_shape, out_specs, scratch_shapes, name, aliases=None, moved=2_000_000):
        return pl.pallas_call(
            body,
            out_shape=out_shape,
            in_specs=in_specs,
            out_specs=out_specs,
            scratch_shapes=scratch_shapes,
            compiler_params=PARAMS,
            input_output_aliases=aliases or {},
            cost_estimate=pl.CostEstimate(flops=2_000_000, bytes_accessed=moved, transcendentals=0),
            name=name,
        )

    first_route = [(q * members + m, (q ^ 1) * members + m) for q in range(groups) for m in range(members)]
    second_route = []
    for q in range(groups):
        for m in range(members):
            if q == 0 or q == groups - 1:
                second_route.append((q * members + m, q * members + (m ^ 1)))
            else:
                second_route.append((q * members + m, (q + 1 if q % 2 else q - 1) * members + m))

    def swap(a, bits):
        return lax.ppermute(a, "mem", [(m, m ^ bits) for m in range(members)])

    def spread(mine, other, first, second):
        first = lax.ppermute(first, ("grp", "mem"), first_route)
        second = lax.ppermute(second, ("grp", "mem"), second_route)
        got = swap(other, 1)
        pairs = members // 2 - 1
        sent = call(
            merge_kernel, [VMEM] * 2, [array(2, *mine.shape[1:])] * pairs, [VMEM] * pairs, [], "merge", moved=200_000
        )(mine, got)
        return [mine, got] + [swap(a, 2 * n + 2) for n, a in enumerate(sent)], first, second

    per = 9 * BLK
    half = array(members // 2, per, LANES)
    solver_rows = jnp.pad(coarse_solver[0], ((0, 0), (0, -coarse_solver.shape[2] % LANES)))
    eff = viscosity * jnp.exp2(-refinement.astype(F32))[:, None]
    mine, other, first, second, tables = call(
        functools.partial(prepare_kernel, members, groups, cap),
        [VMEM] + [HBM] * 4 + [VMEM],
        [half, half, array(16, LANES), array(16, LANES), ints(Table.SIZE * BLK, LANES)],
        [VMEM] * 5,
        [
            pltpu.VMEM((1, 4 * BLK), jnp.int32), pltpu.VMEM((4, BLK), jnp.int32),
            pltpu.VMEM((2, BLK), jnp.int32), pltpu.VMEM((BLK, 6), jnp.int32), scratch(members, BLK, LANES),
            pltpu.SemaphoreType.DMA((4,)),
        ],
        "prepare",
        moved=0,
    )(eff, face_owner.T, face_block.T, plane_block.T, hanging, solver_rows)
    near, from_first, from_second = spread(mine, other, first, second)

    half = array(members // 2, 6 * cap, LANES)
    sent_out = [half, half, array(48, LANES), array(48, LANES)]
    near_refs = members // 2 + 1
    ghost_scratch = [scratch(3, 6 * 48, LANES)]

    def gathered(body, *fixed):
        return lambda *refs: body(*fixed, refs[:near_refs], *refs[near_refs:])

    state, mine, other, first, second, wi, gk, gj, gi, diagonal, inverse, chosen, coarse = call(
        gathered(weights_kernel, members, cap),
        [VMEM] * (near_refs + 5),
        [states] + sent_out
        + [array(5, BLK, CELLS), scalar_field, scalar_field, array(BLK, 4 * LANES), scalar_field, scalar_field]
        + [ints(members * BLK, LANES), array(members, BLK, LANES)],
        [VMEM] * 13,
        [scratch(3, 6 * 16, LANES)],
        "weights",
    )(*near, from_first, from_second, eff, forcing, tables)

    field_scratch = [scratch(3, BLK, CELLS), pltpu.SemaphoreType.DMA((3,))]

    def inside(state, x=None, lift=(), final=False):
        operands = [state, wi, diagonal] + ([] if x is None else [x]) + list(lift)
        return call(
            functools.partial(inside_kernel, x is None, bool(lift), final, members),
            [VMEM] * len(operands),
            [states, field],
            [VMEM, HBM if final else VMEM],
            field_scratch * final,
            "inside",
            {0: 0} if x is None or final else {0: 0, 3: 1},
        )(*operands)

    def side(near, state):
        return call(
            gathered(side_kernel, members, cap),
            [VMEM] * (near_refs + 4),
            [states],
            [VMEM],
            ghost_scratch,
            "side",
            {near_refs: 0},
        )(*near, state, gk, gj, tables)[0]

    def outside(from_first, from_second, state, x, old, new, more=()):
        return call(
            functools.partial(outside_kernel, members, cap, old, new),
            [VMEM] * 7 + [ANY] + [VMEM] * len(more),
            [states] + sent_out + [field],
            [VMEM] * 5 + [ANY],
            ghost_scratch,
            "outside",
            {2: 0, 7: 5},
        )(from_first, from_second, state, inverse, gi, tables, chosen, x, *more)

    rho = 1.0 / SIGMA
    factors = []
    for _ in range(DEG - 1):
        rho_next = 1.0 / (2.0 * SIGMA - rho)
        factors.append((rho_next * rho, 2.0 * rho_next / DELTA))
        rho = rho_next

    def steps(state, sent, x, lift=None, unknowns=None):
        for n, (old, new) in enumerate(factors):
            near, from_first, from_second = spread(*sent)
            more = ()
            if n == 0 and lift is not None:
                state, x = inside(state, x, (lift, from_first, from_second, inverse, gi, tables))
                more = (*near, unknowns, gk, gj)
            else:
                state, x = inside(state, x)
                state = side(near, state)
            state, *sent, x = outside(from_first, from_second, state, x, old, new, more)
        return state, x, spread(*sent)

    state, x, (near, from_first, from_second) = steps(state, (mine, other, first, second), None)
    state, x = inside(state, x)
    state = side(near, state)
    state, payload, x = call(
        functools.partial(coarse_kernel, members, cap),
        [VMEM] * 6 + [ANY],
        [states, array(BLK, LANES), field],
        [VMEM, VMEM, ANY],
        ghost_scratch,
        "coarse",
        {2: 0, 6: 2},
    )(from_first, from_second, state, gi, tables, coarse, x)
    pair = call(add_kernel, [VMEM] * 2, [array(BLK, LANES)], [VMEM], [], "add")(payload, swap(payload, 1))[0]
    parts = [pair] + [swap(pair, 2 * n) for n in range(1, members // 2)]
    half = array(members // 2, 6 * cap + BLK, LANES)
    state, lift, unknowns, *sent, x = call(
        lambda *refs: lift_kernel(members, cap, refs[: len(parts)], *refs[len(parts) :]),
        [VMEM] * (len(parts) + 8) + [ANY],
        [states, array(3 * BLK, LANES), array(BLK, LANES), half, half, array(80, LANES), array(80, LANES), field],
        [VMEM] * 7 + [ANY],
        [],
        "lift",
        {len(parts): 0, len(parts) + 8: 7},
    )(*parts, state, eff, inverse, gk, gj, gi, tables, chosen, x)
    state, x, (near, from_first, from_second) = steps(state, sent, x, lift, unknowns)
    state, x = inside(state, x)
    state = side(near, state)
    residual, velocity = call(
        functools.partial(last_kernel, members, cap),
        [VMEM] * 6,
        [field, field],
        [HBM, HBM],
        ghost_scratch + [scratch(3, BLK, CELLS), pltpu.SemaphoreType.DMA((4,))],
        "last",
    )(from_first, from_second, state, gi, tables, x)
    return velocity, residual


def solution(mesh):
    in_specs = (
        P(None, ("grp", "mem"), None),
        P(("grp", "mem"), None),
        P(("grp", "mem")),
        P(("grp", "mem"), None),
        P(("grp", "mem"), None),
        P(("grp", "mem"), None),
        P(("grp", "mem"), None),
        P("grp", "mem", None),
    )
    out_specs = (P(None, ("grp", "mem"), None), P(None, ("grp", "mem"), None))
    return jax.shard_map(local, mesh=mesh, in_specs=in_specs, out_specs=out_specs, check_vma=False)
```
